32 devices in a mesh: row: 8 (over z, core), col: 4 (over y, x).
Axes of the slice: x: 2, y: 2, z: 4, core: 2. Of those that a mesh axis runs over, the one named last changes fastest.
Arguments:
- f_blocks: bfloat16 [16384, 2048], P('row', 'col'), may hold values from -0.25 to 0.25
- block_cols: int32 [256, 32], P('row', 'col'), may hold values from 0 to 23, as said below
- block_counts: int32 [256, 4], P('row', 'col'), may hold values from 1 to 8, as said below
- p_matrix: bfloat16 [12288, 2048], P('row', 'col'), may hold values from -6 to 6
Outputs:
- product: bfloat16 [16384, 2048], P('row', 'col')
The draws below stay inside these ranges and needn't reach their ends.
Inputs may be any that keep to these rules, and one draw needn't show every extreme that they name: `block_cols`: within one block row of one stored tile the 8 listed block columns are distinct, padded slots included. `block_counts`: some block row of every stored tile is full.
All inputs are finite; a program needn't handle non-finite values.
Results may differ from the reference program's by a relative error of at most 0.001.
Values may be sent and summed in bfloat16 or wider, within the bound.
No kernel may reach another device: no remote copies, remote signals or barrier semaphores. Data moves between devices by JAX's collectives and lax.ppermute only.
A program may use at most 64 MiB of HBM per device.

```python
import jax
import jax.numpy as jnp
from jax import lax

BLOCK = 64
ROW_BLK = 32
K_BLK = 24
COL_BLK = 8
SLOTS = 8
NR_BLK = 256
NK_BLK = 192
NC_BLK = 32
N_ROW = 8
N_COL = 4


def draw_block_cols(key, part):
    scores = jax.random.randint(jax.random.fold_in(key, 11), (NR_BLK * N_COL, K_BLK), 0, 1 << 20)
    scores = scores * K_BLK + jnp.arange(K_BLK, dtype=jnp.int32)[None, :]
    order = jnp.argsort(scores, axis=1).astype(jnp.int32)
    return order[:, :SLOTS].reshape(NR_BLK, N_COL * SLOTS)


def draw_block_counts(key, part):
    counts = jax.random.randint(jax.random.fold_in(key, 23), (NR_BLK, N_COL), 1, SLOTS + 1)
    rows = jnp.arange(NR_BLK, dtype=jnp.int32)[:, None]
    return jnp.where(rows % ROW_BLK == 0, jnp.int32(SLOTS), counts).astype(jnp.int32)


def steps_of(key, shape, cuts, low, high):
    factor_of = 1.0
    for position, shards_of in cuts:
        steps = jax.random.uniform(jax.random.fold_in(jax.random.fold_in(key, 6), position), (shards_of,), jnp.float32, low / len(cuts), high / len(cuts))
        factor_of = factor_of * jnp.repeat(jnp.exp(steps), shape[position] // shards_of).reshape((-1,) + (1,) * (len(shape) - 1 - position))
    return factor_of


def centred(own_key, shape, scale, reach, pieces=(), held_as=jnp.bfloat16):
    result = jax.random.normal(own_key, shape, jnp.float32) * scale
    if len(pieces) > 0:
        result = steps_of(own_key, shape, pieces, -0.22, 0.18) * result
    return jnp.clip(result, min=-reach, max=reach).astype(held_as)


def setup_inputs(seed: int = 0) -> dict:
    key_of = jax.random.split(jax.random.key(seed), 5)
    f_blocks = centred(key_of[0], (NR_BLK * BLOCK, SLOTS * N_COL * BLOCK), (BLOCK * SLOTS) ** -0.5, 0.25, ((0, 8), (1, 4)))
    block_cols = draw_block_cols(jax.random.fold_in(key_of[4], 71), 0)
    block_counts = draw_block_counts(jax.random.fold_in(key_of[4], 71), 0)
    p_matrix = centred(key_of[3], (NK_BLK * BLOCK, NC_BLK * BLOCK), 1.0, 6.0, ((0, 8), (1, 4)))
    return {"f_blocks": f_blocks, "block_cols": block_cols, "block_counts": block_counts, "p_matrix": p_matrix}


def tile_term(f_blocks, block_cols, block_counts, p_matrix, i, j, s):
    g = (j + s) % N_COL
    h = (i + s) % N_ROW
    blocks = lax.dynamic_slice(f_blocks, ((i * ROW_BLK * BLOCK).astype(jnp.int32), (g * SLOTS * BLOCK).astype(jnp.int32)), (ROW_BLK * BLOCK, SLOTS * BLOCK))
    cols = lax.dynamic_slice(block_cols, ((i * ROW_BLK).astype(jnp.int32), (g * SLOTS).astype(jnp.int32)), (ROW_BLK, SLOTS))
    counts = lax.dynamic_slice(block_counts, ((i * ROW_BLK).astype(jnp.int32), g.astype(jnp.int32)), (ROW_BLK, 1))
    live = lax.broadcasted_iota(jnp.int32, (ROW_BLK, SLOTS), 1) < counts
    blocks = blocks.astype(jnp.float32).reshape(ROW_BLK, BLOCK, SLOTS, BLOCK)
    blocks = jnp.where(live[:, None, :, None], blocks, jnp.float32(0.0))
    tile = lax.dynamic_slice(p_matrix, ((h * K_BLK * BLOCK).astype(jnp.int32), (j * COL_BLK * BLOCK).astype(jnp.int32)), (K_BLK * BLOCK, COL_BLK * BLOCK))
    tile = tile.astype(jnp.float32).reshape(K_BLK, BLOCK, COL_BLK * BLOCK)
    picked = tile[cols]
    return jnp.einsum("rakb,rkbc->rac", blocks, picked).reshape(ROW_BLK * BLOCK, COL_BLK * BLOCK)


def reference(f_blocks, block_cols, block_counts, p_matrix):
    def one_tile(index):
        i = index // N_COL
        j = index % N_COL
        first = tile_term(f_blocks, block_cols, block_counts, p_matrix, i, j, 0)
        second = tile_term(f_blocks, block_cols, block_counts, p_matrix, i, j, 1)
        return (first + second).astype(jnp.bfloat16)

    tiles = lax.map(one_tile, jnp.arange(N_ROW * N_COL, dtype=jnp.int32))
    tiles = tiles.reshape(N_ROW, N_COL, ROW_BLK * BLOCK, COL_BLK * BLOCK)
    return tiles.transpose(0, 2, 1, 3).reshape(NR_BLK * BLOCK, NC_BLK * BLOCK)
```

```python
import functools

import jax
import jax.numpy as jnp
from jax import lax
from jax.experimental import pallas as pl
from jax.experimental.pallas import tpu as pltpu
from jax.sharding import PartitionSpec as P

LANES = 128
GROUP = 4
CHUNKS = 4


def shifted(block, axis, distance):
    devices = range(lax.axis_size(axis))
    route = [((i - distance) % len(devices), i) for i in devices]
    return lax.ppermute(block, axis, route)


def spread(marked, first_row, strip_ref, dense_refs, edge, slots):
    for dense in dense_refs:
        dense[...] = jnp.zeros_like(dense)
    high = lax.broadcasted_iota(jnp.int32, (edge, LANES), 1) >= edge
    for pair in range(slots // 2):
        for r, dense in enumerate(dense_refs):
            here = strip_ref[pl.ds(r * edge, edge), pl.ds(pair * LANES, LANES)]
            swapped = jnp.concatenate([here[:, edge:], here[:, :edge]], axis=1)
            for half in range(2):
                column = marked[first_row + r, pair * 2 + half]
                odd = column % 2
                value = jnp.where(odd == half, here, swapped)
                tile = pl.ds(pl.multiple_of((column // 2) * LANES, LANES), LANES)
                mine = high == (odd == 1)
                dense[:, tile] = jnp.where(mine, value, dense[:, tile])


def group_product(marked, first_row, strip_ref, p_ref, dense_refs, edge, slots):
    spread(marked, first_row, strip_ref, dense_refs, edge, slots)
    depth = p_ref.shape[0]
    left = jnp.concatenate([dense[:, :depth] for dense in dense_refs], axis=0)
    return jnp.dot(left, p_ref[...], preferred_element_type=jnp.float32)


def first_kernel(edge, slots, marked, strip_ref, p_ref, total_ref, *dense_refs):
    row = pl.program_id(0) * len(dense_refs)
    total_ref[...] = group_product(marked, row, strip_ref, p_ref, dense_refs, edge, slots)


def second_kernel(edge, slots, start, marked, strip_ref, p_ref, total_ref, _, out_ref, *dense_refs):
    row = start + pl.program_id(0) * len(dense_refs)
    product = group_product(marked, row, strip_ref, p_ref, dense_refs, edge, slots)
    out_ref[...] = (total_ref[...] + product).astype(out_ref.dtype)


def dense_scratch(edge, depth):
    return [pltpu.VMEM((edge, depth + LANES), jnp.bfloat16)] * GROUP


def cost(rows, depth, width, extra):
    return pl.CostEstimate(
        flops=2 * rows * depth * width, bytes_accessed=2 * (rows * width + depth * width) + extra, transcendentals=0
    )


def first_product(marked, strips, p_tile):
    nrows, slots = marked.shape
    edge = strips.shape[0] // nrows
    depth, width = p_tile.shape
    tall = GROUP * edge
    return pl.pallas_call(
        functools.partial(first_kernel, edge, slots),
        grid_spec=pltpu.PrefetchScalarGridSpec(
            num_scalar_prefetch=1,
            grid=(nrows // GROUP,),
            in_specs=[
                pl.BlockSpec((tall, strips.shape[1]), lambda g, m: (g, 0)),
                pl.BlockSpec((depth, width), lambda g, m: (0, 0)),
            ],
            out_specs=pl.BlockSpec((tall, width), lambda g, m: (g, 0)),
            scratch_shapes=dense_scratch(edge, depth),
        ),
        out_shape=jax.ShapeDtypeStruct((nrows * edge, width), jnp.float32),
        cost_estimate=cost(nrows * edge, depth, width, 4 * nrows * edge * width),
        compiler_params=pltpu.CompilerParams(vmem_limit_bytes=24 << 20),
        name="first_step",
    )(marked, strips, p_tile)


def second_product(start, marked, part, p_tile, total, out):
    nrows, slots = marked.shape
    edge = total.shape[0] // nrows
    depth, width = p_tile.shape
    tall = GROUP * edge
    offset = start // GROUP
    out_shape = jax.ShapeDtypeStruct((nrows * edge, width), jnp.bfloat16)
    operands = (marked, part, p_tile, total, total if out is None else out)
    return pl.pallas_call(
        functools.partial(second_kernel, edge, slots, start),
        grid_spec=pltpu.PrefetchScalarGridSpec(
            num_scalar_prefetch=1,
            grid=(part.shape[0] // tall,),
            in_specs=[
                pl.BlockSpec((tall, part.shape[1]), lambda g, m: (g, 0)),
                pl.BlockSpec((depth, width), lambda g, m: (0, 0)),
                pl.BlockSpec((tall, width), lambda g, m: (g + offset, 0)),
                pl.BlockSpec(memory_space=pl.ANY),
            ],
            out_specs=pl.BlockSpec((tall, width), lambda g, m: (g + offset, 0)),
            scratch_shapes=dense_scratch(edge, depth),
        ),
        out_shape=out_shape,
        input_output_aliases={} if out is None else {4: 0},
        cost_estimate=cost(part.shape[0], depth, width, 6 * part.shape[0] * width),
        compiler_params=pltpu.CompilerParams(vmem_limit_bytes=24 << 20),
        name="second_step",
    )(*operands)


def body(f_blocks, block_cols, block_counts, p_matrix):
    nrows, slots = block_cols.shape
    edge = f_blocks.shape[0] // nrows
    spare = p_matrix.shape[0] // edge
    live = lax.broadcasted_iota(jnp.int32, (nrows, slots), 1) < block_counts
    marked = jnp.where(live, block_cols, spare)
    marked_next = shifted(marked, "col", -1)
    step = nrows // CHUNKS
    parts = []
    for c in range(CHUNKS):
        parts.append(shifted(f_blocks[c * step * edge : (c + 1) * step * edge], "col", -1))
    p_second = shifted(p_matrix, "row", -1)
    total = first_product(marked, f_blocks, p_matrix)
    out = None
    for c in range(CHUNKS):
        out = second_product(c * step, marked_next, parts[c], p_second, total, out)
    return out


def solution(mesh):
    return jax.shard_map(
        body,
        mesh=mesh,
        in_specs=(P("row", "col"), P("row", "col"), P("row", "col"), P("row", "col")),
        out_specs=P("row", "col"),
        check_vma=False,
    )
```

```python
import functools

import jax
import jax.numpy as jnp
from jax import lax
from jax.experimental import pallas as pl
from jax.experimental.pallas import tpu as pltpu
from jax.sharding import PartitionSpec as P

GROUP = 4
CHUNKS = 4


def shifted(block, axis, distance):
    devices = range(lax.axis_size(axis))
    route = [((i - distance) % len(devices), i) for i in devices]
    return lax.ppermute(block, axis, route)


def row_product(marked, row, left, p_ref, edge, slots):
    picked = [
        p_ref[pl.ds(pl.multiple_of(marked[row, s] * edge, edge), edge), :] for s in range(slots)
    ]
    return jnp.dot(left, jnp.concatenate(picked, axis=0), preferred_element_type=jnp.float32)


def first_kernel(edge, slots, marked, strip_ref, p_ref, total_ref):
    row = pl.program_id(0) * GROUP
    for r in range(GROUP):
        here = pl.ds(r * edge, edge)
        total_ref[here, :] = row_product(marked, row + r, strip_ref[here, :], p_ref, edge, slots)


def second_kernel(edge, slots, start, marked, strip_ref, p_ref, total_ref, _, out_ref):
    row = start + pl.program_id(0) * GROUP
    for r in range(GROUP):
        here = pl.ds(r * edge, edge)
        product = row_product(marked, row + r, strip_ref[here, :], p_ref, edge, slots)
        out_ref[here, :] = (total_ref[here, :] + product).astype(out_ref.dtype)


def cost(rows, depth, width, extra):
    return pl.CostEstimate(
        flops=2 * rows * depth * width, bytes_accessed=2 * (rows * width + depth * width) + extra, transcendentals=0
    )


def first_product(marked, strips, p_tile):
    nrows, slots = marked.shape
    edge = strips.shape[0] // nrows
    depth, width = p_tile.shape
    tall = GROUP * edge
    return pl.pallas_call(
        functools.partial(first_kernel, edge, slots),
        grid_spec=pltpu.PrefetchScalarGridSpec(
            num_scalar_prefetch=1,
            grid=(nrows // GROUP,),
            in_specs=[
                pl.BlockSpec((tall, strips.shape[1]), lambda g, m: (g, 0)),
                pl.BlockSpec((depth, width), lambda g, m: (0, 0)),
            ],
            out_specs=pl.BlockSpec((tall, width), lambda g, m: (g, 0)),
        ),
        out_shape=jax.ShapeDtypeStruct((nrows * edge, width), jnp.float32),
        cost_estimate=cost(nrows * edge, slots * edge, width, 4 * nrows * edge * width),
        compiler_params=pltpu.CompilerParams(vmem_limit_bytes=24 << 20),
        name="first_step",
    )(marked, strips, p_tile)


def second_product(start, marked, part, p_tile, total, out):
    nrows, slots = marked.shape
    edge = total.shape[0] // nrows
    depth, width = p_tile.shape
    tall = GROUP * edge
    offset = start // GROUP
    out_shape = jax.ShapeDtypeStruct((nrows * edge, width), jnp.bfloat16)
    operands = (marked, part, p_tile, total, total if out is None else out)
    return pl.pallas_call(
        functools.partial(second_kernel, edge, slots, start),
        grid_spec=pltpu.PrefetchScalarGridSpec(
            num_scalar_prefetch=1,
            grid=(part.shape[0] // tall,),
            in_specs=[
                pl.BlockSpec((tall, part.shape[1]), lambda g, m: (g, 0)),
                pl.BlockSpec((depth, width), lambda g, m: (0, 0)),
                pl.BlockSpec((tall, width), lambda g, m: (g + offset, 0)),
                pl.BlockSpec(memory_space=pl.ANY),
            ],
            out_specs=pl.BlockSpec((tall, width), lambda g, m: (g + offset, 0)),
        ),
        out_shape=out_shape,
        input_output_aliases={} if out is None else {4: 0},
        cost_estimate=cost(part.shape[0], slots * edge, width, 6 * part.shape[0] * width),
        compiler_params=pltpu.CompilerParams(vmem_limit_bytes=24 << 20),
        name="second_step",
    )(*operands)


def body(f_blocks, block_cols, block_counts, p_matrix):
    nrows, slots = block_cols.shape
    edge = f_blocks.shape[0] // nrows
    spare = p_matrix.shape[0] // edge
    live = lax.broadcasted_iota(jnp.int32, (nrows, slots), 1) < block_counts
    marked = jnp.where(live, block_cols, spare)
    p_first = jnp.concatenate([p_matrix, jnp.zeros((edge, p_matrix.shape[1]), p_matrix.dtype)], axis=0)
    marked_next = shifted(marked, "col", -1)
    f_blocks, p_first, marked_next = lax.optimization_barrier((f_blocks, p_first, marked_next))
    step = nrows // CHUNKS
    parts = []
    for c in range(CHUNKS):
        parts.append(shifted(f_blocks[c * step * edge : (c + 1) * step * edge], "col", -1))
    p_second = shifted(p_first, "row", -1)
    total = first_product(marked, f_blocks, p_first)
    out = None
    for c in range(CHUNKS):
        out = second_product(c * step, marked_next, parts[c], p_second, total, out)
    return out


def solution(mesh):
    return jax.shard_map(
        body,
        mesh=mesh,
        in_specs=(P("row", "col"), P("row", "col"), P("row", "col"), P("row", "col")),
        out_specs=P("row", "col"),
        check_vma=False,
    )
```

```python
import functools

import jax
import jax.numpy as jnp
from jax import lax
from jax.experimental import pallas as pl
from jax.experimental.pallas import tpu as pltpu
from jax.sharding import PartitionSpec as P

GROUP = 4
PAIR = 2


def shifted(block, axis, distance):
    devices = range(lax.axis_size(axis))
    route = [((i - distance) % len(devices), i) for i in devices]
    return lax.ppermute(block, axis, route)


def params(mib):
    return pltpu.CompilerParams(vmem_limit_bytes=mib << 20)


def cost(flops, moved):
    return pl.CostEstimate(flops=flops, bytes_accessed=moved, transcendentals=0)


def picked_rows(table, row, p_ref, edge, slots):
    blocks = [p_ref[pl.ds(pl.multiple_of(table[row, s] * edge, edge), edge), :] for s in range(slots)]
    return jnp.concatenate(blocks, axis=0)


def pack_kernel(edge, nrows, slots, table, f_ref, out_ref):
    wide = PAIR * edge
    for r in range(nrows):
        for p in range(slots // PAIR):
            to = pl.multiple_of((table[r, slots] + p) * edge, edge)
            out_ref[pl.ds(to, edge), :] = f_ref[pl.ds(r * edge, edge), pl.ds(p * wide, wide)]


def packed_pieces(table, f_blocks, nrows, slots):
    edge = f_blocks.shape[0] // nrows
    pieces = nrows * slots // PAIR
    shape = (pieces * edge, PAIR * edge)
    return pl.pallas_call(
        functools.partial(pack_kernel, edge, nrows, slots),
        grid_spec=pltpu.PrefetchScalarGridSpec(
            num_scalar_prefetch=1,
            grid=(1,),
            in_specs=[pl.BlockSpec(f_blocks.shape, lambda g, t: (0, 0))],
            out_specs=pl.BlockSpec(shape, lambda g, t: (0, 0)),
        ),
        out_shape=jax.ShapeDtypeStruct(shape, f_blocks.dtype),
        cost_estimate=cost(0, 4 * f_blocks.size),
        compiler_params=params(24),
        name="pack_live_pieces",
    )(table, f_blocks)


def first_kernel(edge, slots, table, strip_ref, p_ref, total_ref):
    row = pl.program_id(0) * GROUP
    for r in range(GROUP):
        here = pl.ds(r * edge, edge)
        picked = picked_rows(table, row + r, p_ref, edge, slots)
        total_ref[here, :] = jnp.dot(strip_ref[here, :], picked, preferred_element_type=jnp.float32)


def first_product(table, slots, strips, p_tile):
    nrows = table.shape[0]
    edge = strips.shape[0] // nrows
    depth, width = p_tile.shape
    tall = GROUP * edge
    return pl.pallas_call(
        functools.partial(first_kernel, edge, slots),
        grid_spec=pltpu.PrefetchScalarGridSpec(
            num_scalar_prefetch=1,
            grid=(nrows // GROUP,),
            in_specs=[
                pl.BlockSpec((tall, strips.shape[1]), lambda g, t: (g, 0)),
                pl.BlockSpec((depth, width), lambda g, t: (0, 0)),
            ],
            out_specs=pl.BlockSpec((tall, width), lambda g, t: (g, 0)),
        ),
        out_shape=jax.ShapeDtypeStruct((nrows * edge, width), jnp.float32),
        cost_estimate=cost(2 * strips.size * width, 8 * nrows * edge * width),
        compiler_params=params(24),
        name="first_step",
    )(table, strips, p_tile)


def add_group(table, slots, edge, group, base, pieces_ref, p_ref, total_ref, out_ref):
    for r in range(GROUP):
        row = group * GROUP + r
        here = pl.ds(r * edge, edge)
        left = [
            pieces_ref[pl.ds(pl.multiple_of((table[row, slots + p] - base) * edge, edge), edge), :]
            for p in range(slots // PAIR)
        ]
        picked = picked_rows(table, row, p_ref, edge, slots)
        product = jnp.dot(jnp.concatenate(left, axis=1), picked, preferred_element_type=jnp.float32)
        out_ref[here, :] = (total_ref[here, :] + product).astype(out_ref.dtype)


def early_kernel(edge, slots, table, done, pieces_ref, p_ref, total_ref, out_ref):
    group = pl.program_id(0)

    @pl.when(group < done[0])
    def _():
        add_group(table, slots, edge, group, 0, pieces_ref, p_ref, total_ref, out_ref)


def late_kernel(edge, slots, early, reach, table, done, early_ref, late_ref, p_ref, total_ref, _, out_ref, held, sems):
    group = pl.program_id(0)
    first = jnp.minimum(done[0], pl.num_programs(0) - 1)
    base = jnp.minimum(early - reach, table[first * GROUP, slots])

    @pl.when(group == 0)
    def _():
        start = pl.multiple_of(base * edge, edge)
        ahead = pltpu.make_async_copy(early_ref.at[pl.ds(start, reach * edge)], held.at[pl.ds(0, reach * edge)], sems.at[0])
        rest = pltpu.make_async_copy(late_ref, held.at[pl.ds(reach * edge, late_ref.shape[0])], sems.at[1])
        ahead.start()
        rest.start()
        ahead.wait()
        rest.wait()

    @pl.when(group >= first)
    def _():
        add_group(table, slots, edge, group, base, held, p_ref, total_ref, out_ref)


def early_product(table, slots, done, pieces, p_tile, total):
    nrows = table.shape[0]
    edge = total.shape[0] // nrows
    depth, width = p_tile.shape
    tall = GROUP * edge

    def block(g, t, done):
        return (jnp.minimum(g, jnp.maximum(done[0] - 1, 0)), 0)

    return pl.pallas_call(
        functools.partial(early_kernel, edge, slots),
        grid_spec=pltpu.PrefetchScalarGridSpec(
            num_scalar_prefetch=2,
            grid=(nrows // GROUP,),
            in_specs=[
                pl.BlockSpec(pieces.shape, lambda g, t, d: (0, 0)),
                pl.BlockSpec((depth, width), lambda g, t, d: (0, 0)),
                pl.BlockSpec((tall, width), block),
            ],
            out_specs=pl.BlockSpec((tall, width), block),
        ),
        out_shape=jax.ShapeDtypeStruct(total.shape, jnp.bfloat16),
        cost_estimate=cost(2 * pieces.size * width, 6 * total.size),
        compiler_params=params(24),
        name="second_step_early",
    )(table, done, pieces, p_tile, total)


def late_product(table, slots, done, early, late, p_tile, total, out):
    nrows = table.shape[0]
    edge = total.shape[0] // nrows
    depth, width = p_tile.shape
    tall = GROUP * edge
    reach = GROUP * slots // PAIR
    last = nrows // GROUP - 1

    def block(g, t, done):
        return (jnp.maximum(g, jnp.minimum(done[0], last)), 0)

    return pl.pallas_call(
        functools.partial(late_kernel, edge, slots, early.shape[0] // edge, reach),
        grid_spec=pltpu.PrefetchScalarGridSpec(
            num_scalar_prefetch=2,
            grid=(nrows // GROUP,),
            in_specs=[
                pl.BlockSpec(memory_space=pl.ANY),
                pl.BlockSpec(memory_space=pl.ANY),
                pl.BlockSpec((depth, width), lambda g, t, d: (0, 0)),
                pl.BlockSpec((tall, width), block),
                pl.BlockSpec(memory_space=pl.ANY),
            ],
            out_specs=pl.BlockSpec((tall, width), block),
            scratch_shapes=[
                pltpu.VMEM((reach * edge + late.shape[0], late.shape[1]), late.dtype),
                pltpu.SemaphoreType.DMA((2,)),
            ],
        ),
        out_shape=jax.ShapeDtypeStruct(total.shape, jnp.bfloat16),
        input_output_aliases={6: 0},
        cost_estimate=cost(2 * late.size * width, 6 * total.size),
        compiler_params=params(24),
        name="second_step_late",
    )(table, done, early, late, p_tile, total, out)


def exchange(room, late_room, slots, table, packed, f_blocks, p_first):
    nrows = table.shape[0]
    edge = f_blocks.shape[0] // nrows
    early_room = room - late_room
    table_next = shifted(table, "col", -1)
    early = shifted(packed[: early_room * edge], "col", -1)
    p_second = shifted(p_first, "row", -1)
    late = shifted(packed[early_room * edge : room * edge], "col", -1)
    total = first_product(table, slots, f_blocks, p_first)
    ends = table_next[GROUP - 1 :: GROUP, -1]
    done = jnp.sum((ends <= early_room).astype(jnp.int32)).reshape(1)
    out = early_product(table_next, slots, done, early, p_second, total)
    return late_product(table_next, slots, done, early, late, p_second, total, out)


def body(f_blocks, block_cols, block_counts, p_matrix):
    nrows, slots = block_cols.shape
    edge = f_blocks.shape[0] // nrows
    spare = p_matrix.shape[0] // edge
    live = lax.broadcasted_iota(jnp.int32, (nrows, slots), 1) < block_counts
    marked = jnp.where(live, block_cols, spare)
    number = (block_counts + (PAIR - 1)) // PAIR
    before = lax.broadcasted_iota(jnp.int32, (nrows, nrows), 1) < lax.broadcasted_iota(jnp.int32, (nrows, nrows), 0)
    offset = jnp.sum(jnp.where(before, number.reshape(1, nrows), 0), axis=1, keepdims=True)
    which = lax.broadcasted_iota(jnp.int32, (nrows, slots // PAIR), 1)
    place = offset + jnp.where(which < number, which, 0)
    table = jnp.concatenate([marked, place, offset + number], axis=1)
    most = lax.pmax(jnp.sum(number), ("row", "col"))
    packed = packed_pieces(table, f_blocks, nrows, slots)
    p_first = jnp.concatenate([p_matrix, jnp.zeros((edge, p_matrix.shape[1]), p_matrix.dtype)], axis=0)
    pieces = nrows * slots // PAIR
    step = max(pieces // 16, 1)
    least = 3 * step * 2
    rooms = list(range(least, pieces + 1, step))
    late_room = 3 * step
    index = jnp.clip((most - least + step - 1) // step, 0, len(rooms) - 1)
    branches = [functools.partial(exchange, room, late_room, slots) for room in rooms]
    return lax.switch(index, branches, table, packed, f_blocks, p_first)


def solution(mesh):
    return jax.shard_map(
        body,
        mesh=mesh,
        in_specs=(P("row", "col"), P("row", "col"), P("row", "col"), P("row", "col")),
        out_specs=P("row", "col"),
        check_vma=False,
    )
```

```python
import functools

import jax
import jax.numpy as jnp
from jax import lax
from jax.experimental import pallas as pl
from jax.experimental.pallas import tpu as pltpu
from jax.sharding import PartitionSpec as P

GROUP = 4
PAIR = 2


def shifted(block, axis, distance):
    devices = range(lax.axis_size(axis))
    route = [((i - distance) % len(devices), i) for i in devices]
    return lax.ppermute(block, axis, route)


def params(mib):
    return pltpu.CompilerParams(vmem_limit_bytes=mib << 20)


def cost(flops, moved):
    return pl.CostEstimate(flops=flops, bytes_accessed=moved, transcendentals=0)


def whole(shape):
    return pl.BlockSpec(shape, lambda *_: (0,) * len(shape))


def piece(edge, index, count=1):
    return pl.ds(pl.multiple_of(index * edge, edge), count * edge)


def live_half(value, count, slot, edge):
    lane = lax.broadcasted_iota(jnp.int32, value.shape, 1)
    return jnp.where(lane < jnp.where(count > slot + 1, PAIR, 1) * edge, value, jnp.zeros_like(value))


def leading_kernel(edge, counts, f_ref, cols_ref, counts_ref, out_ref):
    nrows, slots = cols_ref.shape
    for r in range(nrows):
        here = pl.ds(r * edge, edge)
        out_ref[here, :] = live_half(f_ref[here, :], counts[r, 0], 0, edge)
    lane = lax.broadcasted_iota(jnp.int32, (nrows, out_ref.shape[1]), 1)
    notes = jnp.where(lane == slots, counts_ref[...], 0)
    for s in range(slots):
        notes = jnp.where(lane == s, cols_ref[:, s : s + 1], notes)
    out_ref[pl.ds(nrows * edge, nrows), :] = notes.astype(jnp.float32).astype(out_ref.dtype)


def leading_pieces(f_blocks, block_cols, block_counts):
    nrows = block_cols.shape[0]
    edge = f_blocks.shape[0] // nrows
    shape = (nrows * edge + nrows, PAIR * edge)
    return pl.pallas_call(
        functools.partial(leading_kernel, edge),
        grid_spec=pltpu.PrefetchScalarGridSpec(
            num_scalar_prefetch=1,
            grid=(1,),
            in_specs=[
                pl.BlockSpec((nrows * edge, PAIR * edge), lambda g, c: (0, 0)),
                whole(block_cols.shape),
                whole(block_counts.shape),
            ],
            out_specs=whole(shape),
        ),
        out_shape=jax.ShapeDtypeStruct(shape, f_blocks.dtype),
        cost_estimate=cost(0, 4 * nrows * edge * PAIR * edge),
        compiler_params=params(8),
        name="leading_pieces",
    )(block_counts, f_blocks, block_cols, block_counts)


def pack_kernel(edge, nrows, slots, table, f_ref, out_ref):
    parts = slots // PAIR
    for r in range(nrows):
        count = table[r, slots + parts + 1]
        for p in range(parts):
            value = f_ref[pl.ds(r * edge, edge), pl.ds(p * PAIR * edge, PAIR * edge)]
            to = r if p == 0 else nrows + table[r, slots + parts] + (p - 1)
            out_ref[piece(edge, to), :] = live_half(value, count, p * PAIR, edge)
    out_ref[pl.ds(nrows * parts * edge, edge), :] = jnp.zeros((edge, PAIR * edge), out_ref.dtype)


def packed_pieces(table, slots, f_blocks):
    nrows = table.shape[0]
    edge = f_blocks.shape[0] // nrows
    shape = ((nrows * slots // PAIR + 1) * edge, PAIR * edge)
    return pl.pallas_call(
        functools.partial(pack_kernel, edge, nrows, slots),
        grid_spec=pltpu.PrefetchScalarGridSpec(
            num_scalar_prefetch=1,
            grid=(1,),
            in_specs=[whole(f_blocks.shape)],
            out_specs=whole(shape),
        ),
        out_shape=jax.ShapeDtypeStruct(shape, f_blocks.dtype),
        cost_estimate=cost(0, 4 * f_blocks.size),
        compiler_params=params(16),
        name="pack_live_pieces",
    )(table, f_blocks)


def row_product(table, slots, edge, row, place, pieces_ref, p_ref):
    left = [pieces_ref[piece(edge, place(row, p)), :] for p in range(slots // PAIR)]
    picked = [p_ref[piece(edge, table[row, s]), :] for s in range(slots)]
    return jnp.dot(
        jnp.concatenate(left, axis=1), jnp.concatenate(picked, axis=0), preferred_element_type=jnp.float32
    )


def placed(table, slots, base, spare):
    def place(row, p):
        if p == 0:
            return row
        other = table[row, slots + p - 1]
        return jnp.where(other < 0, spare, table.shape[0] + other - base)

    return place


def first_kernel(edge, slots, table, pieces_ref, p_ref, total_ref):
    place = placed(table, slots, 0, pieces_ref.shape[0] // edge - 1)
    for r in range(GROUP):
        row = pl.program_id(0) * GROUP + r
        total_ref[pl.ds(r * edge, edge), :] = row_product(table, slots, edge, row, place, pieces_ref, p_ref)


def first_product(table, slots, pieces, p_tile):
    nrows = table.shape[0]
    depth, width = p_tile.shape
    edge = pieces.shape[1] // PAIR
    tall = GROUP * edge
    return pl.pallas_call(
        functools.partial(first_kernel, edge, slots),
        grid_spec=pltpu.PrefetchScalarGridSpec(
            num_scalar_prefetch=1,
            grid=(nrows // GROUP,),
            in_specs=[whole(pieces.shape), whole(p_tile.shape)],
            out_specs=pl.BlockSpec((tall, width), lambda g, t: (g, 0)),
        ),
        out_shape=jax.ShapeDtypeStruct((nrows * edge, width), jnp.float32),
        cost_estimate=cost(2 * pieces.size * width, 8 * nrows * edge * width),
        compiler_params=params(16),
        name="first_step",
    )(table, pieces, p_tile)


def add_group(table, slots, edge, group, place, held, p_ref, total_ref, out_ref):
    for r in range(GROUP):
        here = pl.ds(r * edge, edge)
        product = row_product(table, slots, edge, group * GROUP + r, place, held, p_ref)
        out_ref[here, :] = (total_ref[here, :] + product).astype(out_ref.dtype)


def fetch(held, sems, edge, parts):
    copies = []
    at = 0
    for k, part in enumerate(parts):
        copies.append(pltpu.make_async_copy(part, held.at[pl.ds(at, part.shape[0])], sems.at[k]))
        at += part.shape[0]
    for copy in copies:
        copy.start()
    held[pl.ds(at, edge), :] = jnp.zeros((edge, held.shape[1]), held.dtype)
    for copy in copies:
        copy.wait()


def early_kernel(edge, slots, spare, table, done, lead_ref, extra_ref, p_ref, total_ref, out_ref, held, sems):
    group = pl.program_id(0)

    @pl.when(group == 0)
    def _():
        fetch(held, sems, edge, [lead_ref.at[pl.ds(0, table.shape[0] * edge)], extra_ref])

    @pl.when(group < done[0])
    def _():
        place = placed(table, slots, 0, spare)
        add_group(table, slots, edge, group, place, held, p_ref, total_ref, out_ref)


def late_kernel(edge, slots, spare, reach, table, done, lead_ref, extra_ref, rest_ref, p_ref, total_ref, _, out_ref, held, sems):
    group = pl.program_id(0)
    first = jnp.minimum(done[0], pl.num_programs(0) - 1)
    base = jnp.minimum(extra_ref.shape[0] // edge - reach, table[first * GROUP, slots + slots // PAIR])

    @pl.when(group == 0)
    def _():
        lead = lead_ref.at[pl.ds(0, table.shape[0] * edge)]
        fetch(held, sems, edge, [lead, extra_ref.at[piece(edge, base, reach)], rest_ref])

    @pl.when(group >= first)
    def _():
        place = placed(table, slots, base, spare)
        add_group(table, slots, edge, group, place, held, p_ref, total_ref, out_ref)


def second_product(table, slots, done, received, p_tile, total, out):
    nrows = table.shape[0]
    depth, width = p_tile.shape
    edge = received[0].shape[1] // PAIR
    tall = GROUP * edge
    groups = nrows // GROUP
    reach = GROUP * (slots // PAIR - 1)
    late = out is not None
    if late:
        spare = nrows + reach + received[2].shape[0] // edge
        kernel = functools.partial(late_kernel, edge, slots, spare, reach)
    else:
        spare = nrows + received[1].shape[0] // edge
        kernel = functools.partial(early_kernel, edge, slots, spare)

    def block(g, t, done):
        if late:
            return (jnp.maximum(g, jnp.minimum(done[0], groups - 1)), 0)
        return (jnp.minimum(g, jnp.maximum(done[0] - 1, 0)), 0)

    anywhere = pl.BlockSpec(memory_space=pl.ANY)
    return pl.pallas_call(
        kernel,
        grid_spec=pltpu.PrefetchScalarGridSpec(
            num_scalar_prefetch=2,
            grid=(groups,),
            in_specs=[anywhere] * len(received)
            + [whole(p_tile.shape), pl.BlockSpec((tall, width), block)]
            + [anywhere] * late,
            out_specs=pl.BlockSpec((tall, width), block),
            scratch_shapes=[
                pltpu.VMEM(((spare + 1) * edge, PAIR * edge), p_tile.dtype),
                pltpu.SemaphoreType.DMA((len(received),)),
            ],
        ),
        out_shape=jax.ShapeDtypeStruct(total.shape, jnp.bfloat16),
        input_output_aliases={4 + len(received): 0} if late else {},
        cost_estimate=cost(total.size * slots * edge, 4 * total.size),
        compiler_params=params(16),
        name="second_step_late" if late else "second_step_early",
    )(table, done, *received, p_tile, total, *([out] if late else []))


def table_of(cols, counts):
    nrows, slots = cols.shape
    number = (counts + (PAIR - 1)) // PAIR - 1
    before = lax.broadcasted_iota(jnp.int32, (nrows, nrows), 1) < lax.broadcasted_iota(jnp.int32, (nrows, nrows), 0)
    offset = jnp.sum(jnp.where(before, number.reshape(1, nrows), 0), axis=1, keepdims=True)
    which = lax.broadcasted_iota(jnp.int32, (nrows, slots // PAIR - 1), 1)
    other = jnp.where(which < number, offset + which, -1)
    return jnp.concatenate([cols, other, offset, offset, counts, offset + number], axis=1)


def finish(first_rest, room, slots, packed, table, lead, extra, p_second, total):
    nrows = table.shape[0]
    edge = packed.shape[1] // PAIR
    rest = shifted(packed[(nrows + first_rest) * edge : (nrows + room) * edge], "col", -1)
    ends = table[GROUP - 1 :: GROUP, -1]
    done = jnp.sum((ends <= first_rest).astype(jnp.int32)).reshape(1)
    out = second_product(table, slots, done, (lead, extra), p_second, total, None)
    return second_product(table, slots, done, (lead, extra, rest), p_second, total, out)


def body(f_blocks, block_cols, block_counts, p_matrix):
    nrows, slots = block_cols.shape
    edge = f_blocks.shape[0] // nrows
    lead = shifted(leading_pieces(f_blocks, block_cols, block_counts), "col", -1)
    p_second = shifted(p_matrix, "row", -1)
    table = table_of(block_cols, block_counts)
    packed = packed_pieces(table, slots, f_blocks)
    others = nrows * (slots // PAIR - 1)
    first_rest = others // 3
    extra = shifted(packed[nrows * edge : (nrows + first_rest) * edge], "col", -1)
    total = first_product(table, slots, packed, p_matrix)

    notes = lead[nrows * edge :, : slots + 1].astype(jnp.float32).astype(jnp.int32)
    table_next = table_of(notes[:, :slots], notes[:, slots:])
    most = jnp.maximum(table[nrows - 1, -1], table_next[nrows - 1, -1])
    distance = 2
    while distance < lax.axis_size("col"):
        most = jnp.maximum(most, shifted(most, "col", -distance))
        distance *= 2
    step = max(others // 24, 1)
    rooms = list(range(first_rest + step, others + 1, step))
    index = jnp.clip((most - rooms[0] + step - 1) // step, 0, len(rooms) - 1)
    branches = [functools.partial(finish, first_rest, room, slots) for room in rooms]
    return lax.switch(index, branches, packed, table_next, lead, extra, p_second, total)


def solution(mesh):
    return jax.shard_map(
        body,
        mesh=mesh,
        in_specs=(P("row", "col"), P("row", "col"), P("row", "col"), P("row", "col")),
        out_specs=P("row", "col"),
        check_vma=False,
    )
```

```python
import functools

import jax
import jax.numpy as jnp
from jax import lax
from jax.experimental import pallas as pl
from jax.experimental.pallas import tpu as pltpu
from jax.sharding import PartitionSpec as P

GROUP = 4
PAIR = 2
SIDE = 256

VMEM = pl.BlockSpec(memory_space=pltpu.VMEM)
SMEM = pl.BlockSpec(memory_space=pltpu.SMEM)
ANY = pl.BlockSpec(memory_space=pl.ANY)


def shifted(block, axis, distance):
    devices = range(lax.axis_size(axis))
    route = [((i - distance) % len(devices), i) for i in devices]
    return lax.ppermute(block, axis, route)


def in_vmem(x):
    return pltpu.with_memory_space_constraint(x, pltpu.VMEM)


def params(mib):
    return pltpu.CompilerParams(vmem_limit_bytes=mib << 20)


def cost(flops, moved):
    return pl.CostEstimate(flops=flops, bytes_accessed=moved, transcendentals=0)


def piece(edge, index, count=1):
    return pl.ds(pl.multiple_of(index * edge, edge), count * edge)


def others_of(count):
    return (count + (PAIR - 1)) // PAIR - 1


def live_half(value, count, slot, edge):
    lane = lax.broadcasted_iota(jnp.int32, value.shape, 1)
    return jnp.where(lane < jnp.where(count > slot + 1, PAIR, 1) * edge, value, jnp.zeros_like(value))


def leading_kernel(edge, counts, f_ref, cols_ref, counts_ref, out_ref):
    slots, nrows = cols_ref.shape
    for r in range(nrows):
        here = pl.ds(r * edge, edge)
        out_ref[here, :] = live_half(f_ref[here, :], counts[0, r], 0, edge)
    tail = out_ref.shape[0] - nrows * edge - slots
    notes = jnp.concatenate([cols_ref[...], jnp.broadcast_to(counts_ref[...], (tail, nrows))], axis=0)
    out_ref[pl.ds(nrows * edge, slots + tail), pl.ds(0, nrows)] = notes.astype(jnp.float32).astype(out_ref.dtype)


def leading_pieces(f_blocks, cols, counts):
    slots, nrows = cols.shape
    edge = f_blocks.shape[0] // nrows
    shape = (nrows * edge + 2 * slots, PAIR * edge)
    return pl.pallas_call(
        functools.partial(leading_kernel, edge),
        grid_spec=pltpu.PrefetchScalarGridSpec(
            num_scalar_prefetch=1,
            grid=(1,),
            in_specs=[
                pl.BlockSpec((nrows * edge, PAIR * edge), lambda g, c: (0, 0)),
                pl.BlockSpec(cols.shape, lambda g, c: (0, 0)),
                pl.BlockSpec(counts.shape, lambda g, c: (0, 0)),
            ],
            out_specs=pl.BlockSpec(shape, lambda g, c: (0, 0)),
        ),
        out_shape=jax.ShapeDtypeStruct(shape, f_blocks.dtype),
        cost_estimate=cost(0, 4 * nrows * edge * PAIR * edge),
        compiler_params=params(8),
        name="leading_pieces",
    )(counts, pltpu.with_memory_space_constraint(f_blocks, pltpu.HBM), cols, counts)


def pack_kernel(edge, nrows, slots, notes, f_ref, out_ref):
    parts = slots // PAIR
    at = 0
    for r in range(nrows):
        count = notes[slots, r]
        for p in range(parts):
            value = f_ref[pl.ds(r * edge, edge), pl.ds(p * PAIR * edge, PAIR * edge)]
            to = r if p == 0 else nrows + at + (p - 1)
            out_ref[piece(edge, to), :] = live_half(value, count, p * PAIR, edge)
        at = at + others_of(count)
    out_ref[pl.ds(nrows * parts * edge, edge), :] = jnp.zeros((edge, PAIR * edge), out_ref.dtype)


def packed_pieces(notes, slots, f_blocks):
    nrows = notes.shape[1]
    edge = f_blocks.shape[0] // nrows
    shape = ((nrows * slots // PAIR + 1) * edge, PAIR * edge)
    return pl.pallas_call(
        functools.partial(pack_kernel, edge, nrows, slots),
        in_specs=[SMEM, VMEM],
        out_specs=VMEM,
        out_shape=jax.ShapeDtypeStruct(shape, f_blocks.dtype),
        cost_estimate=cost(0, 4 * f_blocks.size),
        compiler_params=params(16),
        name="pack_live_pieces",
    )(notes, in_vmem(f_blocks))


def offsets(notes, slots, starts):
    at = jnp.int32(0)
    for r in range(notes.shape[1]):
        starts[r] = at
        at = at + others_of(notes[slots, r])
    starts[notes.shape[1]] = at


def complete(starts, groups, room):
    number = jnp.int32(0)
    for g in range(groups):
        number = number + (starts[(g + 1) * GROUP] <= room).astype(jnp.int32)
    return number


def row_parts(notes, slots, edge, row, left, p_ref):
    step = min(SIDE // edge, slots)
    for n in range(0, p_ref.shape[1], SIDE):
        total = None
        for k in range(0, slots, step):
            picked = [p_ref[piece(edge, notes[s, row]), pl.ds(n, SIDE)] for s in range(k, k + step)]
            here = jnp.concatenate(left[k // PAIR : (k + step) // PAIR], axis=1)
            term = jnp.dot(here, jnp.concatenate(picked, axis=0), preferred_element_type=jnp.float32)
            total = term if total is None else total + term
        yield n, total


def left_pieces(notes, slots, edge, row, starts, lead_ref, held, base, spare):
    live = others_of(notes[slots, row])
    left = [lead_ref[piece(edge, row), :]]
    for p in range(slots // PAIR - 1):
        left.append(held[piece(edge, jnp.where(p < live, starts[row] + p - base, spare)), :])
    return left


def first_kernel(edge, slots, notes, packed_ref, p_ref, total_ref, starts):
    nrows = notes.shape[1]
    offsets(notes, slots, starts)
    spare = packed_ref.shape[0] // edge - 1

    def group(g, carry):
        for r in range(GROUP):
            row = g * GROUP + r
            left = left_pieces(notes, slots, edge, row, starts, packed_ref, packed_ref, -nrows, spare)
            for n, value in row_parts(notes, slots, edge, row, left, p_ref):
                total_ref[piece(edge, row), pl.ds(n, SIDE)] = value
        return carry

    lax.fori_loop(0, nrows // GROUP, group, 0)


def first_product(notes, slots, packed, p_tile):
    nrows = notes.shape[1]
    width = p_tile.shape[1]
    edge = packed.shape[1] // PAIR
    return pl.pallas_call(
        functools.partial(first_kernel, edge, slots),
        in_specs=[SMEM, VMEM, VMEM],
        out_specs=VMEM,
        scratch_shapes=[pltpu.SMEM((nrows + 1,), jnp.int32)],
        out_shape=jax.ShapeDtypeStruct((nrows * edge, width), jnp.float32),
        cost_estimate=cost(2 * packed.size * width, 4 * nrows * edge * width),
        compiler_params=params(16),
        name="first_step",
    )(notes, in_vmem(packed), in_vmem(p_tile))


def add_groups(notes, slots, edge, low, high, starts, lead_ref, held, base, spare, p_ref, total_ref, stage, sem, out_ref):
    def copy(g):
        here = piece(edge, g * GROUP, GROUP)
        return pltpu.make_async_copy(stage.at[here], out_ref.at[here], sem.at[g])

    def group(g, carry):
        for r in range(GROUP):
            row = g * GROUP + r
            left = left_pieces(notes, slots, edge, row, starts, lead_ref, held, base, spare)
            here = piece(edge, row)
            for n, value in row_parts(notes, slots, edge, row, left, p_ref):
                there = pl.ds(n, SIDE)
                stage[here, there] = (total_ref[here, there] + value).astype(stage.dtype)
        copy(g).start()
        return carry

    def settle(g, carry):
        copy(g).wait()
        return carry

    lax.fori_loop(low, high, group, 0)
    lax.fori_loop(low, high, settle, 0)


def fetch(held, sems, edge, parts):
    copies = []
    at = 0
    for k, part in enumerate(parts):
        copies.append(pltpu.make_async_copy(part, held.at[pl.ds(at, part.shape[0])], sems.at[k]))
        at += part.shape[0]
    for copy in copies:
        copy.start()
    held[pl.ds(at, edge), :] = jnp.zeros((edge, held.shape[1]), held.dtype)
    for copy in copies:
        copy.wait()


def early_kernel(edge, slots, notes, lead_ref, extra_ref, p_ref, total_ref, out_ref, starts, held, stage, sems, out_sems):
    groups = notes.shape[1] // GROUP
    room = extra_ref.shape[0] // edge
    offsets(notes, slots, starts)
    fetch(held, sems, edge, [extra_ref])
    done = complete(starts, groups, room)
    add_groups(notes, slots, edge, 0, done, starts, lead_ref, held, 0, room, p_ref, total_ref, stage, out_sems, out_ref)


def late_kernel(
    edge, slots, notes, lead_ref, extra_ref, rest_ref, p_ref, total_ref, _, out_ref, starts, held, stage, sems, out_sems
):
    groups = notes.shape[1] // GROUP
    room = extra_ref.shape[0] // edge
    reach = GROUP * (slots // PAIR - 1)
    offsets(notes, slots, starts)
    fetch(held, sems, edge, [extra_ref.at[pl.ds((room - reach) * edge, reach * edge)], rest_ref])
    done = complete(starts, groups, room)
    spare = held.shape[0] // edge - 1
    add_groups(
        notes, slots, edge, done, groups, starts, lead_ref, held, room - reach, spare, p_ref, total_ref, stage, out_sems, out_ref
    )


def second_product(notes, slots, received, p_tile, total, out):
    nrows = notes.shape[1]
    edge = received[0].shape[1] // PAIR
    groups = nrows // GROUP
    late = out is not None
    room = received[1].shape[0] // edge
    if late:
        room = GROUP * (slots // PAIR - 1) + received[2].shape[0] // edge
    return pl.pallas_call(
        functools.partial(late_kernel if late else early_kernel, edge, slots),
        in_specs=[SMEM] + [VMEM] * (len(received) + 2) + [ANY] * late,
        out_specs=ANY,
        scratch_shapes=[
            pltpu.SMEM((nrows + 1,), jnp.int32),
            pltpu.VMEM(((room + 1) * edge, PAIR * edge), p_tile.dtype),
            pltpu.VMEM(total.shape, jnp.bfloat16),
            pltpu.SemaphoreType.DMA((len(received),)),
            pltpu.SemaphoreType.DMA((groups,)),
        ],
        out_shape=jax.ShapeDtypeStruct(total.shape, jnp.bfloat16),
        input_output_aliases={3 + len(received): 0} if late else {},
        cost_estimate=cost(total.size * slots * edge, 4 * total.size),
        compiler_params=params(16),
        name="second_step_late" if late else "second_step_early",
    )(notes, *[in_vmem(x) for x in received], in_vmem(p_tile), in_vmem(total), *([out] if late else []))


def finish(first_rest, room, slots, packed, notes, lead, extra, p_second, total):
    nrows = notes.shape[1]
    edge = packed.shape[1] // PAIR
    rest = shifted(packed[(nrows + first_rest) * edge : (nrows + room) * edge], "col", -1)
    out = second_product(notes, slots, (lead, extra), p_second, total, None)
    return second_product(notes, slots, (lead, extra, rest), p_second, total, out)


def body(f_blocks, block_cols, block_counts, p_matrix):
    nrows, slots = block_cols.shape
    edge = f_blocks.shape[0] // nrows
    cols, counts = block_cols.T, block_counts.T
    lead = shifted(leading_pieces(f_blocks, cols, counts), "col", -1)
    p_second = shifted(p_matrix, "row", -1)
    notes = jnp.concatenate([cols, jnp.broadcast_to(counts, (slots, nrows))], axis=0)
    packed = packed_pieces(notes, slots, f_blocks)
    others = nrows * (slots // PAIR - 1)
    first_rest = others // 3
    extra = shifted(packed[nrows * edge : (nrows + first_rest) * edge], "col", -1)
    total = first_product(notes, slots, packed, p_matrix)

    notes_next = lead[nrows * edge :, :nrows].astype(jnp.float32).astype(jnp.int32)
    most = jnp.maximum(jnp.sum(others_of(counts)), jnp.sum(others_of(notes_next[slots])))
    distance = 2
    while distance < lax.axis_size("col"):
        most = jnp.maximum(most, shifted(most, "col", -distance))
        distance *= 2
    step = max(others // 24, 1)
    rooms = list(range(first_rest + step, others + 1, step))
    index = jnp.clip((most - rooms[0] + step - 1) // step, 0, len(rooms) - 1)
    branches = [functools.partial(finish, first_rest, room, slots) for room in rooms]
    return lax.switch(index, branches, packed, notes_next, lead, extra, p_second, total)


def solution(mesh):
    return jax.shard_map(
        body,
        mesh=mesh,
        in_specs=(P("row", "col"), P("row", "col"), P("row", "col"), P("row", "col")),
        out_specs=P("row", "col"),
        check_vma=False,
    )
```

```python
import functools

import jax
import jax.numpy as jnp
from jax import lax
from jax.experimental import pallas as pl
from jax.experimental.pallas import tpu as pltpu
from jax.sharding import PartitionSpec as P

GROUP = 4
PAIR = 2

VMEM = pl.BlockSpec(memory_space=pltpu.VMEM)
SMEM = pl.BlockSpec(memory_space=pltpu.SMEM)
HBM = pl.BlockSpec(memory_space=pltpu.HBM)


def shifted(block, axis, distance):
    devices = range(lax.axis_size(axis))
    route = [((i - distance) % len(devices), i) for i in devices]
    return lax.ppermute(block, axis, route)


def in_vmem(x):
    return pltpu.with_memory_space_constraint(x, pltpu.VMEM)


def in_hbm(x):
    return pltpu.with_memory_space_constraint(x, pltpu.HBM)


def params(mib):
    return pltpu.CompilerParams(vmem_limit_bytes=mib << 20)


def cost(flops, moved):
    return pl.CostEstimate(flops=flops, bytes_accessed=moved, transcendentals=0)


def piece(edge, index, count=1):
    return pl.ds(pl.multiple_of(index * edge, edge), count * edge)


def others_of(count):
    return (count + (PAIR - 1)) // PAIR - 1


def live_half(value, count, slot, edge):
    lane = lax.broadcasted_iota(jnp.int32, value.shape, 1)
    return jnp.where(lane < jnp.where(count > slot + 1, PAIR, 1) * edge, value, jnp.zeros_like(value))


def leading_kernel(edge, counts, f_ref, cols_ref, counts_ref, out_ref):
    slots, nrows = cols_ref.shape
    tall = f_ref.shape[0]
    for r in range(tall // edge):
        here = pl.ds(r * edge, edge)
        out_ref[here, :] = live_half(f_ref[here, :], counts[0, r], 0, edge)
    notes = jnp.concatenate([cols_ref[...], jnp.broadcast_to(counts_ref[...], (slots, nrows))], axis=0)
    out_ref[pl.ds(tall, 2 * slots), pl.ds(0, nrows)] = notes.astype(jnp.float32).astype(out_ref.dtype)


def leading_pieces(rows, f_blocks, cols, counts):
    slots, nrows = cols.shape
    edge = f_blocks.shape[0] // nrows
    shape = (rows * edge + 2 * slots, PAIR * edge)
    f_blocks, cols, counts = (in_hbm(x) for x in (f_blocks, cols, counts))
    return pl.pallas_call(
        functools.partial(leading_kernel, edge),
        grid_spec=pltpu.PrefetchScalarGridSpec(
            num_scalar_prefetch=1,
            grid=(1,),
            in_specs=[
                pl.BlockSpec((rows * edge, PAIR * edge), lambda g, c: (0, 0)),
                pl.BlockSpec(cols.shape, lambda g, c: (0, 0)),
                pl.BlockSpec(counts.shape, lambda g, c: (0, 0)),
            ],
            out_specs=pl.BlockSpec(shape, lambda g, c: (0, 0)),
        ),
        out_shape=jax.ShapeDtypeStruct(shape, f_blocks.dtype),
        cost_estimate=cost(0, 4 * rows * edge * PAIR * edge),
        compiler_params=params(8),
        name="leading_pieces",
    )(counts, f_blocks, cols, counts)


def pack_kernel(edge, nrows, slots, notes, f_ref, out_ref):
    parts = slots // PAIR
    at = 0
    for r in range(nrows):
        count = notes[slots, r]
        for p in range(parts):
            value = f_ref[pl.ds(r * edge, edge), pl.ds(p * PAIR * edge, PAIR * edge)]
            to = r if p == 0 else nrows + at + (p - 1)
            out_ref[piece(edge, to), :] = live_half(value, count, p * PAIR, edge)
        at = at + others_of(count)
    out_ref[pl.ds(nrows * parts * edge, edge), :] = jnp.zeros((edge, PAIR * edge), out_ref.dtype)


def packed_pieces(notes, slots, f_blocks):
    nrows = notes.shape[1]
    edge = f_blocks.shape[0] // nrows
    shape = ((nrows * slots // PAIR + 1) * edge, PAIR * edge)
    return pl.pallas_call(
        functools.partial(pack_kernel, edge, nrows, slots),
        in_specs=[SMEM, VMEM],
        out_specs=VMEM,
        out_shape=jax.ShapeDtypeStruct(shape, f_blocks.dtype),
        cost_estimate=cost(0, 4 * f_blocks.size),
        compiler_params=params(16),
        name="pack_live_pieces",
    )(notes, in_vmem(f_blocks))


def offsets(notes, slots, starts):
    at = jnp.int32(0)
    for r in range(notes.shape[1]):
        starts[r] = at
        at = at + others_of(notes[slots, r])
    starts[notes.shape[1]] = at


def complete(starts, groups, room):
    number = jnp.int32(0)
    for g in range(groups):
        number = number + (starts[(g + 1) * GROUP] <= room).astype(jnp.int32)
    return number


def row_product(notes, slots, edge, row, left, p_ref):
    picked = [p_ref[piece(edge, notes[s, row]), :] for s in range(slots)]
    return jnp.dot(
        jnp.concatenate(left, axis=1), jnp.concatenate(picked, axis=0), preferred_element_type=jnp.float32
    )


def left_pieces(notes, slots, edge, row, starts, lead_ref, held, base, spare):
    live = others_of(notes[slots, row])
    left = [lead_ref[piece(edge, row), :]]
    for p in range(slots // PAIR - 1):
        left.append(held[piece(edge, jnp.where(p < live, starts[row] + p - base, spare)), :])
    return left


def first_kernel(edge, slots, notes, packed_ref, p_ref, total_ref, starts):
    nrows = notes.shape[1]
    offsets(notes, slots, starts)
    spare = packed_ref.shape[0] // edge - 1

    def group(g, carry):
        for r in range(GROUP):
            row = g * GROUP + r
            left = left_pieces(notes, slots, edge, row, starts, packed_ref, packed_ref, -nrows, spare)
            total_ref[piece(edge, row), :] = row_product(notes, slots, edge, row, left, p_ref)
        return carry

    lax.fori_loop(0, nrows // GROUP, group, 0)


def first_product(notes, slots, packed, p_tile):
    nrows = notes.shape[1]
    width = p_tile.shape[1]
    edge = packed.shape[1] // PAIR
    return pl.pallas_call(
        functools.partial(first_kernel, edge, slots),
        in_specs=[SMEM, VMEM, VMEM],
        out_specs=VMEM,
        scratch_shapes=[pltpu.SMEM((nrows + 1,), jnp.int32)],
        out_shape=jax.ShapeDtypeStruct((nrows * edge, width), jnp.float32),
        cost_estimate=cost(2 * packed.size * width, 4 * nrows * edge * width),
        compiler_params=params(16),
        name="first_step",
    )(notes, in_vmem(packed), in_vmem(p_tile))


def add_groups(notes, slots, edge, low, high, starts, lead_ref, held, base, spare, p_ref, total_ref, stage, sem, out_ref):
    def copy(g):
        here = piece(edge, g * GROUP, GROUP)
        return pltpu.make_async_copy(stage.at[here], out_ref.at[here], sem.at[g])

    def group(g, carry):
        for r in range(GROUP):
            row = g * GROUP + r
            left = left_pieces(notes, slots, edge, row, starts, lead_ref, held, base, spare)
            here = piece(edge, row)
            value = row_product(notes, slots, edge, row, left, p_ref)
            stage[here, :] = (total_ref[here, :] + value).astype(stage.dtype)
        copy(g).start()
        return carry

    def settle(g, carry):
        copy(g).wait()
        return carry

    lax.fori_loop(low, high, group, 0)
    lax.fori_loop(low, high, settle, 0)


def fetch(held, sems, edge, parts):
    copies = []
    for k, (needed, at, part) in enumerate(parts):
        copies.append((needed, pltpu.make_async_copy(part, held.at[pl.ds(at * edge, part.shape[0])], sems.at[k])))

    def each(act):
        for needed, copy in copies:
            if needed is None:
                act(copy)
            else:
                pl.when(needed)(functools.partial(act, copy))

    each(lambda copy: copy.start())
    held[pl.ds(held.shape[0] - edge, edge), :] = jnp.zeros((edge, held.shape[1]), held.dtype)
    each(lambda copy: copy.wait())


def early_groups(notes, starts, edge, lead_ref, room):
    return jnp.minimum(complete(starts, notes.shape[1] // GROUP, room), lead_ref.shape[0] // edge // GROUP)


def early_kernel(edge, slots, notes, lead_ref, extra_ref, p_ref, total_ref, out_ref, starts, held, stage, sems, out_sems):
    room = extra_ref.shape[0] // edge
    offsets(notes, slots, starts)
    fetch(held, sems, edge, [(None, 0, extra_ref)])
    done = early_groups(notes, starts, edge, lead_ref, room)
    add_groups(notes, slots, edge, 0, done, starts, lead_ref, held, 0, room, p_ref, total_ref, stage, out_sems, out_ref)


def late_kernel(edge, slots, notes, size, lead_ref, extra_ref, later_ref, *refs):
    *rest_refs, p_ref, total_ref, _, out_ref, starts, held, stage, sems, out_sems = refs
    nrows = notes.shape[1]
    groups = nrows // GROUP
    room = extra_ref.shape[0] // edge
    offsets(notes, slots, starts)
    leading = lead_ref.shape[0] // edge
    parts = [(None, 0, lead_ref.at[pl.ds(0, leading * edge)]), (None, leading, later_ref), (None, nrows, extra_ref)]
    parts += [(size[0] == k, nrows + room, rest) for k, rest in enumerate(rest_refs)]
    fetch(held, sems, edge, parts)
    done = early_groups(notes, starts, edge, lead_ref, room)
    spare = held.shape[0] // edge - 1
    add_groups(
        notes, slots, edge, done, groups, starts, held, held, -nrows, spare, p_ref, total_ref, stage, out_sems, out_ref
    )


def second_product(notes, slots, received, p_tile, total, size=None, out=None):
    nrows = notes.shape[1]
    edge = received[0].shape[1] // PAIR
    groups = nrows // GROUP
    late = out is not None
    room = received[1].shape[0] // edge
    if late:
        room += nrows + max(x.shape[0] for x in received[3:]) // edge
    return pl.pallas_call(
        functools.partial(late_kernel if late else early_kernel, edge, slots),
        in_specs=[SMEM] * (1 + late) + [VMEM] * (len(received) + 2) + [HBM] * late,
        out_specs=HBM,
        scratch_shapes=[
            pltpu.SMEM((nrows + 1,), jnp.int32),
            pltpu.VMEM(((room + 1) * edge, PAIR * edge), p_tile.dtype),
            pltpu.VMEM(total.shape, jnp.bfloat16),
            pltpu.SemaphoreType.DMA((len(received),)),
            pltpu.SemaphoreType.DMA((groups,)),
        ],
        out_shape=pltpu.HBM(total.shape, jnp.bfloat16),
        input_output_aliases={4 + len(received): 0} if late else {},
        cost_estimate=cost(total.size * slots * edge, 4 * total.size),
        compiler_params=params(16),
        name="second_step_late" if late else "second_step_early",
    )(
        notes,
        *([size] if late else []),
        *[in_vmem(x) for x in received],
        in_vmem(p_tile),
        in_vmem(total),
        *([in_hbm(out)] if late else []),
    )


def remainder(k, slots, rests, notes, lead, extra, p_second, total):
    rest = [shifted(part, "col", -1) if k == n else part for n, part in enumerate(rests)]
    return second_product(notes, slots, (lead, extra), p_second, total), rest


def body(f_blocks, block_cols, block_counts, p_matrix):
    nrows, slots = block_cols.shape
    edge = f_blocks.shape[0] // nrows
    cols, counts = block_cols.T, block_counts.T
    groups = nrows // GROUP
    leading = (groups - groups * 3 // 8) * GROUP
    others = nrows * (slots // PAIR - 1)
    unit = others // 24
    lead = shifted(leading_pieces(leading, f_blocks, cols, counts), "col", -1)
    p_second = shifted(p_matrix, "row", -1)
    notes = jnp.concatenate([cols, jnp.broadcast_to(counts, (slots, nrows))], axis=0)
    packed = packed_pieces(notes, slots, f_blocks)

    def cut(low, high):
        return packed[low * edge : high * edge]

    always = 10 * unit
    extra = shifted(cut(nrows, nrows + always), "col", -1)
    total = first_product(notes, slots, packed, p_matrix)
    ends = [always + k * unit for k in (2, 3, 4, 5, 6, 7, 9)] + [others]
    later, total, *rests = lax.optimization_barrier(
        (cut(leading, nrows), total, *[cut(nrows + always, nrows + end) for end in ends])
    )
    later = shifted(later, "col", -1)

    notes_next = lead[leading * edge :, :nrows].astype(jnp.float32).astype(jnp.int32)
    most = jnp.maximum(jnp.sum(others_of(counts)), jnp.sum(others_of(notes_next[slots])))
    distance = 2
    while distance < lax.axis_size("col"):
        most = jnp.maximum(most, shifted(most, "col", -distance))
        distance *= 2
    size = sum((most > end).astype(jnp.int32) for end in ends[:-1])
    branches = [functools.partial(remainder, k, slots) for k in range(len(ends))]
    out, rest = lax.switch(size, branches, rests, notes_next, lead, extra, p_second, total)
    received = (lead, extra, later, *rest)
    return second_product(notes_next, slots, received, p_second, total, size.reshape(1), out)


def solution(mesh):
    return jax.shard_map(
        body,
        mesh=mesh,
        in_specs=(P("row", "col"), P("row", "col"), P("row", "col"), P("row", "col")),
        out_specs=P("row", "col"),
        check_vma=False,
    )
```

```python
import functools

import jax
import jax.numpy as jnp
from jax import lax
from jax.experimental import pallas as pl
from jax.experimental.pallas import tpu as pltpu
from jax.sharding import PartitionSpec as P

GROUP = 4
PAIR = 2

SMEM = pl.BlockSpec(memory_space=pltpu.SMEM)
ANY = pl.BlockSpec(memory_space=pl.ANY)
HBM = pl.BlockSpec(memory_space=pltpu.HBM)


def shifted(block, axis, distance):
    devices = range(lax.axis_size(axis))
    route = [((i - distance) % len(devices), i) for i in devices]
    return lax.ppermute(block, axis, route)


def in_hbm(x):
    return pltpu.with_memory_space_constraint(x, pltpu.HBM)


def params(mib):
    return pltpu.CompilerParams(vmem_limit_bytes=mib << 20)


def cost(flops, moved):
    return pl.CostEstimate(flops=flops, bytes_accessed=moved, transcendentals=0)


def piece(edge, index, count=1):
    return pl.ds(pl.multiple_of(index * edge, edge), count * edge)


def others_of(count):
    return (count + (PAIR - 1)) // PAIR - 1


def live_half(value, count, slot, edge):
    lane = lax.broadcasted_iota(jnp.int32, value.shape, 1)
    return jnp.where(lane < jnp.where(count > slot + 1, PAIR, 1) * edge, value, jnp.zeros_like(value))


def leading_kernel(edge, counts, f_ref, cols_ref, counts_ref, out_ref):
    slots, nrows = cols_ref.shape
    tall = f_ref.shape[0]
    for r in range(tall // edge):
        here = pl.ds(r * edge, edge)
        out_ref[here, :] = live_half(f_ref[here, :], counts[0, r], 0, edge)
    notes = jnp.concatenate([cols_ref[...], jnp.broadcast_to(counts_ref[...], (slots, nrows))], axis=0)
    out_ref[pl.ds(tall, 2 * slots), pl.ds(0, nrows)] = notes.astype(jnp.float32).astype(out_ref.dtype)


def leading_pieces(rows, f_blocks, cols, counts):
    slots, nrows = cols.shape
    edge = f_blocks.shape[0] // nrows
    shape = (rows * edge + 2 * slots, PAIR * edge)
    f_blocks, cols, counts = (in_hbm(x) for x in (f_blocks, cols, counts))
    return pl.pallas_call(
        functools.partial(leading_kernel, edge),
        grid_spec=pltpu.PrefetchScalarGridSpec(
            num_scalar_prefetch=1,
            grid=(1,),
            in_specs=[
                pl.BlockSpec((rows * edge, PAIR * edge), lambda g, c: (0, 0)),
                pl.BlockSpec(cols.shape, lambda g, c: (0, 0)),
                pl.BlockSpec(counts.shape, lambda g, c: (0, 0)),
            ],
            out_specs=pl.BlockSpec(shape, lambda g, c: (0, 0)),
        ),
        out_shape=jax.ShapeDtypeStruct(shape, f_blocks.dtype),
        cost_estimate=cost(0, 4 * rows * edge * PAIR * edge),
        compiler_params=params(8),
        name="leading_pieces",
    )(counts, f_blocks, cols, counts)


def pack_kernel(edge, slots, notes, f_ref, out_ref, extra_ref, f_here, packed, sems):
    nrows = notes.shape[1]
    parts = slots // PAIR
    fetched = []
    for g in range(nrows // GROUP):
        here = piece(edge, g * GROUP, GROUP)
        fetched.append(pltpu.make_async_copy(f_ref.at[here], f_here.at[here], sems.at[g]))
        fetched[-1].start()
    at = 0
    for r in range(nrows):
        if r % GROUP == 0:
            fetched[r // GROUP].wait()
        count = notes[slots, r]
        for p in range(parts):
            value = f_here[pl.ds(r * edge, edge), pl.ds(p * PAIR * edge, PAIR * edge)]
            to = r if p == 0 else nrows + at + (p - 1)
            packed[piece(edge, to), :] = live_half(value, count, p * PAIR, edge)
        at = at + others_of(count)
    packed[pl.ds(nrows * parts * edge, edge), :] = jnp.zeros((edge, PAIR * edge), packed.dtype)
    copies = [
        pltpu.make_async_copy(packed.at[pl.ds(nrows * edge, extra_ref.shape[0])], extra_ref, sems.at[0]),
        pltpu.make_async_copy(packed, out_ref, sems.at[1]),
    ]
    for copy in copies:
        copy.start()
    for copy in copies:
        copy.wait()


def packed_pieces(notes, slots, always, f_blocks):
    nrows = notes.shape[1]
    edge = f_blocks.shape[0] // nrows
    shape = ((nrows * slots // PAIR + 1) * edge, PAIR * edge)
    return pl.pallas_call(
        functools.partial(pack_kernel, edge, slots),
        in_specs=[SMEM, ANY],
        out_specs=[ANY, ANY],
        scratch_shapes=[
            pltpu.VMEM(f_blocks.shape, f_blocks.dtype),
            pltpu.VMEM(shape, f_blocks.dtype),
            pltpu.SemaphoreType.DMA((nrows // GROUP,)),
        ],
        out_shape=[
            jax.ShapeDtypeStruct(shape, f_blocks.dtype),
            jax.ShapeDtypeStruct((always * edge, PAIR * edge), f_blocks.dtype),
        ],
        cost_estimate=cost(0, 4 * f_blocks.size),
        compiler_params=params(16),
        name="pack_live_pieces",
    )(notes, f_blocks)


def cut_kernel(ranges, packed_ref, *refs):
    *out_refs, sems = refs
    copies = [
        pltpu.make_async_copy(packed_ref.at[pl.ds(low, high - low)], out_ref, sems.at[k])
        for k, ((low, high), out_ref) in enumerate(zip(ranges, out_refs))
    ]
    for copy in copies:
        copy.start()
    for copy in copies:
        copy.wait()


def cut_pieces(ranges, packed):
    edge = packed.shape[1] // PAIR
    rows = [(low * edge, high * edge) for low, high in ranges]
    return pl.pallas_call(
        functools.partial(cut_kernel, rows),
        in_specs=[ANY],
        out_specs=[ANY] * len(rows),
        scratch_shapes=[pltpu.SemaphoreType.DMA((len(rows),))],
        out_shape=[jax.ShapeDtypeStruct((high - low, packed.shape[1]), packed.dtype) for low, high in rows],
        cost_estimate=cost(0, 4 * sum(high - low for low, high in rows) * packed.shape[1]),
        compiler_params=params(2),
        name="cut_pieces",
    )(packed)


def row_product(notes, slots, edge, row, left, p_ref):
    picked = [p_ref[piece(edge, notes[s, row]), :] for s in range(slots)]
    return jnp.dot(
        jnp.concatenate(left, axis=1), jnp.concatenate(picked, axis=0), preferred_element_type=jnp.float32
    )


def left_pieces(notes, slots, edge, row, starts, held):
    nrows = notes.shape[1]
    spare = held.shape[0] // edge - 1
    live = others_of(notes[slots, row])
    left = [held[piece(edge, row), :]]
    for p in range(slots // PAIR - 1):
        left.append(held[piece(edge, jnp.where(p < live, nrows + starts[row] + p, spare)), :])
    return left


def step_kernel(edge, slots, name, leading, places, notes, *refs):
    size = None
    if name == "late":
        size, *refs = refs
    part_refs, refs = refs[: len(places)], refs[len(places) :]
    p_ref, *refs = refs
    total_ref = None
    if name != "first":
        total_ref, *refs = refs
    if name == "late":
        _, *refs = refs
    out_ref, starts, held, p_here, stage, sems, out_sems, *refs = refs
    nrows = notes.shape[1]
    groups = nrows // GROUP

    copies = [(None, pltpu.make_async_copy(p_ref, p_here, sems.at[0]))]
    for k, ((which, at, rows), part) in enumerate(zip(places, part_refs)):
        copy = pltpu.make_async_copy(part.at[pl.ds(0, rows * edge)], held.at[piece(edge, at, rows)], sems.at[k + 1])
        copies.append((None if which is None else size[0] == which, copy))

    def each(act):
        for needed, copy in copies:
            if needed is None:
                act(copy)
            else:
                pl.when(needed)(functools.partial(act, copy))

    each(lambda copy: copy.start())

    at = jnp.int32(0)
    for r in range(nrows):
        starts[r] = at
        at = at + others_of(notes[slots, r])
    starts[nrows] = at
    low, high = 0, groups
    if name != "first":
        room = places[-1][2] if name == "early" else places[2][2]
        done = jnp.int32(0)
        for g in range(leading // GROUP):
            done = done + (starts[(g + 1) * GROUP] <= room).astype(jnp.int32)
        low, high = (0, done) if name == "early" else (done, groups)

    def total_copy(g):
        here = piece(edge, g * GROUP, GROUP)
        return pltpu.make_async_copy(total_ref.at[here], refs[0].at[here], refs[1].at[g])

    def out_copy(g):
        here = piece(edge, g * GROUP, GROUP)
        return pltpu.make_async_copy(stage.at[here], out_ref.at[here], out_sems.at[g])

    def over(act):
        def step(g, carry):
            act(g)
            return carry

        lax.fori_loop(low, high, step, 0)

    if name != "first":
        over(lambda g: total_copy(g).start())
    if name != "first":
        held[pl.ds(held.shape[0] - edge, edge), :] = jnp.zeros((edge, held.shape[1]), held.dtype)
    each(lambda copy: copy.wait())

    def group(g):
        if name != "first":
            total_copy(g).wait()
        for r in range(GROUP):
            row = g * GROUP + r
            here = piece(edge, row)
            left = left_pieces(notes, slots, edge, row, starts, held)
            value = row_product(notes, slots, edge, row, left, p_here)
            if name != "first":
                value = refs[0][here, :] + value
            stage[here, :] = value.astype(stage.dtype)
        out_copy(g).start()

    over(group)
    over(lambda g: out_copy(g).wait())


def step_product(name, notes, slots, leading, places, parts, p_tile, total=None, size=None, out=None):
    nrows = notes.shape[1]
    depth, width = p_tile.shape
    edge = parts[0].shape[1] // PAIR
    groups = nrows // GROUP
    room = max(at + rows for _, at, rows in places)
    dtype = jnp.float32 if name == "first" else jnp.bfloat16
    tall = nrows * edge
    later = name != "first"
    late = name == "late"
    return pl.pallas_call(
        functools.partial(step_kernel, edge, slots, name, leading, places),
        in_specs=[SMEM] * (1 + late) + [ANY] * (len(parts) + 1 + later) + [HBM] * late,
        out_specs=HBM if later else ANY,
        scratch_shapes=[
            pltpu.SMEM((nrows + 1,), jnp.int32),
            pltpu.VMEM(((room + later) * edge, PAIR * edge), p_tile.dtype),
            pltpu.VMEM(p_tile.shape, p_tile.dtype),
            pltpu.VMEM((tall, width), dtype),
            pltpu.SemaphoreType.DMA((len(parts) + 1,)),
            pltpu.SemaphoreType.DMA((groups,)),
        ]
        + [pltpu.VMEM((tall, width), jnp.float32), pltpu.SemaphoreType.DMA((groups,))] * later,
        out_shape=(pltpu.HBM if later else jax.ShapeDtypeStruct)((tall, width), dtype),
        input_output_aliases={4 + len(parts): 0} if late else {},
        cost_estimate=cost(tall * width * slots * edge, 4 * tall * width),
        compiler_params=params(16),
        name="step_" + name,
    )(
        notes,
        *([size] if late else []),
        *parts,
        p_tile,
        *([total] if later else []),
        *([in_hbm(out)] if late else []),
    )


def remainder(k, slots, leading, places, rests, notes, lead, extra, p_second, total):
    rest = [shifted(part, "col", -1) if k == n else part for n, part in enumerate(rests)]
    return step_product("early", notes, slots, leading, places, (lead, extra), p_second, total), rest


def body(f_blocks, block_cols, block_counts, p_matrix):
    nrows, slots = block_cols.shape
    edge = f_blocks.shape[0] // nrows
    cols, counts = block_cols.T, block_counts.T
    groups = nrows // GROUP
    leading = (groups - groups * 3 // 8) * GROUP
    others = nrows * (slots // PAIR - 1)
    unit = others // 24
    always = 10 * unit
    ends = [always + k * unit for k in (2, 3, 4, 5, 6, 7, 9)] + [others]

    lead = shifted(leading_pieces(leading, f_blocks, cols, counts), "col", -1)
    p_second = shifted(p_matrix, "row", -1)
    notes = jnp.concatenate([cols, jnp.broadcast_to(counts, (slots, nrows))], axis=0)
    packed, extra = packed_pieces(notes, slots, always, f_blocks)
    extra = shifted(extra, "col", -1)
    later, *rests = cut_pieces([(leading, nrows)] + [(nrows + always, nrows + end) for end in ends], packed)
    every = packed.shape[0] // edge
    total = step_product("first", notes, slots, leading, [(None, 0, every)], (packed,), p_matrix)
    later, total = lax.optimization_barrier((later, total))
    later = shifted(later, "col", -1)

    notes_next = lead[leading * edge :, :nrows].astype(jnp.float32).astype(jnp.int32)
    most = jnp.maximum(jnp.sum(others_of(counts)), jnp.sum(others_of(notes_next[slots])))
    distance = 2
    while distance < lax.axis_size("col"):
        most = jnp.maximum(most, shifted(most, "col", -distance))
        distance *= 2
    size = sum((most > end).astype(jnp.int32) for end in ends[:-1])
    early = [(None, 0, leading), (None, nrows, always)]
    late = [early[0], (None, leading, nrows - leading), early[1]]
    late += [(k, nrows + always, end - always) for k, end in enumerate(ends)]
    branches = [functools.partial(remainder, k, slots, leading, early) for k in range(len(ends))]
    out, rest = lax.switch(size, branches, rests, notes_next, lead, extra, p_second, total)
    parts = (lead, later, extra, *rest)
    return step_product("late", notes_next, slots, leading, late, parts, p_second, total, size.reshape(1), out)


def solution(mesh):
    return jax.shard_map(
        body,
        mesh=mesh,
        in_specs=(P("row", "col"), P("row", "col"), P("row", "col"), P("row", "col")),
        out_specs=P("row", "col"),
        check_vma=False,
    )
```

```python
import functools

import jax
import jax.numpy as jnp
from jax import lax
from jax.experimental import pallas as pl
from jax.experimental.pallas import tpu as pltpu
from jax.sharding import PartitionSpec as P

GROUP = 4
PAIR = 2

SMEM = pl.BlockSpec(memory_space=pltpu.SMEM)
ANY = pl.BlockSpec(memory_space=pl.ANY)
HBM = pl.BlockSpec(memory_space=pltpu.HBM)


def shifted(block, axis, distance):
    devices = range(lax.axis_size(axis))
    route = [((i - distance) % len(devices), i) for i in devices]
    return lax.ppermute(block, axis, route)


def in_hbm(x):
    return pltpu.with_memory_space_constraint(x, pltpu.HBM)


def params(mib):
    return pltpu.CompilerParams(vmem_limit_bytes=mib << 20)


def cost(flops, moved):
    return pl.CostEstimate(flops=flops, bytes_accessed=moved, transcendentals=0)


def piece(edge, index, count=1):
    return pl.ds(pl.multiple_of(index * edge, edge), count * edge)


def others_of(count):
    return (count + (PAIR - 1)) // PAIR - 1


def live_half(value, count, slot, edge):
    lane = lax.broadcasted_iota(jnp.int32, value.shape, 1)
    return jnp.where(lane < jnp.where(count > slot + 1, PAIR, 1) * edge, value, jnp.zeros_like(value))


def leading_kernel(edge, counts, f_ref, cols_ref, counts_ref, out_ref):
    slots, nrows = cols_ref.shape
    tall = f_ref.shape[0]
    for r in range(tall // edge):
        here = pl.ds(r * edge, edge)
        out_ref[here, :] = live_half(f_ref[here, :], counts[0, r], 0, edge)
    notes = jnp.concatenate([cols_ref[...], jnp.broadcast_to(counts_ref[...], (slots, nrows))], axis=0)
    out_ref[pl.ds(tall, 2 * slots), pl.ds(0, nrows)] = notes.astype(jnp.float32).astype(out_ref.dtype)


def leading_pieces(rows, f_blocks, cols, counts):
    slots, nrows = cols.shape
    edge = f_blocks.shape[0] // nrows
    shape = (rows * edge + 2 * slots, PAIR * edge)
    f_blocks, cols, counts = (in_hbm(x) for x in (f_blocks, cols, counts))
    return pl.pallas_call(
        functools.partial(leading_kernel, edge),
        grid_spec=pltpu.PrefetchScalarGridSpec(
            num_scalar_prefetch=1,
            grid=(1,),
            in_specs=[
                pl.BlockSpec((rows * edge, PAIR * edge), lambda g, c: (0, 0)),
                pl.BlockSpec(cols.shape, lambda g, c: (0, 0)),
                pl.BlockSpec(counts.shape, lambda g, c: (0, 0)),
            ],
            out_specs=pl.BlockSpec(shape, lambda g, c: (0, 0)),
        ),
        out_shape=jax.ShapeDtypeStruct(shape, f_blocks.dtype),
        cost_estimate=cost(0, 4 * rows * edge * PAIR * edge),
        compiler_params=params(8),
        name="leading_pieces",
    )(counts, f_blocks, cols, counts)


def pack_kernel(edge, slots, notes, f_ref, out_ref, extra_ref, f_here, packed, sems):
    nrows = notes.shape[1]
    parts = slots // PAIR
    fetched = []
    for g in range(nrows // GROUP):
        here = piece(edge, g * GROUP, GROUP)
        fetched.append(pltpu.make_async_copy(f_ref.at[here], f_here.at[here], sems.at[g]))
        fetched[-1].start()
    at = 0
    for r in range(nrows):
        if r % GROUP == 0:
            fetched[r // GROUP].wait()
        count = notes[slots, r]
        for p in range(parts):
            value = f_here[pl.ds(r * edge, edge), pl.ds(p * PAIR * edge, PAIR * edge)]
            to = r if p == 0 else nrows + at + (p - 1)
            packed[piece(edge, to), :] = live_half(value, count, p * PAIR, edge)
        at = at + others_of(count)
    packed[pl.ds(nrows * parts * edge, edge), :] = jnp.zeros((edge, PAIR * edge), packed.dtype)
    copies = [
        pltpu.make_async_copy(packed.at[pl.ds(nrows * edge, extra_ref.shape[0])], extra_ref, sems.at[0]),
        pltpu.make_async_copy(packed, out_ref, sems.at[1]),
    ]
    for copy in copies:
        copy.start()
    for copy in copies:
        copy.wait()


def packed_pieces(notes, slots, always, f_blocks):
    nrows = notes.shape[1]
    edge = f_blocks.shape[0] // nrows
    shape = ((nrows * slots // PAIR + 1) * edge, PAIR * edge)
    return pl.pallas_call(
        functools.partial(pack_kernel, edge, slots),
        in_specs=[SMEM, ANY],
        out_specs=[ANY, ANY],
        scratch_shapes=[
            pltpu.VMEM(f_blocks.shape, f_blocks.dtype),
            pltpu.VMEM(shape, f_blocks.dtype),
            pltpu.SemaphoreType.DMA((nrows // GROUP,)),
        ],
        out_shape=[
            jax.ShapeDtypeStruct(shape, f_blocks.dtype),
            jax.ShapeDtypeStruct((always * edge, PAIR * edge), f_blocks.dtype),
        ],
        cost_estimate=cost(0, 4 * f_blocks.size),
        compiler_params=params(16),
        name="pack_live_pieces",
    )(notes, f_blocks)


def cut_kernel(ranges, packed_ref, *refs):
    out_refs, sems = refs[: len(ranges)], refs[-1]
    copies = [
        pltpu.make_async_copy(packed_ref.at[pl.ds(low, high - low)], out_ref, sems.at[k])
        for k, ((low, high), out_ref) in enumerate(zip(ranges, out_refs))
    ]
    for copy in copies:
        copy.start()
    for copy in copies:
        copy.wait()


def cut_pieces(ranges, packed):
    edge = packed.shape[1] // PAIR
    rows = [(low * edge, high * edge) for low, high in ranges]
    return pl.pallas_call(
        functools.partial(cut_kernel, rows),
        in_specs=[ANY],
        out_specs=[ANY] * (2 * len(rows)),
        scratch_shapes=[pltpu.SemaphoreType.DMA((len(rows),))],
        out_shape=[jax.ShapeDtypeStruct((high - low, packed.shape[1]), packed.dtype) for low, high in rows] * 2,
        cost_estimate=cost(0, 4 * sum(high - low for low, high in rows) * packed.shape[1]),
        compiler_params=params(2),
        name="cut_pieces",
    )(packed)


def row_product(notes, slots, edge, row, left, p_ref):
    picked = [p_ref[piece(edge, notes[s, row]), :] for s in range(slots)]
    return jnp.dot(
        jnp.concatenate(left, axis=1), jnp.concatenate(picked, axis=0), preferred_element_type=jnp.float32
    )


def left_pieces(notes, slots, edge, row, starts, held):
    nrows = notes.shape[1]
    spare = held.shape[0] // edge - 1
    live = others_of(notes[slots, row])
    left = [held[piece(edge, row), :]]
    for p in range(slots // PAIR - 1):
        left.append(held[piece(edge, jnp.where(p < live, nrows + starts[row] + p, spare)), :])
    return left


def step_kernel(edge, slots, name, leading, places, notes, *refs):
    size = None
    if name == "late":
        size, *refs = refs
    part_refs, refs = refs[: len(places)], refs[len(places) :]
    p_ref, *refs = refs
    total_ref = None
    if name != "first":
        total_ref, *refs = refs
    if name == "late":
        _, *refs = refs
    out_ref, starts, held, p_here, stage, sems, out_sems, *refs = refs
    nrows = notes.shape[1]
    groups = nrows // GROUP

    p_copy = pltpu.make_async_copy(p_ref, p_here, sems.at[0])
    p_copy.start()

    at = jnp.int32(0)
    for r in range(nrows):
        starts[r] = at
        at = at + others_of(notes[slots, r])
    starts[nrows] = at
    low, high = 0, groups
    if name != "first":
        room = [count for kind, _, count in places if kind == "second"][0]
        done = jnp.int32(0)
        for g in range(leading // GROUP):
            done = done + (starts[(g + 1) * GROUP] <= room).astype(jnp.int32)
        low, high = (0, done) if name == "early" else (done, groups)

    copies = []
    for (kind, at, count), part in zip(places, part_refs):
        step = count
        if name == "late" and kind == "second":
            step = -(-count // 4)
        for first in range(0, count, step):
            needed = None
            if name == "late" and kind == "first":
                needed = low < leading // GROUP
            elif name == "late" and kind == "second":
                needed = starts[low * GROUP] < first + step
            elif not isinstance(kind, str):
                needed = size[0] == kind
            tall = min(step, count - first) * edge
            source = part.at[pl.ds(first * edge, tall)]
            target = held.at[pl.ds((at + first) * edge, tall)]
            copies.append((needed, pltpu.make_async_copy(source, target, sems.at[1 + len(copies)])))

    def each(act):
        for needed, copy in copies:
            if needed is None:
                act(copy)
            else:
                pl.when(needed)(functools.partial(act, copy))

    each(lambda copy: copy.start())

    def total_copy(g):
        here = piece(edge, g * GROUP, GROUP)
        return pltpu.make_async_copy(total_ref.at[here], refs[0].at[here], refs[1].at[g])

    def out_copy(g):
        here = piece(edge, g * GROUP, GROUP)
        return pltpu.make_async_copy(stage.at[here], out_ref.at[here], out_sems.at[g])

    def over(act):
        def step(g, carry):
            act(g)
            return carry

        lax.fori_loop(low, high, step, 0)

    if name != "first":
        over(lambda g: total_copy(g).start())
    if name != "first":
        held[pl.ds(held.shape[0] - edge, edge), :] = jnp.zeros((edge, held.shape[1]), held.dtype)
    each(lambda copy: copy.wait())
    p_copy.wait()

    def group(g):
        if name != "first":
            total_copy(g).wait()
        for r in range(GROUP):
            row = g * GROUP + r
            here = piece(edge, row)
            left = left_pieces(notes, slots, edge, row, starts, held)
            value = row_product(notes, slots, edge, row, left, p_here)
            if name != "first":
                value = refs[0][here, :] + value
            stage[here, :] = value.astype(stage.dtype)
        out_copy(g).start()

    over(group)
    over(lambda g: out_copy(g).wait())


def step_product(name, notes, slots, leading, places, parts, p_tile, total=None, size=None, out=None):
    nrows = notes.shape[1]
    depth, width = p_tile.shape
    edge = parts[0].shape[1] // PAIR
    groups = nrows // GROUP
    room = max(at + rows for _, at, rows in places)
    dtype = jnp.float32 if name == "first" else jnp.bfloat16
    tall = nrows * edge
    later = name != "first"
    late = name == "late"
    return pl.pallas_call(
        functools.partial(step_kernel, edge, slots, name, leading, places),
        in_specs=[SMEM] * (1 + late) + [ANY] * (len(parts) + 1 + later) + [HBM] * late,
        out_specs=HBM if later else ANY,
        scratch_shapes=[
            pltpu.SMEM((nrows + 1,), jnp.int32),
            pltpu.VMEM(((room + later) * edge, PAIR * edge), p_tile.dtype),
            pltpu.VMEM(p_tile.shape, p_tile.dtype),
            pltpu.VMEM((tall, width), dtype),
            pltpu.SemaphoreType.DMA((len(parts) + 8,)),
            pltpu.SemaphoreType.DMA((groups,)),
        ]
        + [pltpu.VMEM((tall, width), jnp.float32), pltpu.SemaphoreType.DMA((groups,))] * later,
        out_shape=(pltpu.HBM if later else jax.ShapeDtypeStruct)((tall, width), dtype),
        input_output_aliases={4 + len(parts): 0} if late else {},
        cost_estimate=cost(tall * width * slots * edge, 4 * tall * width),
        compiler_params=params(16),
        name="step_" + name,
    )(
        notes,
        *([size] if late else []),
        *parts,
        p_tile,
        *([total] if later else []),
        *([in_hbm(out)] if late else []),
    )


def remainder(k, slots, leading, places, rests, unused, notes, lead, extra, p_second, total):
    rest = [shifted(part, "col", -1) if k == n else other for n, (part, other) in enumerate(zip(rests, unused))]
    return step_product("early", notes, slots, leading, places, (lead, extra), p_second, total), rest


def body(f_blocks, block_cols, block_counts, p_matrix):
    nrows, slots = block_cols.shape
    edge = f_blocks.shape[0] // nrows
    cols, counts = block_cols.T, block_counts.T
    groups = nrows // GROUP
    leading = (groups - groups // 4) * GROUP
    others = nrows * (slots // PAIR - 1)
    unit = others // 24
    always = 11 * unit
    ends = [always + k * unit for k in (1, 2, 3, 4, 5, 6, 8)] + [others]

    lead, p_second = lax.optimization_barrier((leading_pieces(leading, f_blocks, cols, counts), p_matrix))
    lead = shifted(lead, "col", -1)
    notes = jnp.concatenate([cols, jnp.broadcast_to(counts, (slots, nrows))], axis=0)
    packed, extra = packed_pieces(notes, slots, always, f_blocks)
    extra = shifted(extra, "col", -1)
    p_second = shifted(p_second, "row", -1)
    rests = cut_pieces([(nrows + always, nrows + end) for end in ends] + [(leading, nrows)], packed)
    rests, later, unused = rests[: len(ends)], rests[len(ends)], rests[len(ends) + 1 : -1]
    every = packed.shape[0] // edge
    total = step_product("first", notes, slots, leading, [("all", 0, every)], (packed,), p_matrix)
    later, total = lax.optimization_barrier((later, total))
    later = shifted(later, "col", -1)

    notes_next = lead[leading * edge :, :nrows].astype(jnp.float32).astype(jnp.int32)
    most = jnp.maximum(jnp.sum(others_of(counts)), jnp.sum(others_of(notes_next[slots])))
    distance = 2
    while distance < lax.axis_size("col"):
        most = jnp.maximum(most, shifted(most, "col", -distance))
        distance *= 2
    size = sum((most > end).astype(jnp.int32) for end in ends[:-1])
    early = [("first", 0, leading), ("second", nrows, always)]
    late = [early[0], ("later", leading, nrows - leading), early[1]]
    late += [(k, nrows + always, end - always) for k, end in enumerate(ends)]
    branches = [functools.partial(remainder, k, slots, leading, early) for k in range(len(ends))]
    out, rest = lax.switch(size, branches, rests, unused, notes_next, lead, extra, p_second, total)
    parts = (lead, later, extra, *rest)
    return step_product("late", notes_next, slots, leading, late, parts, p_second, total, size.reshape(1), out)


def solution(mesh):
    return jax.shard_map(
        body,
        mesh=mesh,
        in_specs=(P("row", "col"), P("row", "col"), P("row", "col"), P("row", "col")),
        out_specs=P("row", "col"),
        check_vma=False,
    )
```

```python
import functools

import jax
import jax.numpy as jnp
from jax import lax
from jax.experimental import pallas as pl
from jax.experimental.pallas import tpu as pltpu
from jax.sharding import PartitionSpec as P

GROUP = 4
PAIR = 2

SMEM = pl.BlockSpec(memory_space=pltpu.SMEM)
ANY = pl.BlockSpec(memory_space=pl.ANY)
HBM = pl.BlockSpec(memory_space=pltpu.HBM)


def shifted(block, axis, distance):
    devices = range(lax.axis_size(axis))
    route = [((i - distance) % len(devices), i) for i in devices]
    return lax.ppermute(block, axis, route)


def in_hbm(x):
    return pltpu.with_memory_space_constraint(x, pltpu.HBM)


def params(mib):
    return pltpu.CompilerParams(vmem_limit_bytes=mib << 20)


def cost(flops, moved):
    return pl.CostEstimate(flops=flops, bytes_accessed=moved, transcendentals=0)


def piece(edge, index, count=1):
    return pl.ds(pl.multiple_of(index * edge, edge), count * edge)


def others_of(count):
    return (count + (PAIR - 1)) // PAIR - 1


def live_half(value, count, slot, edge):
    lane = lax.broadcasted_iota(jnp.int32, value.shape, 1)
    return jnp.where(lane < jnp.where(count > slot + 1, PAIR, 1) * edge, value, jnp.zeros_like(value))


def leading_kernel(edge, counts, f_ref, cols_ref, counts_ref, out_ref):
    slots, nrows = cols_ref.shape
    tall = f_ref.shape[0]
    for r in range(tall // edge):
        here = pl.ds(r * edge, edge)
        out_ref[here, :] = live_half(f_ref[here, :], counts[0, r], 0, edge)
    notes = jnp.concatenate([cols_ref[...], jnp.broadcast_to(counts_ref[...], (slots, nrows))], axis=0)
    out_ref[pl.ds(tall, 2 * slots), pl.ds(0, nrows)] = notes.astype(jnp.float32).astype(out_ref.dtype)


def leading_pieces(rows, f_blocks, cols, counts):
    slots, nrows = cols.shape
    edge = f_blocks.shape[0] // nrows
    shape = (rows * edge + 2 * slots, PAIR * edge)
    f_blocks, cols, counts = (in_hbm(x) for x in (f_blocks, cols, counts))
    return pl.pallas_call(
        functools.partial(leading_kernel, edge),
        grid_spec=pltpu.PrefetchScalarGridSpec(
            num_scalar_prefetch=1,
            grid=(1,),
            in_specs=[
                pl.BlockSpec((rows * edge, PAIR * edge), lambda g, c: (0, 0)),
                pl.BlockSpec(cols.shape, lambda g, c: (0, 0)),
                pl.BlockSpec(counts.shape, lambda g, c: (0, 0)),
            ],
            out_specs=pl.BlockSpec(shape, lambda g, c: (0, 0)),
        ),
        out_shape=jax.ShapeDtypeStruct(shape, f_blocks.dtype),
        cost_estimate=cost(0, 4 * rows * edge * PAIR * edge),
        compiler_params=params(8),
        name="leading_pieces",
    )(counts, f_blocks, cols, counts)


def pack_kernel(edge, slots, notes, f_ref, out_ref, extra_ref, f_here, packed, sems):
    nrows = notes.shape[1]
    parts = slots // PAIR
    fetched = []
    for g in range(nrows // GROUP):
        here = piece(edge, g * GROUP, GROUP)
        fetched.append(pltpu.make_async_copy(f_ref.at[here], f_here.at[here], sems.at[g]))
        fetched[-1].start()
    at = 0
    for r in range(nrows):
        if r % GROUP == 0:
            fetched[r // GROUP].wait()
        count = notes[slots, r]
        for p in range(parts):
            value = f_here[pl.ds(r * edge, edge), pl.ds(p * PAIR * edge, PAIR * edge)]
            to = r if p == 0 else nrows + at + (p - 1)
            packed[piece(edge, to), :] = live_half(value, count, p * PAIR, edge)
        at = at + others_of(count)
    packed[pl.ds(nrows * parts * edge, edge), :] = jnp.zeros((edge, PAIR * edge), packed.dtype)
    copies = [
        pltpu.make_async_copy(packed.at[pl.ds(nrows * edge, extra_ref.shape[0])], extra_ref, sems.at[0]),
        pltpu.make_async_copy(packed, out_ref, sems.at[1]),
    ]
    for copy in copies:
        copy.start()
    for copy in copies:
        copy.wait()


def packed_pieces(notes, slots, always, f_blocks):
    nrows = notes.shape[1]
    edge = f_blocks.shape[0] // nrows
    shape = ((nrows * slots // PAIR + 1) * edge, PAIR * edge)
    return pl.pallas_call(
        functools.partial(pack_kernel, edge, slots),
        in_specs=[SMEM, ANY],
        out_specs=[ANY, ANY],
        scratch_shapes=[
            pltpu.VMEM(f_blocks.shape, f_blocks.dtype),
            pltpu.VMEM(shape, f_blocks.dtype),
            pltpu.SemaphoreType.DMA((nrows // GROUP,)),
        ],
        out_shape=[
            jax.ShapeDtypeStruct(shape, f_blocks.dtype),
            jax.ShapeDtypeStruct((always * edge, PAIR * edge), f_blocks.dtype),
        ],
        cost_estimate=cost(0, 4 * f_blocks.size),
        compiler_params=params(16),
        name="pack_live_pieces",
    )(notes, f_blocks)


def cut_kernel(ranges, packed_ref, *refs):
    out_refs, sems = refs[: len(ranges)], refs[-1]
    copies = [
        pltpu.make_async_copy(packed_ref.at[pl.ds(low, high - low)], out_ref, sems.at[k])
        for k, ((low, high), out_ref) in enumerate(zip(ranges, out_refs))
    ]
    for copy in copies:
        copy.start()
    for copy in copies:
        copy.wait()


def cut_pieces(ranges, packed):
    edge = packed.shape[1] // PAIR
    rows = [(low * edge, high * edge) for low, high in ranges]
    return pl.pallas_call(
        functools.partial(cut_kernel, rows),
        in_specs=[ANY],
        out_specs=[ANY] * (2 * len(rows)),
        scratch_shapes=[pltpu.SemaphoreType.DMA((len(rows),))],
        out_shape=[jax.ShapeDtypeStruct((high - low, packed.shape[1]), packed.dtype) for low, high in rows] * 2,
        cost_estimate=cost(0, 4 * sum(high - low for low, high in rows) * packed.shape[1]),
        compiler_params=params(2),
        name="cut_pieces",
    )(packed)


def row_product(notes, slots, edge, row, left, p_ref):
    picked = [p_ref[piece(edge, notes[s, row]), :] for s in range(slots)]
    return jnp.dot(
        jnp.concatenate(left, axis=1), jnp.concatenate(picked, axis=0), preferred_element_type=jnp.float32
    )


def left_pieces(notes, slots, edge, row, starts, held):
    nrows = notes.shape[1]
    spare = held.shape[0] // edge - 1
    live = others_of(notes[slots, row])
    left = [held[piece(edge, row), :]]
    for p in range(slots // PAIR - 1):
        left.append(held[piece(edge, jnp.where(p < live, nrows + starts[row] + p, spare)), :])
    return left


def step_kernel(edge, slots, name, leading, places, notes, *refs):
    size = None
    if name == "late":
        size, *refs = refs
    part_refs, refs = refs[: len(places)], refs[len(places) :]
    p_ref, *refs = refs
    total_ref = None
    if name != "first":
        total_ref, *refs = refs
    if name == "late":
        _, *refs = refs
    out_ref, starts, held, p_here, stage, sems, out_sems, *refs = refs
    nrows = notes.shape[1]
    groups = nrows // GROUP

    p_copy = pltpu.make_async_copy(p_ref, p_here, sems.at[0])
    p_copy.start()

    at = jnp.int32(0)
    for r in range(nrows):
        starts[r] = at
        at = at + others_of(notes[slots, r])
    starts[nrows] = at
    low, high = 0, groups
    if name != "first":
        room = [count for kind, _, count in places if kind == "second"][0]
        done = jnp.int32(0)
        for g in range(leading // GROUP):
            done = done + (starts[(g + 1) * GROUP] <= room).astype(jnp.int32)
        low, high = (0, done) if name == "early" else (done, groups)

    copies = []
    for (kind, at, count), part in zip(places, part_refs):
        step = count
        if name == "late" and kind == "second":
            step = -(-count // 4)
        for first in range(0, count, step):
            needed = None
            if name == "late" and kind == "first":
                needed = low < leading // GROUP
            elif name == "late" and kind == "second":
                needed = starts[low * GROUP] < first + step
            elif not isinstance(kind, str):
                needed = size[0] == kind
            tall = min(step, count - first) * edge
            source = part.at[pl.ds(first * edge, tall)]
            target = held.at[pl.ds((at + first) * edge, tall)]
            copies.append((needed, pltpu.make_async_copy(source, target, sems.at[1 + len(copies)])))

    def each(act):
        for needed, copy in copies:
            if needed is None:
                act(copy)
            else:
                pl.when(needed)(functools.partial(act, copy))

    each(lambda copy: copy.start())

    def total_copy(g):
        here = piece(edge, g * GROUP, GROUP)
        return pltpu.make_async_copy(total_ref.at[here], refs[0].at[here], refs[1].at[g])

    def out_copy(g):
        here = piece(edge, g * GROUP, GROUP)
        return pltpu.make_async_copy(stage.at[here], out_ref.at[here], out_sems.at[g])

    def over(act):
        def step(g, carry):
            act(g)
            return carry

        lax.fori_loop(low, high, step, 0)

    if name != "first":
        over(lambda g: total_copy(g).start())
    if name != "first":
        held[pl.ds(held.shape[0] - edge, edge), :] = jnp.zeros((edge, held.shape[1]), held.dtype)
    each(lambda copy: copy.wait())
    p_copy.wait()

    def group(g):
        if name != "first":
            total_copy(g).wait()
        for r in range(GROUP):
            row = g * GROUP + r
            here = piece(edge, row)
            left = left_pieces(notes, slots, edge, row, starts, held)
            value = row_product(notes, slots, edge, row, left, p_here)
            if name != "first":
                value = refs[0][here, :] + value
            stage[here, :] = value.astype(stage.dtype)
        out_copy(g).start()

    over(group)
    over(lambda g: out_copy(g).wait())


def step_product(name, notes, slots, leading, places, parts, p_tile, total=None, size=None, out=None):
    nrows = notes.shape[1]
    depth, width = p_tile.shape
    edge = parts[0].shape[1] // PAIR
    groups = nrows // GROUP
    room = max(at + rows for _, at, rows in places)
    dtype = jnp.float32 if name == "first" else jnp.bfloat16
    tall = nrows * edge
    later = name != "first"
    late = name == "late"
    return pl.pallas_call(
        functools.partial(step_kernel, edge, slots, name, leading, places),
        in_specs=[SMEM] * (1 + late) + [ANY] * len(parts) + [HBM] * (1 + later + late),
        out_specs=HBM,
        scratch_shapes=[
            pltpu.SMEM((nrows + 1,), jnp.int32),
            pltpu.VMEM(((room + later) * edge, PAIR * edge), p_tile.dtype),
            pltpu.VMEM(p_tile.shape, p_tile.dtype),
            pltpu.VMEM((tall, width), dtype),
            pltpu.SemaphoreType.DMA((len(parts) + 8,)),
            pltpu.SemaphoreType.DMA((groups,)),
        ]
        + [pltpu.VMEM((tall, width), jnp.float32), pltpu.SemaphoreType.DMA((groups,))] * later,
        out_shape=pltpu.HBM((tall, width), dtype),
        input_output_aliases={4 + len(parts): 0} if late else {},
        cost_estimate=cost((1 if later else 20) * tall * width * slots * edge, 4 * tall * width),
        compiler_params=params(16),
        name="step_" + name,
    )(
        notes,
        *([size] if late else []),
        *parts,
        in_hbm(p_tile),
        *([in_hbm(total)] if later else []),
        *([in_hbm(out)] if late else []),
    )


def remainder(k, slots, leading, places, rests, unused, notes, lead, extra, p_second, total):
    rest = [shifted(part, "col", -1) if k == n else other for n, (part, other) in enumerate(zip(rests, unused))]
    return step_product("early", notes, slots, leading, places, (lead, extra), p_second, total), rest


def body(f_blocks, block_cols, block_counts, p_matrix):
    nrows, slots = block_cols.shape
    edge = f_blocks.shape[0] // nrows
    cols, counts = block_cols.T, block_counts.T
    groups = nrows // GROUP
    leading = (groups - groups // 4) * GROUP
    others = nrows * (slots // PAIR - 1)
    unit = others // 24
    always = 11 * unit
    ends = [always + k * unit for k in (1, 2, 3, 4, 5, 6, 8)] + [others]

    lead = shifted(leading_pieces(leading, f_blocks, cols, counts), "col", -1)
    notes = jnp.concatenate([cols, jnp.broadcast_to(counts, (slots, nrows))], axis=0)
    packed, extra = packed_pieces(notes, slots, always, f_blocks)
    extra = shifted(extra, "col", -1)
    p_second, packed = lax.optimization_barrier((p_matrix, packed))
    p_second = shifted(p_second, "row", -1)
    rests = cut_pieces([(nrows + always, nrows + end) for end in ends] + [(leading, nrows)], packed)
    rests, later, unused = rests[: len(ends)], rests[len(ends)], rests[len(ends) + 1 : -1]
    every = packed.shape[0] // edge
    notes_next = lead[leading * edge :, :nrows].astype(jnp.float32).astype(jnp.int32)
    packed, notes_next = lax.optimization_barrier((packed, notes_next))
    total = step_product("first", notes, slots, leading, [("all", 0, every)], (packed,), p_matrix)
    later, total = lax.optimization_barrier((later, total))
    later = shifted(later, "col", -1)

    most = jnp.maximum(jnp.sum(others_of(counts)), jnp.sum(others_of(notes_next[slots])))
    distance = 2
    while distance < lax.axis_size("col"):
        most = jnp.maximum(most, shifted(most, "col", -distance))
        distance *= 2
    size = sum((most > end).astype(jnp.int32) for end in ends[:-1])
    early = [("first", 0, leading), ("second", nrows, always)]
    late = [early[0], ("later", leading, nrows - leading), early[1]]
    late += [(k, nrows + always, end - always) for k, end in enumerate(ends)]
    branches = [functools.partial(remainder, k, slots, leading, early) for k in range(len(ends))]
    out, rest = lax.switch(size, branches, rests, unused, notes_next, lead, extra, p_second, total)
    parts = (lead, later, extra, *rest)
    return step_product("late", notes_next, slots, leading, late, parts, p_second, total, size.reshape(1), out)


def solution(mesh):
    return jax.shard_map(
        body,
        mesh=mesh,
        in_specs=(P("row", "col"), P("row", "col"), P("row", "col"), P("row", "col")),
        out_specs=P("row", "col"),
        check_vma=False,
    )
```

```python
import functools

import jax
import jax.numpy as jnp
from jax import lax
from jax.experimental import pallas as pl
from jax.experimental.pallas import tpu as pltpu
from jax.sharding import PartitionSpec as P

GROUP = 4
PAIR = 2
SIDE = 256
UNITS = 2

SMEM = pl.BlockSpec(memory_space=pltpu.SMEM)
ANY = pl.BlockSpec(memory_space=pl.ANY)
HBM = pl.BlockSpec(memory_space=pltpu.HBM)


def shifted(block, axis, distance):
    devices = range(lax.axis_size(axis))
    route = [((i - distance) % len(devices), i) for i in devices]
    return lax.ppermute(block, axis, route)


def in_hbm(x):
    return pltpu.with_memory_space_constraint(x, pltpu.HBM)


def params(mib):
    return pltpu.CompilerParams(vmem_limit_bytes=mib << 20)


def cost(flops, moved):
    return pl.CostEstimate(flops=flops, bytes_accessed=moved, transcendentals=0)


def piece(edge, index, count=1):
    return pl.ds(pl.multiple_of(index * edge, edge), count * edge)


def others_of(count):
    return (count + (PAIR - 1)) // PAIR - 1


def live_half(value, count, slot, edge):
    lane = lax.broadcasted_iota(jnp.int32, value.shape, 1)
    return jnp.where(lane < jnp.where(count > slot + 1, PAIR, 1) * edge, value, jnp.zeros_like(value))


def leading_kernel(edge, counts, f_ref, cols_ref, counts_ref, out_ref):
    slots, nrows = cols_ref.shape
    tall = f_ref.shape[0]
    for r in range(tall // edge):
        here = pl.ds(r * edge, edge)
        out_ref[here, :] = live_half(f_ref[here, :], counts[0, r], 0, edge)
    notes = jnp.concatenate([cols_ref[...], jnp.broadcast_to(counts_ref[...], (slots, nrows))], axis=0)
    out_ref[pl.ds(tall, 2 * slots), pl.ds(0, nrows)] = notes.astype(jnp.float32).astype(out_ref.dtype)


def leading_pieces(rows, f_blocks, cols, counts):
    slots, nrows = cols.shape
    edge = f_blocks.shape[0] // nrows
    shape = (rows * edge + 2 * slots, PAIR * edge)
    f_blocks, cols, counts = (in_hbm(x) for x in (f_blocks, cols, counts))
    return pl.pallas_call(
        functools.partial(leading_kernel, edge),
        grid_spec=pltpu.PrefetchScalarGridSpec(
            num_scalar_prefetch=1,
            grid=(1,),
            in_specs=[
                pl.BlockSpec((rows * edge, PAIR * edge), lambda g, c: (0, 0)),
                pl.BlockSpec(cols.shape, lambda g, c: (0, 0)),
                pl.BlockSpec(counts.shape, lambda g, c: (0, 0)),
            ],
            out_specs=pl.BlockSpec(shape, lambda g, c: (0, 0)),
        ),
        out_shape=jax.ShapeDtypeStruct(shape, f_blocks.dtype),
        cost_estimate=cost(0, 4 * rows * edge * PAIR * edge),
        compiler_params=params(8),
        name="leading_pieces",
    )(counts, f_blocks, cols, counts)


def pack_kernel(edge, slots, notes, f_ref, out_ref, extra_ref, f_here, packed, sems):
    nrows = notes.shape[1]
    parts = slots // PAIR
    fetched = []
    for g in range(nrows // GROUP):
        here = piece(edge, g * GROUP, GROUP)
        fetched.append(pltpu.make_async_copy(f_ref.at[here], f_here.at[here], sems.at[g]))
        fetched[-1].start()
    at = 0
    for r in range(nrows):
        if r % GROUP == 0:
            fetched[r // GROUP].wait()
        count = notes[slots, r]
        for p in range(parts):
            value = f_here[pl.ds(r * edge, edge), pl.ds(p * PAIR * edge, PAIR * edge)]
            to = r if p == 0 else nrows + at + (p - 1)
            packed[piece(edge, to), :] = live_half(value, count, p * PAIR, edge)
        at = at + others_of(count)
    packed[pl.ds(nrows * parts * edge, edge), :] = jnp.zeros((edge, PAIR * edge), packed.dtype)
    copies = [
        pltpu.make_async_copy(packed.at[pl.ds(nrows * edge, extra_ref.shape[0])], extra_ref, sems.at[0]),
        pltpu.make_async_copy(packed, out_ref, sems.at[1]),
    ]
    for copy in copies:
        copy.start()
    for copy in copies:
        copy.wait()


def packed_pieces(notes, slots, always, f_blocks):
    nrows = notes.shape[1]
    edge = f_blocks.shape[0] // nrows
    shape = ((nrows * slots // PAIR + 1) * edge, PAIR * edge)
    return pl.pallas_call(
        functools.partial(pack_kernel, edge, slots),
        in_specs=[SMEM, ANY],
        out_specs=[ANY, ANY],
        scratch_shapes=[
            pltpu.VMEM(f_blocks.shape, f_blocks.dtype),
            pltpu.VMEM(shape, f_blocks.dtype),
            pltpu.SemaphoreType.DMA((nrows // GROUP,)),
        ],
        out_shape=[
            jax.ShapeDtypeStruct(shape, f_blocks.dtype),
            jax.ShapeDtypeStruct((always * edge, PAIR * edge), f_blocks.dtype),
        ],
        cost_estimate=cost(0, 4 * f_blocks.size),
        compiler_params=params(16),
        name="pack_live_pieces",
    )(notes, f_blocks)


def cut_kernel(ranges, packed_ref, *refs):
    out_refs, sems = refs[: len(ranges)], refs[-1]
    copies = [
        pltpu.make_async_copy(packed_ref.at[pl.ds(low, high - low)], out_ref, sems.at[k])
        for k, ((low, high), out_ref) in enumerate(zip(ranges, out_refs))
    ]
    for copy in copies:
        copy.start()
    for copy in copies:
        copy.wait()


def cut_pieces(ranges, packed):
    edge = packed.shape[1] // PAIR
    rows = [(low * edge, high * edge) for low, high in ranges]
    return pl.pallas_call(
        functools.partial(cut_kernel, rows),
        in_specs=[ANY],
        out_specs=[ANY] * (2 * len(rows)),
        scratch_shapes=[pltpu.SemaphoreType.DMA((len(rows),))],
        out_shape=[jax.ShapeDtypeStruct((high - low, packed.shape[1]), packed.dtype) for low, high in rows] * 2,
        cost_estimate=cost(0, 4 * sum(high - low for low, high in rows) * packed.shape[1]),
        compiler_params=params(2),
        name="cut_pieces",
    )(packed)


def row_start(notes, slots, edge, row, left, p_ref, sums):
    step = SIDE // edge
    for k in range(slots // step):
        here = jnp.concatenate(left[k * step // PAIR : (k + 1) * step // PAIR], axis=1)
        for n, acc in enumerate(sums):
            picked = [
                p_ref[piece(edge, notes[s, row]), pl.ds(n * SIDE, SIDE)] for s in range(k * step, (k + 1) * step)
            ]
            pltpu.matmul_push_rhs(jnp.concatenate(picked, axis=0), k % 2, n % UNITS)
            pltpu.matmul_acc_lhs(acc, here, load_staged_rhs=k % 2)


def left_pieces(notes, slots, edge, row, starts, held):
    nrows = notes.shape[1]
    spare = held.shape[0] // edge - 1
    live = others_of(notes[slots, row])
    left = [held[piece(edge, row), :]]
    for p in range(slots // PAIR - 1):
        left.append(held[piece(edge, jnp.where(p < live, nrows + starts[row] + p, spare)), :])
    return left


def step_kernel(edge, slots, name, leading, places, notes, *refs):
    size = None
    if name == "late":
        size, *refs = refs
    part_refs, refs = refs[: len(places)], refs[len(places) :]
    p_ref, *refs = refs
    total_ref = None
    if name != "first":
        total_ref, *refs = refs
    if name == "late":
        _, *refs = refs
    out_ref, starts, held, p_here, stage, sems, out_sems, *refs = refs
    nrows = notes.shape[1]
    groups = nrows // GROUP
    across = p_here.shape[1] // SIDE

    p_copy = pltpu.make_async_copy(p_ref, p_here, sems.at[0])
    p_copy.start()

    at = jnp.int32(0)
    for r in range(nrows):
        starts[r] = at
        at = at + others_of(notes[slots, r])
    starts[nrows] = at
    low, high = 0, groups
    if name != "first":
        room = [count for kind, _, count in places if kind == "second"][0]
        done = jnp.int32(0)
        for g in range(leading // GROUP):
            done = done + (starts[(g + 1) * GROUP] <= room).astype(jnp.int32)
        low, high = (0, done) if name == "early" else (done, groups)

    copies = []
    for (kind, at, count), part in zip(places, part_refs):
        step = count
        if name == "late" and kind == "second":
            step = -(-count // 4)
        for first in range(0, count, step):
            needed = None
            if name == "late" and kind == "first":
                needed = low < leading // GROUP
            elif name == "late" and kind == "second":
                needed = starts[low * GROUP] < first + step
            elif not isinstance(kind, str):
                needed = size[0] == kind
            tall = min(step, count - first) * edge
            source = part.at[pl.ds(first * edge, tall)]
            target = held.at[pl.ds((at + first) * edge, tall)]
            copies.append((needed, pltpu.make_async_copy(source, target, sems.at[1 + len(copies)])))

    def each(act):
        for needed, copy in copies:
            if needed is None:
                act(copy)
            else:
                pl.when(needed)(functools.partial(act, copy))

    each(lambda copy: copy.start())

    def total_copy(g):
        here = piece(edge, g * GROUP, GROUP)
        return pltpu.make_async_copy(total_ref.at[here], refs[0].at[here], refs[1].at[g])

    def out_copy(g):
        here = piece(edge, g * GROUP, GROUP)
        return pltpu.make_async_copy(stage.at[here], out_ref.at[here], out_sems.at[g])

    def over(act):
        def step(g, carry):
            act(g)
            return carry

        lax.fori_loop(low, high, step, 0)

    if name != "first":
        over(lambda g: total_copy(g).start())
    if name != "first":
        held[pl.ds(held.shape[0] - edge, edge), :] = jnp.zeros((edge, held.shape[1]), held.dtype)
    each(lambda copy: copy.wait())
    p_copy.wait()

    def group(g, *accs):
        sums = [accs[:across], accs[across:]]
        if name != "first":
            total_copy(g).wait()
        for r in range(GROUP + 1):
            if r < GROUP:
                row = g * GROUP + r
                left = left_pieces(notes, slots, edge, row, starts, held)
                row_start(notes, slots, edge, row, left, p_here, sums[r % 2])
            if r > 0:
                here = piece(edge, g * GROUP + r - 1)
                for n, acc in enumerate(sums[(r - 1) % 2]):
                    there = pl.ds(n * SIDE, SIDE)
                    value = pltpu.matmul_pop(acc)
                    if name != "first":
                        value = refs[0][here, there] + value
                    stage[here, there] = value.astype(stage.dtype)
        out_copy(g).start()

    spaces = [pltpu.ACC(n % UNITS)((edge, SIDE), jnp.float32) for n in range(across)] * 2
    pl.run_scoped(lambda *accs: over(lambda g: group(g, *accs)), *spaces)
    over(lambda g: out_copy(g).wait())


def step_product(name, notes, slots, leading, places, parts, p_tile, total=None, size=None, out=None):
    nrows = notes.shape[1]
    depth, width = p_tile.shape
    edge = parts[0].shape[1] // PAIR
    groups = nrows // GROUP
    room = max(at + rows for _, at, rows in places)
    dtype = jnp.float32 if name == "first" else jnp.bfloat16
    tall = nrows * edge
    later = name != "first"
    late = name == "late"
    return pl.pallas_call(
        functools.partial(step_kernel, edge, slots, name, leading, places),
        in_specs=[SMEM] * (1 + late) + [ANY] * (len(parts) + 1 + later) + [HBM] * late,
        out_specs=HBM if later else ANY,
        scratch_shapes=[
            pltpu.SMEM((nrows + 1,), jnp.int32),
            pltpu.VMEM(((room + later) * edge, PAIR * edge), p_tile.dtype),
            pltpu.VMEM(p_tile.shape, p_tile.dtype),
            pltpu.VMEM((tall, width), dtype),
            pltpu.SemaphoreType.DMA((len(parts) + 8,)),
            pltpu.SemaphoreType.DMA((groups,)),
        ]
        + [pltpu.VMEM((tall, width), jnp.float32), pltpu.SemaphoreType.DMA((groups,))] * later,
        out_shape=(pltpu.HBM if later else jax.ShapeDtypeStruct)((tall, width), dtype),
        input_output_aliases={4 + len(parts): 0} if late else {},
        cost_estimate=cost((1 if later else 20) * tall * width * slots * edge, 4 * tall * width),
        compiler_params=params(16),
        name="step_" + name,
    )(
        notes,
        *([size] if late else []),
        *parts,
        p_tile,
        *([total] if later else []),
        *([in_hbm(out)] if late else []),
    )


def remainder(k, slots, leading, places, rests, unused, notes, lead, extra, p_second, total):
    rest = [shifted(part, "col", -1) if k == n else other for n, (part, other) in enumerate(zip(rests, unused))]
    return step_product("early", notes, slots, leading, places, (lead, extra), p_second, total), rest


def body(f_blocks, block_cols, block_counts, p_matrix):
    nrows, slots = block_cols.shape
    edge = f_blocks.shape[0] // nrows
    cols, counts = block_cols.T, block_counts.T
    groups = nrows // GROUP
    leading = (groups - groups // 4) * GROUP
    others = nrows * (slots // PAIR - 1)
    unit = others // 24
    always = 11 * unit
    ends = [always + k * unit for k in (1, 2, 3, 4, 5, 6, 8)] + [others]

    lead = shifted(leading_pieces(leading, f_blocks, cols, counts), "col", -1)
    notes = jnp.concatenate([cols, jnp.broadcast_to(counts, (slots, nrows))], axis=0)
    packed, extra = packed_pieces(notes, slots, always, f_blocks)
    extra = shifted(extra, "col", -1)
    p_second, packed = lax.optimization_barrier((p_matrix, packed))
    p_second = shifted(p_second, "row", -1)
    rests = cut_pieces([(nrows + always, nrows + end) for end in ends] + [(leading, nrows)], packed)
    rests, later, unused = rests[: len(ends)], rests[len(ends)], rests[len(ends) + 1 : -1]
    every = packed.shape[0] // edge
    notes_next = lead[leading * edge :, :nrows].astype(jnp.float32).astype(jnp.int32)
    packed, notes_next = lax.optimization_barrier((packed, notes_next))
    total = step_product("first", notes, slots, leading, [("all", 0, every)], (packed,), p_matrix)
    later, total = lax.optimization_barrier((later, total))
    later = shifted(later, "col", -1)

    most = jnp.maximum(jnp.sum(others_of(counts)), jnp.sum(others_of(notes_next[slots])))
    distance = 2
    while distance < lax.axis_size("col"):
        most = jnp.maximum(most, shifted(most, "col", -distance))
        distance *= 2
    size = sum((most > end).astype(jnp.int32) for end in ends[:-1])
    early = [("first", 0, leading), ("second", nrows, always)]
    late = [early[0], ("later", leading, nrows - leading), early[1]]
    late += [(k, nrows + always, end - always) for k, end in enumerate(ends)]
    branches = [functools.partial(remainder, k, slots, leading, early) for k in range(len(ends))]
    out, rest = lax.switch(size, branches, rests, unused, notes_next, lead, extra, p_second, total)
    parts = (lead, later, extra, *rest)
    return step_product("late", notes_next, slots, leading, late, parts, p_second, total, size.reshape(1), out)


def solution(mesh):
    return jax.shard_map(
        body,
        mesh=mesh,
        in_specs=(P("row", "col"), P("row", "col"), P("row", "col"), P("row", "col")),
        out_specs=P("row", "col"),
        check_vma=False,
    )
```

```python
import functools

import jax
import jax.numpy as jnp
from jax import lax
from jax.experimental import pallas as pl
from jax.experimental.pallas import tpu as pltpu
from jax.sharding import PartitionSpec as P

GROUP = 4
PAIR = 2

SMEM = pl.BlockSpec(memory_space=pltpu.SMEM)
ANY = pl.BlockSpec(memory_space=pl.ANY)
HBM = pl.BlockSpec(memory_space=pltpu.HBM)


def shifted(block, axis, distance):
    devices = range(lax.axis_size(axis))
    route = [((i - distance) % len(devices), i) for i in devices]
    return lax.ppermute(block, axis, route)


def in_hbm(x):
    return pltpu.with_memory_space_constraint(x, pltpu.HBM)


def params(mib):
    return pltpu.CompilerParams(vmem_limit_bytes=mib << 20)


def cost(flops, moved):
    return pl.CostEstimate(flops=flops, bytes_accessed=moved, transcendentals=0)


def piece(edge, index, count=1):
    return pl.ds(pl.multiple_of(index * edge, edge), count * edge)


def beyond(count):
    more = jnp.maximum(count - PAIR, 0)
    return more // PAIR, more % PAIR


def pieces_of(counts):
    full, single = beyond(counts)
    return jnp.sum(full) + (jnp.sum(single) + 1) // PAIR


def walk(counts, full_at, single_at, row_done):
    at, opened = jnp.int32(0), jnp.int32(-1)
    for r in range(len(counts)):
        full, single = beyond(counts[r])
        full_at(r, at)
        shares = jnp.logical_and(single == 1, opened >= 0)
        opens = jnp.logical_and(single == 1, opened < 0)
        single_at(r, jnp.where(shares, opened, at + full), shares)
        opened = jnp.where(opens, at + full, jnp.where(shares, -1, opened))
        at = at + full + opens.astype(jnp.int32)
        row_done(r, at, opened)


def leading_kernel(f_ref, cols_ref, counts_ref, out_ref):
    slots, nrows = cols_ref.shape
    tall = f_ref.shape[0]
    out_ref[pl.ds(0, tall), :] = f_ref[...]
    notes = jnp.concatenate([cols_ref[...], jnp.broadcast_to(counts_ref[...], (slots, nrows))], axis=0)
    out_ref[pl.ds(tall, 2 * slots), pl.ds(0, nrows)] = notes.astype(jnp.float32).astype(out_ref.dtype)


def leading_pieces(rows, f_blocks, cols, counts):
    slots, nrows = cols.shape
    edge = f_blocks.shape[0] // nrows
    shape = (rows * edge + 2 * slots, PAIR * edge)
    f_blocks, cols, counts = (in_hbm(x) for x in (f_blocks, cols, counts))
    return pl.pallas_call(
        leading_kernel,
        grid=(1,),
        in_specs=[
            pl.BlockSpec((rows * edge, PAIR * edge), lambda g: (0, 0)),
            pl.BlockSpec(cols.shape, lambda g: (0, 0)),
            pl.BlockSpec(counts.shape, lambda g: (0, 0)),
        ],
        out_specs=pl.BlockSpec(shape, lambda g: (0, 0)),
        out_shape=jax.ShapeDtypeStruct(shape, f_blocks.dtype),
        cost_estimate=cost(0, 4 * rows * edge * PAIR * edge),
        compiler_params=params(8),
        name="leading_pieces",
    )(f_blocks, cols, counts)


def pack_kernel(edge, slots, notes, f_ref, out_ref, extra_ref, f_here, packed, sems):
    nrows = notes.shape[1]
    parts = slots // PAIR
    fetched = []
    for g in range(nrows // GROUP):
        here = piece(edge, g * GROUP, GROUP)
        fetched.append(pltpu.make_async_copy(f_ref.at[here], f_here.at[here], sems.at[g]))
        fetched[-1].start()
    wide = PAIR * edge

    def strip(r, p):
        return f_here[pl.ds(r * edge, edge), pl.ds(pl.multiple_of(p * wide, wide), wide)]

    def full_at(r, at):
        if r % GROUP == 0:
            fetched[r // GROUP].wait()
        packed[pl.ds(r * edge, edge), :] = strip(r, 0)
        for p in range(1, parts):
            packed[piece(edge, nrows + at + (p - 1)), :] = strip(r, p)

    def single_at(r, at, shares):
        @pl.when(shares)
        def _():
            value = strip(r, 1 + beyond(notes[slots, r])[0])
            here = piece(edge, nrows + at)
            moved = jnp.concatenate([value[:, edge:], value[:, :edge]], axis=1)
            low = lax.broadcasted_iota(jnp.int32, value.shape, 1) < edge
            packed[here, :] = jnp.where(low, packed[here, :], moved)

    walk([notes[slots, r] for r in range(nrows)], full_at, single_at, lambda *_: None)
    copies = [
        pltpu.make_async_copy(packed.at[pl.ds(nrows * edge, extra_ref.shape[0])], extra_ref, sems.at[0]),
        pltpu.make_async_copy(packed, out_ref, sems.at[1]),
    ]
    for copy in copies:
        copy.start()
    for copy in copies:
        copy.wait()


def packed_pieces(notes, slots, always, f_blocks):
    nrows = notes.shape[1]
    edge = f_blocks.shape[0] // nrows
    shape = (nrows * slots // PAIR * edge, PAIR * edge)
    return pl.pallas_call(
        functools.partial(pack_kernel, edge, slots),
        in_specs=[SMEM, ANY],
        out_specs=[ANY, ANY],
        scratch_shapes=[
            pltpu.VMEM(f_blocks.shape, f_blocks.dtype),
            pltpu.VMEM(shape, f_blocks.dtype),
            pltpu.SemaphoreType.DMA((nrows // GROUP,)),
        ],
        out_shape=[
            jax.ShapeDtypeStruct(shape, f_blocks.dtype),
            jax.ShapeDtypeStruct((always * edge, PAIR * edge), f_blocks.dtype),
        ],
        cost_estimate=cost(0, 4 * f_blocks.size),
        compiler_params=params(16),
        name="pack_live_pieces",
    )(notes, f_blocks)


def cut_kernel(ranges, packed_ref, *refs):
    out_refs, sems = refs[: len(ranges)], refs[-1]
    copies = [
        pltpu.make_async_copy(packed_ref.at[pl.ds(low, high - low)], out_ref, sems.at[k])
        for k, ((low, high), out_ref) in enumerate(zip(ranges, out_refs))
    ]
    for copy in copies:
        copy.start()
    for copy in copies:
        copy.wait()


def cut_pieces(ranges, packed):
    edge = packed.shape[1] // PAIR
    rows = [(low * edge, high * edge) for low, high in ranges]
    return pl.pallas_call(
        functools.partial(cut_kernel, rows),
        in_specs=[ANY],
        out_specs=[ANY] * (2 * len(rows)),
        scratch_shapes=[pltpu.SemaphoreType.DMA((len(rows),))],
        out_shape=[jax.ShapeDtypeStruct((high - low, packed.shape[1]), packed.dtype) for low, high in rows] * 2,
        cost_estimate=cost(0, 4 * sum(high - low for low, high in rows) * packed.shape[1]),
        compiler_params=params(2),
        name="cut_pieces",
    )(packed)


def row_product(notes, slots, edge, row, starts, singles, held, p_ref):
    nrows = notes.shape[1]
    zero = p_ref.shape[0] // edge - 1
    count = notes[slots, row]
    full, single = beyond(count)
    code = singles[row]
    second = code % 2
    left = [held[piece(edge, row), :]]
    picks = [notes[0, row], jnp.where(count > 1, notes[1, row], zero)]
    for p in range(slots // PAIR - 1):
        alone = jnp.logical_and(p == full, single == 1)
        at = jnp.where(p < full, nrows + starts[row] + p, jnp.where(alone, nrows + code // 2, row))
        left.append(held[piece(edge, at), :])
        even, odd = notes[PAIR * (p + 1), row], notes[PAIR * (p + 1) + 1, row]
        picks.append(jnp.where(jnp.logical_or(p < full, jnp.logical_and(alone, second == 0)), even, zero))
        picks.append(jnp.where(p < full, odd, jnp.where(jnp.logical_and(alone, second == 1), even, zero)))
    picked = [p_ref[piece(edge, pick), :] for pick in picks]
    return jnp.dot(
        jnp.concatenate(left, axis=1), jnp.concatenate(picked, axis=0), preferred_element_type=jnp.float32
    )


def step_kernel(edge, slots, name, leading, places, notes, *refs):
    size = None
    if name == "late":
        size, *refs = refs
    part_refs, refs = refs[: len(places)], refs[len(places) :]
    p_ref, *refs = refs
    total_ref = None
    if name != "first":
        total_ref, *refs = refs
    if name == "late":
        _, *refs = refs
    out_ref, starts, singles, opened, held, p_here, stage, sems, out_sems, *refs = refs
    nrows = notes.shape[1]
    groups = nrows // GROUP

    depth = p_ref.shape[0]
    p_copy = pltpu.make_async_copy(p_ref, p_here.at[pl.ds(0, depth)], sems.at[0])
    p_copy.start()
    p_here[pl.ds(depth, edge), :] = jnp.zeros((edge, p_here.shape[1]), p_here.dtype)

    def full_at(r, at):
        starts[r] = at

    def single_at(r, at, shares):
        singles[r] = at * 2 + shares.astype(jnp.int32)

    def row_done(r, at, still):
        starts[r + 1] = at
        opened[r + 1] = jnp.where(still < 0, at, still)

    opened[0] = jnp.int32(0)
    walk([notes[slots, r] for r in range(nrows)], full_at, single_at, row_done)
    low, high = 0, groups
    if name != "first":
        room = [count for kind, _, count in places if kind == "second"][0]
        done = jnp.int32(0)
        for g in range(leading // GROUP):
            done = done + (starts[(g + 1) * GROUP] <= room).astype(jnp.int32)
        low, high = (0, done) if name == "early" else (done, groups)

    copies = []
    for (kind, at, count), part in zip(places, part_refs):
        step = count
        if name == "late" and kind == "second":
            step = -(-count // 4)
        for first in range(0, count, step):
            needed = None
            if name == "late" and kind == "first":
                needed = low < leading // GROUP
            elif name == "late" and kind == "second":
                needed = opened[low * GROUP] < first + step
            elif not isinstance(kind, str):
                needed = size[0] == kind
            tall = min(step, count - first) * edge
            source = part.at[pl.ds(first * edge, tall)]
            target = held.at[pl.ds((at + first) * edge, tall)]
            copies.append((needed, pltpu.make_async_copy(source, target, sems.at[1 + len(copies)])))

    def each(act):
        for needed, copy in copies:
            if needed is None:
                act(copy)
            else:
                pl.when(needed)(functools.partial(act, copy))

    each(lambda copy: copy.start())

    def total_copy(g):
        here = piece(edge, g * GROUP, GROUP)
        return pltpu.make_async_copy(total_ref.at[here], refs[0].at[here], refs[1].at[g])

    def out_copy(g):
        here = piece(edge, g * GROUP, GROUP)
        return pltpu.make_async_copy(stage.at[here], out_ref.at[here], out_sems.at[g])

    def over(act):
        def step(g, carry):
            act(g)
            return carry

        lax.fori_loop(low, high, step, 0)

    if name != "first":
        over(lambda g: total_copy(g).start())
    each(lambda copy: copy.wait())
    p_copy.wait()

    def group(g):
        if name != "first":
            total_copy(g).wait()
        for r in range(GROUP):
            row = g * GROUP + r
            here = piece(edge, row)
            value = row_product(notes, slots, edge, row, starts, singles, held, p_here)
            if name != "first":
                value = refs[0][here, :] + value
            stage[here, :] = value.astype(stage.dtype)
        out_copy(g).start()

    over(group)
    over(lambda g: out_copy(g).wait())


def step_product(name, notes, slots, leading, places, parts, p_tile, total=None, size=None, out=None):
    nrows = notes.shape[1]
    depth, width = p_tile.shape
    edge = parts[0].shape[1] // PAIR
    groups = nrows // GROUP
    room = max(at + rows for _, at, rows in places)
    dtype = jnp.float32 if name == "first" else jnp.bfloat16
    tall = nrows * edge
    later = name != "first"
    late = name == "late"
    return pl.pallas_call(
        functools.partial(step_kernel, edge, slots, name, leading, places),
        in_specs=[SMEM] * (1 + late) + [ANY] * len(parts) + [HBM] * (1 + later + late),
        out_specs=HBM,
        scratch_shapes=[
            pltpu.SMEM((nrows + 1,), jnp.int32),
            pltpu.SMEM((nrows,), jnp.int32),
            pltpu.SMEM((nrows + 1,), jnp.int32),
            pltpu.VMEM((room * edge, PAIR * edge), p_tile.dtype),
            pltpu.VMEM((depth + edge, width), p_tile.dtype),
            pltpu.VMEM((tall, width), dtype),
            pltpu.SemaphoreType.DMA((len(parts) + 8,)),
            pltpu.SemaphoreType.DMA((groups,)),
        ]
        + [pltpu.VMEM((tall, width), jnp.float32), pltpu.SemaphoreType.DMA((groups,))] * later,
        out_shape=pltpu.HBM((tall, width), dtype),
        input_output_aliases={4 + len(parts): 0} if late else {},
        cost_estimate=cost((1 if later else 20) * tall * width * slots * edge, 4 * tall * width),
        compiler_params=params(16),
        name="step_" + name,
    )(
        notes,
        *([size] if late else []),
        *parts,
        in_hbm(p_tile),
        *([in_hbm(total)] if later else []),
        *([in_hbm(out)] if late else []),
    )


def remainder(k, slots, leading, places, rests, unused, notes, lead, extra, p_second, total):
    rest = [shifted(part, "col", -1) if k == n else other for n, (part, other) in enumerate(zip(rests, unused))]
    return step_product("early", notes, slots, leading, places, (lead, extra), p_second, total), rest


def body(f_blocks, block_cols, block_counts, p_matrix):
    nrows, slots = block_cols.shape
    edge = f_blocks.shape[0] // nrows
    cols, counts = block_cols.T, block_counts.T
    groups = nrows // GROUP
    leading = (groups - groups // 4) * GROUP
    others = nrows * (slots // PAIR - 1)
    unit = others // 24
    always = 10 * unit
    ends = [always + k * unit for k in (1, 2, 3, 4, 5, 6, 8)] + [others]

    lead = shifted(leading_pieces(leading, f_blocks, cols, counts), "col", -1)
    notes = jnp.concatenate([cols, jnp.broadcast_to(counts, (slots, nrows))], axis=0)
    packed, extra = packed_pieces(notes, slots, always, f_blocks)
    extra = shifted(extra, "col", -1)
    p_second, packed = lax.optimization_barrier((p_matrix, packed))
    p_second = shifted(p_second, "row", -1)
    rests = cut_pieces([(nrows + always, nrows + end) for end in ends] + [(leading, nrows)], packed)
    rests, later, unused = rests[: len(ends)], rests[len(ends)], rests[len(ends) + 1 : -1]
    every = packed.shape[0] // edge
    notes_next = lead[leading * edge :, :nrows].astype(jnp.float32).astype(jnp.int32)
    packed, notes_next = lax.optimization_barrier((packed, notes_next))
    total = step_product("first", notes, slots, leading, [("all", 0, every)], (packed,), p_matrix)
    later, total = lax.optimization_barrier((later, total))
    later = shifted(later, "col", -1)

    most = jnp.maximum(pieces_of(counts), pieces_of(notes_next[slots]))
    distance = 2
    while distance < lax.axis_size("col"):
        most = jnp.maximum(most, shifted(most, "col", -distance))
        distance *= 2
    size = sum((most > end).astype(jnp.int32) for end in ends[:-1])
    early = [("first", 0, leading), ("second", nrows, always)]
    late = [early[0], ("later", leading, nrows - leading), early[1]]
    late += [(k, nrows + always, end - always) for k, end in enumerate(ends)]
    branches = [functools.partial(remainder, k, slots, leading, early) for k in range(len(ends))]
    out, rest = lax.switch(size, branches, rests, unused, notes_next, lead, extra, p_second, total)
    parts = (lead, later, extra, *rest)
    return step_product("late", notes_next, slots, leading, late, parts, p_second, total, size.reshape(1), out)


def solution(mesh):
    return jax.shard_map(
        body,
        mesh=mesh,
        in_specs=(P("row", "col"), P("row", "col"), P("row", "col"), P("row", "col")),
        out_specs=P("row", "col"),
        check_vma=False,
    )
```

```python
import functools

import jax
import jax.numpy as jnp
from jax import lax
from jax.experimental import pallas as pl
from jax.experimental.pallas import tpu as pltpu
from jax.sharding import PartitionSpec as P

GROUP = 4
PAIR = 2

SMEM = pl.BlockSpec(memory_space=pltpu.SMEM)
ANY = pl.BlockSpec(memory_space=pl.ANY)
HBM = pl.BlockSpec(memory_space=pltpu.HBM)


def shifted(block, axis, distance):
    devices = range(lax.axis_size(axis))
    route = [((i - distance) % len(devices), i) for i in devices]
    return lax.ppermute(block, axis, route)


def in_hbm(x):
    return pltpu.with_memory_space_constraint(x, pltpu.HBM)


def params(mib):
    return pltpu.CompilerParams(vmem_limit_bytes=mib << 20)


def cost(flops, moved):
    return pl.CostEstimate(flops=flops, bytes_accessed=moved, transcendentals=0)


def piece(edge, index, count=1):
    return pl.ds(pl.multiple_of(index * edge, edge), count * edge)


def beyond(count):
    more = jnp.maximum(count - PAIR, 0)
    return more // PAIR, more % PAIR


def walk(counts, full_at, single_at, row_done):
    at, opened = jnp.int32(0), jnp.int32(-1)
    for r in range(len(counts)):
        full, single = beyond(counts[r])
        full_at(r, at)
        shares = jnp.logical_and(single == 1, opened >= 0)
        opens = jnp.logical_and(single == 1, opened < 0)
        single_at(r, jnp.where(shares, opened, at + full), shares)
        opened = jnp.where(opens, at + full, jnp.where(shares, -1, opened))
        at = at + full + opens.astype(jnp.int32)
        row_done(r, at, opened)


def write_table(notes, slots, table):
    nrows = notes.shape[1]

    def full_at(r, at):
        table[0, r] = at

    def single_at(r, at, shares):
        table[1, r] = at * 2 + shares.astype(jnp.int32)

    def row_done(r, at, opened):
        table[0, r + 1] = at
        table[2, r + 1] = jnp.where(opened < 0, at, opened)

    table[2, 0] = jnp.int32(0)
    walk([notes[slots, r] for r in range(nrows)], full_at, single_at, row_done)


def table_shape(nrows):
    return jax.ShapeDtypeStruct((3, nrows + 1), jnp.int32)


def read_kernel(slots, notes, notes_next, table, most_ref):
    write_table(notes_next, slots, table)
    nrows = notes.shape[1]
    full, single = jnp.int32(0), jnp.int32(0)
    for r in range(nrows):
        more, rest = beyond(notes[slots, r])
        full, single = full + more, single + rest
    most = jnp.maximum(full + (single + 1) // PAIR, table[0, nrows])
    most_ref[...] = jnp.full(most_ref.shape, most, jnp.int32)


def read_notes(notes, notes_next, slots):
    return pl.pallas_call(
        functools.partial(read_kernel, slots),
        in_specs=[SMEM, SMEM],
        out_specs=[SMEM, pl.BlockSpec(memory_space=pltpu.VMEM)],
        out_shape=[table_shape(notes.shape[1]), jax.ShapeDtypeStruct((8, 128), jnp.int32)],
        cost_estimate=cost(20 << 30, 4096),
        compiler_params=params(2),
        name="read_notes",
    )(notes, notes_next)


def pick_kernel(ends, one_ref, other_ref, size):
    most = jnp.max(jnp.maximum(one_ref[...], other_ref[...]))
    index = jnp.int32(0)
    for end in ends[:-1]:
        index = index + (most > end).astype(jnp.int32)
    size[0] = index


def pick_size(ends, one, other):
    vector = pl.BlockSpec(memory_space=pltpu.VMEM)
    return pl.pallas_call(
        functools.partial(pick_kernel, ends),
        in_specs=[vector, vector],
        out_specs=SMEM,
        out_shape=jax.ShapeDtypeStruct((1,), jnp.int32),
        cost_estimate=cost(0, 4096),
        compiler_params=params(2),
        name="pick_size",
    )(one, other)


def leading_kernel(f_ref, cols_ref, counts_ref, out_ref):
    slots, nrows = cols_ref.shape
    tall = f_ref.shape[0]
    out_ref[pl.ds(0, tall), :] = f_ref[...]
    notes = jnp.concatenate([cols_ref[...], jnp.broadcast_to(counts_ref[...], (slots, nrows))], axis=0)
    out_ref[pl.ds(tall, 2 * slots), pl.ds(0, nrows)] = notes.astype(jnp.float32).astype(out_ref.dtype)


def leading_pieces(rows, f_blocks, cols, counts):
    slots, nrows = cols.shape
    edge = f_blocks.shape[0] // nrows
    shape = (rows * edge + 2 * slots, PAIR * edge)
    f_blocks, cols, counts = (in_hbm(x) for x in (f_blocks, cols, counts))
    return pl.pallas_call(
        leading_kernel,
        grid=(1,),
        in_specs=[
            pl.BlockSpec((rows * edge, PAIR * edge), lambda g: (0, 0)),
            pl.BlockSpec(cols.shape, lambda g: (0, 0)),
            pl.BlockSpec(counts.shape, lambda g: (0, 0)),
        ],
        out_specs=pl.BlockSpec(shape, lambda g: (0, 0)),
        out_shape=jax.ShapeDtypeStruct(shape, f_blocks.dtype),
        cost_estimate=cost(0, 4 * rows * edge * PAIR * edge),
        compiler_params=params(8),
        name="leading_pieces",
    )(f_blocks, cols, counts)


def pack_kernel(edge, slots, notes, f_ref, out_ref, extra_ref, table, f_here, packed, sems):
    nrows = notes.shape[1]
    parts = slots // PAIR
    fetched = []
    for g in range(nrows // GROUP):
        here = piece(edge, g * GROUP, GROUP)
        fetched.append(pltpu.make_async_copy(f_ref.at[here], f_here.at[here], sems.at[g]))
        fetched[-1].start()
    wide = PAIR * edge

    def strip(r, p):
        return f_here[pl.ds(r * edge, edge), pl.ds(pl.multiple_of(p * wide, wide), wide)]

    def full_at(r, at):
        if r % GROUP == 0:
            fetched[r // GROUP].wait()
        packed[pl.ds(r * edge, edge), :] = strip(r, 0)
        for p in range(1, parts):
            packed[piece(edge, nrows + at + (p - 1)), :] = strip(r, p)

    def single_at(r, at, shares):
        @pl.when(shares)
        def _():
            value = strip(r, 1 + beyond(notes[slots, r])[0])
            here = piece(edge, nrows + at)
            moved = jnp.concatenate([value[:, edge:], value[:, :edge]], axis=1)
            low = lax.broadcasted_iota(jnp.int32, value.shape, 1) < edge
            packed[here, :] = jnp.where(low, packed[here, :], moved)

    walk([notes[slots, r] for r in range(nrows)], full_at, single_at, lambda *_: None)
    copies = [
        pltpu.make_async_copy(packed.at[pl.ds(nrows * edge, extra_ref.shape[0])], extra_ref, sems.at[0]),
        pltpu.make_async_copy(packed, out_ref, sems.at[1]),
    ]
    for copy in copies:
        copy.start()
    write_table(notes, slots, table)
    for copy in copies:
        copy.wait()


def packed_pieces(notes, slots, always, f_blocks):
    nrows = notes.shape[1]
    edge = f_blocks.shape[0] // nrows
    shape = (nrows * slots // PAIR * edge, PAIR * edge)
    return pl.pallas_call(
        functools.partial(pack_kernel, edge, slots),
        in_specs=[SMEM, ANY],
        out_specs=[ANY, ANY, SMEM],
        scratch_shapes=[
            pltpu.VMEM(f_blocks.shape, f_blocks.dtype),
            pltpu.VMEM(shape, f_blocks.dtype),
            pltpu.SemaphoreType.DMA((nrows // GROUP,)),
        ],
        out_shape=[
            jax.ShapeDtypeStruct(shape, f_blocks.dtype),
            jax.ShapeDtypeStruct((always * edge, PAIR * edge), f_blocks.dtype),
            table_shape(nrows),
        ],
        cost_estimate=cost(0, 4 * f_blocks.size),
        compiler_params=params(16),
        name="pack_live_pieces",
    )(notes, f_blocks)


def cut_kernel(ranges, packed_ref, *refs):
    out_refs, sems = refs[: len(ranges)], refs[-1]
    copies = [
        pltpu.make_async_copy(packed_ref.at[pl.ds(low, high - low)], out_ref, sems.at[k])
        for k, ((low, high), out_ref) in enumerate(zip(ranges, out_refs))
    ]
    for copy in copies:
        copy.start()
    for copy in copies:
        copy.wait()


def cut_pieces(ranges, packed):
    edge = packed.shape[1] // PAIR
    rows = [(low * edge, high * edge) for low, high in ranges]
    return pl.pallas_call(
        functools.partial(cut_kernel, rows),
        in_specs=[ANY],
        out_specs=[ANY] * (2 * len(rows)),
        scratch_shapes=[pltpu.SemaphoreType.DMA((len(rows),))],
        out_shape=[jax.ShapeDtypeStruct((high - low, packed.shape[1]), packed.dtype) for low, high in rows] * 2,
        cost_estimate=cost(0, 4 * sum(high - low for low, high in rows) * packed.shape[1]),
        compiler_params=params(2),
        name="cut_pieces",
    )(packed)


def row_product(notes, table, slots, edge, row, held, p_ref):
    nrows = notes.shape[1]
    zero = p_ref.shape[0] // edge - 1
    count = notes[slots, row]
    full, single = beyond(count)
    code = table[1, row]
    second = code % 2
    left = [held[piece(edge, row), :]]
    picks = [notes[0, row], jnp.where(count > 1, notes[1, row], zero)]
    for p in range(slots // PAIR - 1):
        alone = jnp.logical_and(p == full, single == 1)
        at = jnp.where(p < full, nrows + table[0, row] + p, jnp.where(alone, nrows + code // 2, row))
        left.append(held[piece(edge, at), :])
        even, odd = notes[PAIR * (p + 1), row], notes[PAIR * (p + 1) + 1, row]
        picks.append(jnp.where(jnp.logical_or(p < full, jnp.logical_and(alone, second == 0)), even, zero))
        picks.append(jnp.where(p < full, odd, jnp.where(jnp.logical_and(alone, second == 1), even, zero)))
    picked = [p_ref[piece(edge, pick), :] for pick in picks]
    return jnp.dot(
        jnp.concatenate(left, axis=1), jnp.concatenate(picked, axis=0), preferred_element_type=jnp.float32
    )


def step_kernel(edge, slots, name, leading, places, notes, table, *refs):
    size = None
    if name == "late":
        size, *refs = refs
    part_refs, refs = refs[: len(places)], refs[len(places) :]
    p_ref, *refs = refs
    total_ref = None
    if name != "first":
        total_ref, *refs = refs
    if name == "late":
        _, *refs = refs
    out_ref, held, p_here, stage, sems, out_sems, *refs = refs
    nrows = notes.shape[1]
    groups = nrows // GROUP

    depth = p_ref.shape[0]
    p_copy = pltpu.make_async_copy(p_ref, p_here.at[pl.ds(0, depth)], sems.at[0])
    p_copy.start()
    p_here[pl.ds(depth, edge), :] = jnp.zeros((edge, p_here.shape[1]), p_here.dtype)

    low, high = 0, groups
    if name != "first":
        room = [count for kind, _, count in places if kind == "second"][0]
        done = jnp.int32(0)
        for g in range(leading // GROUP):
            done = done + (table[0, (g + 1) * GROUP] <= room).astype(jnp.int32)
        low, high = (0, done) if name == "early" else (done, groups)

    copies = []
    for (kind, at, count), part in zip(places, part_refs):
        step = count
        if name == "late" and kind == "second":
            step = -(-count // 4)
        for first in range(0, count, step):
            needed = None
            if name == "late" and kind == "first":
                needed = low < leading // GROUP
            elif name == "late" and kind == "second":
                needed = table[2, low * GROUP] < first + step
            elif not isinstance(kind, str):
                needed = size[0] == kind
            tall = min(step, count - first) * edge
            source = part.at[pl.ds(first * edge, tall)]
            target = held.at[pl.ds((at + first) * edge, tall)]
            copies.append((needed, pltpu.make_async_copy(source, target, sems.at[1 + len(copies)])))

    def each(act):
        for needed, copy in copies:
            if needed is None:
                act(copy)
            else:
                pl.when(needed)(functools.partial(act, copy))

    each(lambda copy: copy.start())

    def total_copy(g):
        here = piece(edge, g * GROUP, GROUP)
        return pltpu.make_async_copy(total_ref.at[here], refs[0].at[here], refs[1].at[g])

    def out_copy(g):
        here = piece(edge, g * GROUP, GROUP)
        return pltpu.make_async_copy(stage.at[here], out_ref.at[here], out_sems.at[g])

    def over(act):
        def step(g, carry):
            act(g)
            return carry

        lax.fori_loop(low, high, step, 0)

    if name != "first":
        over(lambda g: total_copy(g).start())
    each(lambda copy: copy.wait())
    p_copy.wait()

    def group(g):
        if name != "first":
            total_copy(g).wait()
        for r in range(GROUP):
            row = g * GROUP + r
            here = piece(edge, row)
            value = row_product(notes, table, slots, edge, row, held, p_here)
            if name != "first":
                value = refs[0][here, :] + value
            stage[here, :] = value.astype(stage.dtype)
        out_copy(g).start()

    over(group)
    over(lambda g: out_copy(g).wait())


def step_product(name, notes, table, slots, leading, places, parts, p_tile, total=None, size=None, out=None):
    nrows = notes.shape[1]
    depth, width = p_tile.shape
    edge = parts[0].shape[1] // PAIR
    groups = nrows // GROUP
    room = max(at + rows for _, at, rows in places)
    dtype = jnp.float32 if name == "first" else jnp.bfloat16
    tall = nrows * edge
    later = name != "first"
    late = name == "late"
    return pl.pallas_call(
        functools.partial(step_kernel, edge, slots, name, leading, places),
        in_specs=[SMEM] * (2 + late) + [ANY] * len(parts) + [HBM] * (1 + later + late),
        out_specs=HBM,
        scratch_shapes=[
            pltpu.VMEM((room * edge, PAIR * edge), p_tile.dtype),
            pltpu.VMEM((depth + edge, width), p_tile.dtype),
            pltpu.VMEM((tall, width), dtype),
            pltpu.SemaphoreType.DMA((len(parts) + 8,)),
            pltpu.SemaphoreType.DMA((groups,)),
        ]
        + [pltpu.VMEM((tall, width), jnp.float32), pltpu.SemaphoreType.DMA((groups,))] * later,
        out_shape=pltpu.HBM((tall, width), dtype),
        input_output_aliases={5 + len(parts): 0} if late else {},
        cost_estimate=cost(tall * width * slots * edge, 4 * tall * width),
        compiler_params=params(16),
        name="step_" + name,
    )(
        notes,
        table,
        *([size] if late else []),
        *parts,
        in_hbm(p_tile),
        *([in_hbm(total)] if later else []),
        *([in_hbm(out)] if late else []),
    )


def remainder(k, slots, leading, places, rests, unused, notes, table, lead, extra, p_second, total):
    rest = [shifted(part, "col", -1) if k == n else other for n, (part, other) in enumerate(zip(rests, unused))]
    return step_product("early", notes, table, slots, leading, places, (lead, extra), p_second, total), rest


def body(f_blocks, block_cols, block_counts, p_matrix):
    nrows, slots = block_cols.shape
    edge = f_blocks.shape[0] // nrows
    cols, counts = block_cols.T, block_counts.T
    groups = nrows // GROUP
    leading = (groups - groups // 4) * GROUP
    others = nrows * (slots // PAIR - 1)
    unit = others // 24
    always = 10 * unit
    ends = [always + k * unit for k in (1, 2, 3, 4, 5, 6, 8)] + [others]

    lead = shifted(leading_pieces(leading, f_blocks, cols, counts), "col", -1)
    notes = jnp.concatenate([cols, jnp.broadcast_to(counts, (slots, nrows))], axis=0)
    packed, extra, table = packed_pieces(notes, slots, always, f_blocks)
    extra = shifted(extra, "col", -1)
    p_second, packed = lax.optimization_barrier((p_matrix, packed))
    p_second = shifted(p_second, "row", -1)
    rests = cut_pieces([(nrows + always, nrows + end) for end in ends] + [(leading, nrows)], packed)
    rests, later, unused = rests[: len(ends)], rests[len(ends)], rests[len(ends) + 1 : -1]
    every = packed.shape[0] // edge
    total = step_product("first", notes, table, slots, leading, [("all", 0, every)], (packed,), p_matrix)
    later, total, lead = lax.optimization_barrier((later, total, lead))
    later = shifted(later, "col", -1)

    notes_next = lead[leading * edge :, :nrows].astype(jnp.float32).astype(jnp.int32)
    table_next, most = read_notes(notes, notes_next, slots)
    other = most
    distance = 2
    while distance < lax.axis_size("col"):
        most = jnp.maximum(most, other)
        other = shifted(most, "col", -distance)
        distance *= 2
    size = pick_size(ends, most, other)
    early = [("first", 0, leading), ("second", nrows, always)]
    late = [early[0], ("later", leading, nrows - leading), early[1]]
    late += [(k, nrows + always, end - always) for k, end in enumerate(ends)]
    branches = [functools.partial(remainder, k, slots, leading, early) for k in range(len(ends))]
    out, rest = lax.switch(size[0], branches, rests, unused, notes_next, table_next, lead, extra, p_second, total)
    parts = (lead, later, extra, *rest)
    return step_product("late", notes_next, table_next, slots, leading, late, parts, p_second, total, size, out)


def solution(mesh):
    return jax.shard_map(
        body,
        mesh=mesh,
        in_specs=(P("row", "col"), P("row", "col"), P("row", "col"), P("row", "col")),
        out_specs=P("row", "col"),
        check_vma=False,
    )
```

```python
import functools

import jax
import jax.numpy as jnp
from jax import lax
from jax.experimental import pallas as pl
from jax.experimental.pallas import tpu as pltpu
from jax.sharding import PartitionSpec as P

GROUP = 4
PAIR = 2

SMEM = pl.BlockSpec(memory_space=pltpu.SMEM)
ANY = pl.BlockSpec(memory_space=pl.ANY)
HBM = pl.BlockSpec(memory_space=pltpu.HBM)


def shifted(block, axis, distance):
    devices = range(lax.axis_size(axis))
    route = [((i - distance) % len(devices), i) for i in devices]
    return lax.ppermute(block, axis, route)


def in_hbm(x):
    return pltpu.with_memory_space_constraint(x, pltpu.HBM)


def params(mib):
    return pltpu.CompilerParams(vmem_limit_bytes=mib << 20)


def cost(flops, moved):
    return pl.CostEstimate(flops=flops, bytes_accessed=moved, transcendentals=0)


def piece(edge, index, count=1):
    return pl.ds(pl.multiple_of(index * edge, edge), count * edge)


def beyond(count):
    more = jnp.maximum(count - PAIR, 0)
    return more // PAIR, more % PAIR


def walk(counts, full_at, single_at, row_done):
    at, opened = jnp.int32(0), jnp.int32(-1)
    for r in range(len(counts)):
        full, single = beyond(counts[r])
        full_at(r, at)
        shares = jnp.logical_and(single == 1, opened >= 0)
        opens = jnp.logical_and(single == 1, opened < 0)
        single_at(r, jnp.where(shares, opened, at + full), shares)
        opened = jnp.where(opens, at + full, jnp.where(shares, -1, opened))
        at = at + full + opens.astype(jnp.int32)
        row_done(r, at, opened)


def write_table(notes, slots, zero, table):
    nrows = notes.shape[1]
    others = slots // PAIR - 1
    places = {}

    def full_at(r, at):
        table[0, r] = at
        places[r] = at

    def single_at(r, at, shares):
        count = notes[slots, r]
        full, single = beyond(count)
        table[2 + others, r] = notes[0, r]
        table[3 + others, r] = jnp.where(count > 1, notes[1, r], zero)
        for p in range(others):
            alone = jnp.logical_and(p == full, single == 1)
            table[2 + p, r] = jnp.where(p < full, nrows + places[r] + p, jnp.where(alone, nrows + at, r))
            even, odd = notes[PAIR * (p + 1), r], notes[PAIR * (p + 1) + 1, r]
            first = jnp.logical_or(p < full, jnp.logical_and(alone, jnp.logical_not(shares)))
            row = 2 + others + PAIR * (p + 1)
            table[row, r] = jnp.where(first, even, zero)
            table[row + 1, r] = jnp.where(p < full, odd, jnp.where(jnp.logical_and(alone, shares), even, zero))

    def row_done(r, at, opened):
        table[0, r + 1] = at
        table[1, r + 1] = jnp.where(opened < 0, at, opened)

    table[1, 0] = jnp.int32(0)
    walk([notes[slots, r] for r in range(nrows)], full_at, single_at, row_done)


def table_shape(nrows, slots):
    return jax.ShapeDtypeStruct((2 + slots // PAIR - 1 + slots, nrows + 1), jnp.int32)


def read_kernel(slots, notes, notes_next, most_ref):
    most = jnp.int32(0)
    for tile in (notes, notes_next):
        full, single = jnp.int32(0), jnp.int32(0)
        for r in range(tile.shape[1]):
            more, rest = beyond(tile[slots, r])
            full, single = full + more, single + rest
        most = jnp.maximum(most, full + (single + 1) // PAIR)
    most_ref[...] = jnp.full(most_ref.shape, most, jnp.int32)


def read_notes(notes, notes_next, slots):
    return pl.pallas_call(
        functools.partial(read_kernel, slots),
        in_specs=[SMEM, SMEM],
        out_specs=pl.BlockSpec(memory_space=pltpu.VMEM),
        out_shape=jax.ShapeDtypeStruct((8, 128), jnp.int32),
        cost_estimate=cost(20 << 30, 4096),
        compiler_params=params(2),
        name="read_notes",
    )(notes, notes_next)


def table_of(notes, slots, zero):
    return pl.pallas_call(
        lambda notes, table: write_table(notes, slots, zero, table),
        in_specs=[SMEM],
        out_specs=SMEM,
        out_shape=table_shape(notes.shape[1], slots),
        cost_estimate=cost(0, 4096),
        compiler_params=params(2),
        name="make_table",
    )(notes)


def pick_kernel(ends, one_ref, other_ref, size):
    most = jnp.max(jnp.maximum(one_ref[...], other_ref[...]))
    index = jnp.int32(0)
    for end in ends[:-1]:
        index = index + (most > end).astype(jnp.int32)
    size[0] = index


def pick_size(ends, one, other):
    vector = pl.BlockSpec(memory_space=pltpu.VMEM)
    return pl.pallas_call(
        functools.partial(pick_kernel, ends),
        in_specs=[vector, vector],
        out_specs=SMEM,
        out_shape=jax.ShapeDtypeStruct((1,), jnp.int32),
        cost_estimate=cost(0, 4096),
        compiler_params=params(2),
        name="pick_size",
    )(one, other)


def leading_kernel(f_ref, cols_ref, counts_ref, out_ref):
    slots, nrows = cols_ref.shape
    tall = f_ref.shape[0]
    out_ref[pl.ds(0, tall), :] = f_ref[...]
    notes = jnp.concatenate([cols_ref[...], jnp.broadcast_to(counts_ref[...], (slots, nrows))], axis=0)
    out_ref[pl.ds(tall, 2 * slots), pl.ds(0, nrows)] = notes.astype(jnp.float32).astype(out_ref.dtype)


def leading_pieces(rows, f_blocks, cols, counts):
    slots, nrows = cols.shape
    edge = f_blocks.shape[0] // nrows
    shape = (rows * edge + 2 * slots, PAIR * edge)
    f_blocks, cols, counts = (in_hbm(x) for x in (f_blocks, cols, counts))
    return pl.pallas_call(
        leading_kernel,
        grid=(1,),
        in_specs=[
            pl.BlockSpec((rows * edge, PAIR * edge), lambda g: (0, 0)),
            pl.BlockSpec(cols.shape, lambda g: (0, 0)),
            pl.BlockSpec(counts.shape, lambda g: (0, 0)),
        ],
        out_specs=pl.BlockSpec(shape, lambda g: (0, 0)),
        out_shape=jax.ShapeDtypeStruct(shape, f_blocks.dtype),
        cost_estimate=cost(0, 4 * rows * edge * PAIR * edge),
        compiler_params=params(8),
        name="leading_pieces",
    )(f_blocks, cols, counts)


def pack_kernel(edge, slots, notes, f_ref, out_ref, extra_ref, f_here, packed, sems):
    nrows = notes.shape[1]
    parts = slots // PAIR
    fetched = []
    for g in range(nrows // GROUP):
        here = piece(edge, g * GROUP, GROUP)
        fetched.append(pltpu.make_async_copy(f_ref.at[here], f_here.at[here], sems.at[g]))
        fetched[-1].start()
    wide = PAIR * edge

    def strip(r, p):
        return f_here[pl.ds(r * edge, edge), pl.ds(pl.multiple_of(p * wide, wide), wide)]

    def full_at(r, at):
        if r % GROUP == 0:
            fetched[r // GROUP].wait()
        packed[pl.ds(r * edge, edge), :] = strip(r, 0)
        for p in range(1, parts):
            packed[piece(edge, nrows + at + (p - 1)), :] = strip(r, p)

    def single_at(r, at, shares):
        @pl.when(shares)
        def _():
            value = strip(r, 1 + beyond(notes[slots, r])[0])
            here = piece(edge, nrows + at)
            moved = jnp.concatenate([value[:, edge:], value[:, :edge]], axis=1)
            low = lax.broadcasted_iota(jnp.int32, value.shape, 1) < edge
            packed[here, :] = jnp.where(low, packed[here, :], moved)

    walk([notes[slots, r] for r in range(nrows)], full_at, single_at, lambda *_: None)
    copies = [
        pltpu.make_async_copy(packed.at[pl.ds(nrows * edge, extra_ref.shape[0])], extra_ref, sems.at[0]),
        pltpu.make_async_copy(packed, out_ref, sems.at[1]),
    ]
    for copy in copies:
        copy.start()
    for copy in copies:
        copy.wait()


def packed_pieces(notes, slots, always, f_blocks):
    nrows = notes.shape[1]
    edge = f_blocks.shape[0] // nrows
    shape = (nrows * slots // PAIR * edge, PAIR * edge)
    return pl.pallas_call(
        functools.partial(pack_kernel, edge, slots),
        in_specs=[SMEM, ANY],
        out_specs=[ANY, ANY],
        scratch_shapes=[
            pltpu.VMEM(f_blocks.shape, f_blocks.dtype),
            pltpu.VMEM(shape, f_blocks.dtype),
            pltpu.SemaphoreType.DMA((nrows // GROUP,)),
        ],
        out_shape=[
            jax.ShapeDtypeStruct(shape, f_blocks.dtype),
            jax.ShapeDtypeStruct((always * edge, PAIR * edge), f_blocks.dtype),
        ],
        cost_estimate=cost(0, 4 * f_blocks.size),
        compiler_params=params(16),
        name="pack_live_pieces",
    )(notes, f_blocks)


def cut_kernel(ranges, slots, zero, notes, packed_ref, table, *refs):
    out_refs, sems = refs[: len(ranges)], refs[-1]
    copies = [
        pltpu.make_async_copy(packed_ref.at[pl.ds(low, high - low)], out_ref, sems.at[k])
        for k, ((low, high), out_ref) in enumerate(zip(ranges, out_refs))
    ]
    for copy in copies:
        copy.start()
    write_table(notes, slots, zero, table)
    for copy in copies:
        copy.wait()


def cut_pieces(ranges, notes, slots, zero, packed):
    edge = packed.shape[1] // PAIR
    rows = [(low * edge, high * edge) for low, high in ranges]
    return pl.pallas_call(
        functools.partial(cut_kernel, rows, slots, zero),
        in_specs=[SMEM, ANY],
        out_specs=[SMEM] + [ANY] * (2 * len(rows)),
        scratch_shapes=[pltpu.SemaphoreType.DMA((len(rows),))],
        out_shape=[table_shape(notes.shape[1], slots)]
        + [jax.ShapeDtypeStruct((high - low, packed.shape[1]), packed.dtype) for low, high in rows] * 2,
        cost_estimate=cost(0, 4 * sum(high - low for low, high in rows) * packed.shape[1]),
        compiler_params=params(2),
        name="cut_pieces",
    )(notes, packed)


def row_product(table, slots, edge, row, held, p_ref):
    others = slots // PAIR - 1
    left = [held[piece(edge, row), :]]
    left += [held[piece(edge, table[2 + p, row]), :] for p in range(others)]
    picked = [p_ref[piece(edge, table[2 + others + s, row]), :] for s in range(slots)]
    return jnp.dot(
        jnp.concatenate(left, axis=1), jnp.concatenate(picked, axis=0), preferred_element_type=jnp.float32
    )


def step_kernel(edge, slots, name, leading, places, table, *refs):
    size = None
    if name == "late":
        size, *refs = refs
    part_refs, refs = refs[: len(places)], refs[len(places) :]
    p_ref, *refs = refs
    total_ref = None
    if name != "first":
        total_ref, *refs = refs
    if name == "late":
        _, *refs = refs
    out_ref, held, p_here, stage, sems, out_sems, *refs = refs
    nrows = table.shape[1] - 1
    groups = nrows // GROUP

    depth = p_ref.shape[0]
    p_copy = pltpu.make_async_copy(p_ref, p_here.at[pl.ds(0, depth)], sems.at[0])
    p_copy.start()
    p_here[pl.ds(depth, edge), :] = jnp.zeros((edge, p_here.shape[1]), p_here.dtype)

    low, high = 0, groups
    if name != "first":
        room = [count for kind, _, count in places if kind == "second"][0]
        done = jnp.int32(0)
        for g in range(leading // GROUP):
            done = done + (table[0, (g + 1) * GROUP] <= room).astype(jnp.int32)
        low, high = (0, done) if name == "early" else (done, groups)

    copies = []
    for (kind, at, count), part in zip(places, part_refs):
        step = count
        if name == "late" and kind == "second":
            step = -(-count // 4)
        for first in range(0, count, step):
            needed = None
            if name == "late" and kind == "first":
                needed = low < leading // GROUP
            elif name == "late" and kind == "second":
                needed = table[1, low * GROUP] < first + step
            elif not isinstance(kind, str):
                needed = size[0] == kind
            tall = min(step, count - first) * edge
            source = part.at[pl.ds(first * edge, tall)]
            target = held.at[pl.ds((at + first) * edge, tall)]
            copies.append((needed, pltpu.make_async_copy(source, target, sems.at[1 + len(copies)])))

    def each(act):
        for needed, copy in copies:
            if needed is None:
                act(copy)
            else:
                pl.when(needed)(functools.partial(act, copy))

    each(lambda copy: copy.start())

    def total_copy(g):
        here = piece(edge, g * GROUP, GROUP)
        return pltpu.make_async_copy(total_ref.at[here], refs[0].at[here], refs[1].at[g])

    def out_copy(g):
        here = piece(edge, g * GROUP, GROUP)
        return pltpu.make_async_copy(stage.at[here], out_ref.at[here], out_sems.at[g])

    def over(act):
        def step(g, carry):
            act(g)
            return carry

        lax.fori_loop(low, high, step, 0)

    if name != "first":
        over(lambda g: total_copy(g).start())
    each(lambda copy: copy.wait())
    p_copy.wait()

    def group(g):
        if name != "first":
            total_copy(g).wait()
        for r in range(GROUP):
            row = g * GROUP + r
            here = piece(edge, row)
            value = row_product(table, slots, edge, row, held, p_here)
            if name != "first":
                value = refs[0][here, :] + value
            stage[here, :] = value.astype(stage.dtype)
        out_copy(g).start()

    over(group)
    over(lambda g: out_copy(g).wait())


def step_product(name, table, slots, leading, places, parts, p_tile, total=None, size=None, out=None):
    nrows = table.shape[1] - 1
    depth, width = p_tile.shape
    edge = parts[0].shape[1] // PAIR
    groups = nrows // GROUP
    room = max(at + rows for _, at, rows in places)
    dtype = jnp.float32 if name == "first" else jnp.bfloat16
    tall = nrows * edge
    later = name != "first"
    late = name == "late"
    return pl.pallas_call(
        functools.partial(step_kernel, edge, slots, name, leading, places),
        in_specs=[SMEM] * (1 + late) + [ANY] * len(parts) + [HBM] * (1 + later + late),
        out_specs=HBM,
        scratch_shapes=[
            pltpu.VMEM((room * edge, PAIR * edge), p_tile.dtype),
            pltpu.VMEM((depth + edge, width), p_tile.dtype),
            pltpu.VMEM((tall, width), dtype),
            pltpu.SemaphoreType.DMA((len(parts) + 8,)),
            pltpu.SemaphoreType.DMA((groups,)),
        ]
        + [pltpu.VMEM((tall, width), jnp.float32), pltpu.SemaphoreType.DMA((groups,))] * later,
        out_shape=pltpu.HBM((tall, width), dtype),
        input_output_aliases={4 + len(parts): 0} if late else {},
        cost_estimate=cost(tall * width * slots * edge, 4 * tall * width),
        compiler_params=params(16),
        name="step_" + name,
    )(
        table,
        *([size] if late else []),
        *parts,
        in_hbm(p_tile),
        *([in_hbm(total)] if later else []),
        *([in_hbm(out)] if late else []),
    )


def remainder(k, slots, leading, places, rests, unused, table, lead, extra, p_second, total):
    rest = [shifted(part, "col", -1) if k == n else other for n, (part, other) in enumerate(zip(rests, unused))]
    return step_product("early", table, slots, leading, places, (lead, extra), p_second, total), rest


def body(f_blocks, block_cols, block_counts, p_matrix):
    nrows, slots = block_cols.shape
    edge = f_blocks.shape[0] // nrows
    cols, counts = block_cols.T, block_counts.T
    groups = nrows // GROUP
    leading = (groups - groups // 4) * GROUP
    others = nrows * (slots // PAIR - 1)
    unit = others // 24
    always = 10 * unit
    ends = [always + k * unit for k in (1, 2, 3, 4, 5, 6, 8)] + [others]

    lead = shifted(leading_pieces(leading, f_blocks, cols, counts), "col", -1)
    notes = jnp.concatenate([cols, jnp.broadcast_to(counts, (slots, nrows))], axis=0)
    packed, extra = packed_pieces(notes, slots, always, f_blocks)
    extra = shifted(extra, "col", -1)
    p_second, packed = lax.optimization_barrier((p_matrix, packed))
    p_second = shifted(p_second, "row", -1)
    zero = p_matrix.shape[0] // edge
    ranges = [(nrows + always, nrows + end) for end in ends] + [(leading, nrows)]
    table, *rests = cut_pieces(ranges, notes, slots, zero, packed)
    rests, later, unused = rests[: len(ends)], rests[len(ends)], rests[len(ends) + 1 : -1]
    every = packed.shape[0] // edge
    total = step_product("first", table, slots, leading, [("all", 0, every)], (packed,), p_matrix)
    later, total, lead = lax.optimization_barrier((later, total, lead))
    later = shifted(later, "col", -1)

    notes_next = lead[leading * edge :, :nrows].astype(jnp.float32).astype(jnp.int32)
    most = read_notes(notes, notes_next, slots)
    notes_next, most = lax.optimization_barrier((notes_next, most))
    table_next = table_of(notes_next, slots, zero)
    other = most
    distance = 2
    while distance < lax.axis_size("col"):
        most = jnp.maximum(most, other)
        other = shifted(most, "col", -distance)
        distance *= 2
    size = pick_size(ends, most, other)
    early = [("first", 0, leading), ("second", nrows, always)]
    late = [early[0], ("later", leading, nrows - leading), early[1]]
    late += [(k, nrows + always, end - always) for k, end in enumerate(ends)]
    branches = [functools.partial(remainder, k, slots, leading, early) for k in range(len(ends))]
    out, rest = lax.switch(size[0], branches, rests, unused, table_next, lead, extra, p_second, total)
    parts = (lead, later, extra, *rest)
    return step_product("late", table_next, slots, leading, late, parts, p_second, total, size, out)


def solution(mesh):
    return jax.shard_map(
        body,
        mesh=mesh,
        in_specs=(P("row", "col"), P("row", "col"), P("row", "col"), P("row", "col")),
        out_specs=P("row", "col"),
        check_vma=False,
    )
```

```python
import functools

import jax
import jax.numpy as jnp
from jax import lax
from jax.experimental import pallas as pl
from jax.experimental.pallas import tpu as pltpu
from jax.sharding import PartitionSpec as P

GROUP = 4
PAIR = 2
SPLIT = 8
BATCH = 8

SMEM = pl.BlockSpec(memory_space=pltpu.SMEM)
ANY = pl.BlockSpec(memory_space=pl.ANY)
HBM = pl.BlockSpec(memory_space=pltpu.HBM)


def shifted(block, axis, distance):
    devices = range(lax.axis_size(axis))
    route = [((i - distance) % len(devices), i) for i in devices]
    return lax.ppermute(block, axis, route)


def in_hbm(x):
    return pltpu.with_memory_space_constraint(x, pltpu.HBM)


def params(mib):
    return pltpu.CompilerParams(vmem_limit_bytes=mib << 20)


def cost(flops, moved):
    return pl.CostEstimate(flops=flops, bytes_accessed=moved, transcendentals=0)


def piece(edge, index, count=1):
    return pl.ds(pl.multiple_of(index * edge, edge), count * edge)


def beyond(count):
    more = jnp.maximum(count - PAIR, 0)
    return more // PAIR, more % PAIR


def walk(counts, full_at, single_at, row_done):
    at, opened = jnp.int32(0), jnp.int32(-1)
    for r in range(len(counts)):
        full, single = beyond(counts[r])
        full_at(r, at)
        shares = jnp.logical_and(single == 1, opened >= 0)
        opens = jnp.logical_and(single == 1, opened < 0)
        single_at(r, jnp.where(shares, opened, at + full), shares)
        opened = jnp.where(opens, at + full, jnp.where(shares, -1, opened))
        at = at + full + opens.astype(jnp.int32)
        row_done(r, at, opened)


def write_table(notes, slots, zero, table):
    nrows = notes.shape[1]
    others = slots // PAIR - 1
    places = {}

    def full_at(r, at):
        table[0, r] = at
        places[r] = at

    def single_at(r, at, shares):
        count = notes[slots, r]
        full, single = beyond(count)
        table[2 + others, r] = notes[0, r]
        table[3 + others, r] = jnp.where(count > 1, notes[1, r], zero)
        for p in range(others):
            alone = jnp.logical_and(p == full, single == 1)
            table[2 + p, r] = jnp.where(p < full, nrows + places[r] + p, jnp.where(alone, nrows + at, r))
            even, odd = notes[PAIR * (p + 1), r], notes[PAIR * (p + 1) + 1, r]
            first = jnp.logical_or(p < full, jnp.logical_and(alone, jnp.logical_not(shares)))
            row = 2 + others + PAIR * (p + 1)
            table[row, r] = jnp.where(first, even, zero)
            table[row + 1, r] = jnp.where(p < full, odd, jnp.where(jnp.logical_and(alone, shares), even, zero))

    def row_done(r, at, opened):
        table[0, r + 1] = at
        table[1, r + 1] = jnp.where(opened < 0, at, opened)

    table[1, 0] = jnp.int32(0)
    walk([notes[slots, r] for r in range(nrows)], full_at, single_at, row_done)


def table_shape(nrows, slots):
    return jax.ShapeDtypeStruct((2 + slots // PAIR - 1 + slots, nrows + 1), jnp.int32)


def read_kernel(slots, notes, notes_next, most_ref):
    most = jnp.int32(0)
    for tile in (notes, notes_next):
        full, single = jnp.int32(0), jnp.int32(0)
        for r in range(tile.shape[1]):
            more, rest = beyond(tile[slots, r])
            full, single = full + more, single + rest
        most = jnp.maximum(most, full + (single + 1) // PAIR)
    most_ref[...] = jnp.full(most_ref.shape, most, jnp.int32)


def read_notes(notes, notes_next, slots):
    return pl.pallas_call(
        functools.partial(read_kernel, slots),
        in_specs=[SMEM, SMEM],
        out_specs=pl.BlockSpec(memory_space=pltpu.VMEM),
        out_shape=jax.ShapeDtypeStruct((8, 128), jnp.int32),
        cost_estimate=cost(20 << 30, 4096),
        compiler_params=params(2),
        name="read_notes",
    )(notes, notes_next)


def table_of(notes, slots, zero):
    return pl.pallas_call(
        lambda notes, table: write_table(notes, slots, zero, table),
        in_specs=[SMEM],
        out_specs=SMEM,
        out_shape=table_shape(notes.shape[1], slots),
        cost_estimate=cost(0, 4096),
        compiler_params=params(2),
        name="make_table",
    )(notes)


def pick_kernel(ends, one_ref, other_ref, size):
    most = jnp.max(jnp.maximum(one_ref[...], other_ref[...]))
    index = jnp.int32(0)
    for end in ends[:-1]:
        index = index + (most > end).astype(jnp.int32)
    size[0] = index


def pick_size(ends, one, other):
    vector = pl.BlockSpec(memory_space=pltpu.VMEM)
    return pl.pallas_call(
        functools.partial(pick_kernel, ends),
        in_specs=[vector, vector],
        out_specs=SMEM,
        out_shape=jax.ShapeDtypeStruct((1,), jnp.int32),
        cost_estimate=cost(0, 4096),
        compiler_params=params(2),
        name="pick_size",
    )(one, other)


def leading_kernel(f_ref, cols_ref, counts_ref, out_ref):
    slots, nrows = cols_ref.shape
    tall = f_ref.shape[0]
    out_ref[pl.ds(0, tall), :] = f_ref[...]
    notes = jnp.concatenate([cols_ref[...], jnp.broadcast_to(counts_ref[...], (slots, nrows))], axis=0)
    out_ref[pl.ds(tall, 2 * slots), pl.ds(0, nrows)] = notes.astype(jnp.float32).astype(out_ref.dtype)


def leading_pieces(rows, f_blocks, cols, counts):
    slots, nrows = cols.shape
    edge = f_blocks.shape[0] // nrows
    shape = (rows * edge + 2 * slots, PAIR * edge)
    f_blocks, cols, counts = (in_hbm(x) for x in (f_blocks, cols, counts))
    return pl.pallas_call(
        leading_kernel,
        grid=(1,),
        in_specs=[
            pl.BlockSpec((rows * edge, PAIR * edge), lambda g: (0, 0)),
            pl.BlockSpec(cols.shape, lambda g: (0, 0)),
            pl.BlockSpec(counts.shape, lambda g: (0, 0)),
        ],
        out_specs=pl.BlockSpec(shape, lambda g: (0, 0)),
        out_shape=jax.ShapeDtypeStruct(shape, f_blocks.dtype),
        cost_estimate=cost(0, 4 * rows * edge * PAIR * edge),
        compiler_params=params(8),
        name="leading_pieces",
    )(f_blocks, cols, counts)


def pack_kernel(edge, slots, notes, f_ref, out_ref, extra_ref, f_here, packed, sems):
    nrows = notes.shape[1]
    parts = slots // PAIR
    fetched = []
    for g in range(nrows // GROUP):
        here = piece(edge, g * GROUP, GROUP)
        fetched.append(pltpu.make_async_copy(f_ref.at[here], f_here.at[here], sems.at[g]))
        fetched[-1].start()
    wide = PAIR * edge

    def strip(r, p):
        return f_here[pl.ds(r * edge, edge), pl.ds(pl.multiple_of(p * wide, wide), wide)]

    def full_at(r, at):
        if r % GROUP == 0:
            fetched[r // GROUP].wait()
        packed[pl.ds(r * edge, edge), :] = strip(r, 0)
        for p in range(1, parts):
            packed[piece(edge, nrows + at + (p - 1)), :] = strip(r, p)

    def single_at(r, at, shares):
        @pl.when(shares)
        def _():
            value = strip(r, 1 + beyond(notes[slots, r])[0])
            here = piece(edge, nrows + at)
            moved = jnp.concatenate([value[:, edge:], value[:, :edge]], axis=1)
            low = lax.broadcasted_iota(jnp.int32, value.shape, 1) < edge
            packed[here, :] = jnp.where(low, packed[here, :], moved)

    walk([notes[slots, r] for r in range(nrows)], full_at, single_at, lambda *_: None)
    copies = [
        pltpu.make_async_copy(packed.at[pl.ds(nrows * edge, extra_ref.shape[0])], extra_ref, sems.at[0]),
        pltpu.make_async_copy(packed, out_ref, sems.at[1]),
    ]
    for copy in copies:
        copy.start()
    for copy in copies:
        copy.wait()


def packed_pieces(notes, slots, always, f_blocks):
    nrows = notes.shape[1]
    edge = f_blocks.shape[0] // nrows
    shape = (nrows * slots // PAIR * edge, PAIR * edge)
    return pl.pallas_call(
        functools.partial(pack_kernel, edge, slots),
        in_specs=[SMEM, ANY],
        out_specs=[ANY, ANY],
        scratch_shapes=[
            pltpu.VMEM(f_blocks.shape, f_blocks.dtype),
            pltpu.VMEM(shape, f_blocks.dtype),
            pltpu.SemaphoreType.DMA((nrows // GROUP,)),
        ],
        out_shape=[
            jax.ShapeDtypeStruct(shape, f_blocks.dtype),
            jax.ShapeDtypeStruct((always * edge, PAIR * edge), f_blocks.dtype),
        ],
        cost_estimate=cost(0, 4 * f_blocks.size),
        compiler_params=params(16),
        name="pack_live_pieces",
    )(notes, f_blocks)


def cut_kernel(ranges, slots, zero, notes, packed_ref, table, *refs):
    out_refs, sems = refs[: len(ranges)], refs[-1]
    copies = [
        pltpu.make_async_copy(packed_ref.at[pl.ds(low, high - low)], out_ref, sems.at[k])
        for k, ((low, high), out_ref) in enumerate(zip(ranges, out_refs))
    ]
    for copy in copies:
        copy.start()
    write_table(notes, slots, zero, table)
    for copy in copies:
        copy.wait()


def cut_pieces(ranges, notes, slots, zero, packed):
    edge = packed.shape[1] // PAIR
    rows = [(low * edge, high * edge) for low, high in ranges]
    return pl.pallas_call(
        functools.partial(cut_kernel, rows, slots, zero),
        in_specs=[SMEM, ANY],
        out_specs=[SMEM] + [ANY] * (2 * len(rows)),
        scratch_shapes=[pltpu.SemaphoreType.DMA((len(rows),))],
        out_shape=[table_shape(notes.shape[1], slots)]
        + [jax.ShapeDtypeStruct((high - low, packed.shape[1]), packed.dtype) for low, high in rows] * 2,
        cost_estimate=cost(0, 4 * sum(high - low for low, high in rows) * packed.shape[1]),
        compiler_params=params(2),
        name="cut_pieces",
    )(notes, packed)


def row_product(table, slots, edge, row, held, p_ref):
    others = slots // PAIR - 1
    left = [held[piece(edge, row), :]]
    left += [held[piece(edge, table[2 + p, row]), :] for p in range(others)]
    picked = [p_ref[piece(edge, table[2 + others + s, row]), :] for s in range(slots)]
    return jnp.dot(
        jnp.concatenate(left, axis=1), jnp.concatenate(picked, axis=0), preferred_element_type=jnp.float32
    )


def step_kernel(edge, slots, name, leading, places, table, *refs):
    size = None
    if name == "late":
        size, *refs = refs
    part_refs, refs = refs[: len(places)], refs[len(places) :]
    p_ref, *refs = refs
    total_ref = None
    if name != "first":
        total_ref, *refs = refs
    if name == "late":
        _, *refs = refs
    out_ref, held, p_here, stage, sems, out_sems, *refs = refs
    nrows = table.shape[1] - 1
    groups = nrows // GROUP

    depth = p_ref.shape[0]
    p_copies = []
    for k in range(SPLIT):
        here = pl.ds(k * (depth // SPLIT), depth // SPLIT)
        p_copies.append(pltpu.make_async_copy(p_ref.at[here], p_here.at[here], sems.at[k]))
        p_copies[-1].start()
    p_here[pl.ds(depth, edge), :] = jnp.zeros((edge, p_here.shape[1]), p_here.dtype)

    low, high = 0, groups
    if name != "first":
        room = [count for kind, _, count in places if kind == "second"][0]
        done = jnp.int32(0)
        for g in range(leading // GROUP):
            done = done + (table[0, (g + 1) * GROUP] <= room).astype(jnp.int32)
        low, high = (0, done) if name == "early" else (done, groups)

    copies = []
    for (kind, at, count), part in zip(places, part_refs):
        for first in range(0, count, BATCH):
            needed = None
            if name == "late" and kind == "first":
                needed = low < leading // GROUP
            elif name == "late" and kind == "second":
                needed = table[1, low * GROUP] < first + BATCH
            elif not isinstance(kind, str):
                needed = size[0] == kind
            tall = min(BATCH, count - first) * edge
            source = part.at[pl.ds(first * edge, tall)]
            target = held.at[pl.ds((at + first) * edge, tall)]
            copies.append((needed, pltpu.make_async_copy(source, target, sems.at[SPLIT + len(copies)])))

    def each(act):
        for needed, copy in copies:
            if needed is None:
                act(copy)
            else:
                pl.when(needed)(functools.partial(act, copy))

    each(lambda copy: copy.start())

    def total_copy(g):
        here = piece(edge, g * GROUP, GROUP)
        return pltpu.make_async_copy(total_ref.at[here], refs[0].at[here], refs[1].at[g])

    def out_copy(row):
        here = piece(edge, row)
        return pltpu.make_async_copy(stage.at[here], out_ref.at[here], out_sems.at[row])

    def over(act):
        def step(g, carry):
            act(g)
            return carry

        lax.fori_loop(low, high, step, 0)

    if name != "first":
        over(lambda g: total_copy(g).start())
    each(lambda copy: copy.wait())
    for copy in p_copies:
        copy.wait()

    def group(g):
        if name != "first":
            total_copy(g).wait()
        for r in range(GROUP):
            row = g * GROUP + r
            here = piece(edge, row)
            value = row_product(table, slots, edge, row, held, p_here)
            if name != "first":
                value = refs[0][here, :] + value
            stage[here, :] = value.astype(stage.dtype)
            out_copy(row).start()

    over(group)

    def settle(g):
        for r in range(GROUP):
            out_copy(g * GROUP + r).wait()

    over(settle)


def step_product(name, table, slots, leading, places, parts, p_tile, total=None, size=None, out=None):
    nrows = table.shape[1] - 1
    depth, width = p_tile.shape
    edge = parts[0].shape[1] // PAIR
    groups = nrows // GROUP
    room = max(at + rows for _, at, rows in places)
    dtype = jnp.float32 if name == "first" else jnp.bfloat16
    tall = nrows * edge
    later = name != "first"
    late = name == "late"
    return pl.pallas_call(
        functools.partial(step_kernel, edge, slots, name, leading, places),
        in_specs=[SMEM] * (1 + late) + [ANY] * len(parts) + [HBM] * (1 + later + late),
        out_specs=HBM,
        scratch_shapes=[
            pltpu.VMEM((room * edge, PAIR * edge), p_tile.dtype),
            pltpu.VMEM((depth + edge, width), p_tile.dtype),
            pltpu.VMEM((tall, width), dtype),
            pltpu.SemaphoreType.DMA((SPLIT + sum(-(-count // BATCH) for _, _, count in places),)),
            pltpu.SemaphoreType.DMA((nrows,)),
        ]
        + [pltpu.VMEM((tall, width), jnp.float32), pltpu.SemaphoreType.DMA((groups,))] * later,
        out_shape=pltpu.HBM((tall, width), dtype),
        input_output_aliases={4 + len(parts): 0} if late else {},
        cost_estimate=cost(tall * width * slots * edge, 4 * tall * width),
        compiler_params=params(16),
        name="step_" + name,
    )(
        table,
        *([size] if late else []),
        *parts,
        in_hbm(p_tile),
        *([in_hbm(total)] if later else []),
        *([in_hbm(out)] if late else []),
    )


def remainder(k, slots, leading, places, rests, unused, table, lead, extra, p_second, total):
    rest = [shifted(part, "col", -1) if k == n else other for n, (part, other) in enumerate(zip(rests, unused))]
    return step_product("early", table, slots, leading, places, (lead, extra), p_second, total), rest


def body(f_blocks, block_cols, block_counts, p_matrix):
    nrows, slots = block_cols.shape
    edge = f_blocks.shape[0] // nrows
    cols, counts = block_cols.T, block_counts.T
    groups = nrows // GROUP
    leading = (groups - groups // 4) * GROUP
    others = nrows * (slots // PAIR - 1)
    unit = others // 24
    always = 10 * unit
    ends = [always + k * unit for k in (1, 2, 3, 4, 5, 6, 8)] + [others]

    lead = shifted(leading_pieces(leading, f_blocks, cols, counts), "col", -1)
    notes = jnp.concatenate([cols, jnp.broadcast_to(counts, (slots, nrows))], axis=0)
    packed, extra = packed_pieces(notes, slots, always, f_blocks)
    extra = shifted(extra, "col", -1)
    p_second, packed = lax.optimization_barrier((p_matrix, packed))
    p_second = shifted(p_second, "row", -1)
    zero = p_matrix.shape[0] // edge
    ranges = [(nrows + always, nrows + end) for end in ends] + [(leading, nrows)]
    table, *rests = cut_pieces(ranges, notes, slots, zero, packed)
    rests, later, unused = rests[: len(ends)], rests[len(ends)], rests[len(ends) + 1 : -1]
    every = packed.shape[0] // edge
    total = step_product("first", table, slots, leading, [("all", 0, every)], (packed,), p_matrix)
    later, total, lead = lax.optimization_barrier((later, total, lead))
    later = shifted(later, "col", -1)

    notes_next = lead[leading * edge :, :nrows].astype(jnp.float32).astype(jnp.int32)
    most = read_notes(notes, notes_next, slots)
    notes_next, most = lax.optimization_barrier((notes_next, most))
    table_next = table_of(notes_next, slots, zero)
    other = most
    distance = 2
    while distance < lax.axis_size("col"):
        most = jnp.maximum(most, other)
        other = shifted(most, "col", -distance)
        distance *= 2
    size = pick_size(ends, most, other)
    early = [("first", 0, leading), ("second", nrows, always)]
    late = [early[0], ("later", leading, nrows - leading), early[1]]
    late += [(k, nrows + always, end - always) for k, end in enumerate(ends)]
    branches = [functools.partial(remainder, k, slots, leading, early) for k in range(len(ends))]
    out, rest = lax.switch(size[0], branches, rests, unused, table_next, lead, extra, p_second, total)
    parts = (lead, later, extra, *rest)
    return step_product("late", table_next, slots, leading, late, parts, p_second, total, size, out)


def solution(mesh):
    return jax.shard_map(
        body,
        mesh=mesh,
        in_specs=(P("row", "col"), P("row", "col"), P("row", "col"), P("row", "col")),
        out_specs=P("row", "col"),
        check_vma=False,
    )
```

```python
import functools

import jax
import jax.numpy as jnp
from jax import lax
from jax.experimental import pallas as pl
from jax.experimental.pallas import tpu as pltpu
from jax.sharding import PartitionSpec as P

GROUP = 4
PAIR = 2

SMEM = pl.BlockSpec(memory_space=pltpu.SMEM)
ANY = pl.BlockSpec(memory_space=pl.ANY)
HBM = pl.BlockSpec(memory_space=pltpu.HBM)


def shifted(block, axis, distance):
    devices = range(lax.axis_size(axis))
    route = [((i - distance) % len(devices), i) for i in devices]
    return lax.ppermute(block, axis, route)


def in_hbm(x):
    return pltpu.with_memory_space_constraint(x, pltpu.HBM)


def params(mib):
    return pltpu.CompilerParams(vmem_limit_bytes=mib << 20)


def cost(flops, moved):
    return pl.CostEstimate(flops=flops, bytes_accessed=moved, transcendentals=0)


def piece(edge, index, count=1):
    return pl.ds(pl.multiple_of(index * edge, edge), count * edge)


def beyond(count):
    more = jnp.maximum(count - PAIR, 0)
    return more // PAIR, more % PAIR


def walk(counts, full_at, single_at, row_done):
    at, opened = jnp.int32(0), jnp.int32(-1)
    for r in range(len(counts)):
        full, single = beyond(counts[r])
        full_at(r, at)
        shares = jnp.logical_and(single == 1, opened >= 0)
        opens = jnp.logical_and(single == 1, opened < 0)
        single_at(r, jnp.where(shares, opened, at + full), shares)
        opened = jnp.where(opens, at + full, jnp.where(shares, -1, opened))
        at = at + full + opens.astype(jnp.int32)
        row_done(r, at, opened)


def write_table(notes, slots, table):
    nrows = notes.shape[1]

    def full_at(r, at):
        table[0, r] = at

    def single_at(r, at, shares):
        table[1, r] = at * 2 + shares.astype(jnp.int32)

    def row_done(r, at, opened):
        table[0, r + 1] = at
        table[2, r + 1] = jnp.where(opened < 0, at, opened)

    table[2, 0] = jnp.int32(0)
    walk([notes[slots, r] for r in range(nrows)], full_at, single_at, row_done)


def table_shape(nrows):
    return jax.ShapeDtypeStruct((3, nrows + 1), jnp.int32)


def read_kernel(slots, notes, notes_next, table, most_ref):
    write_table(notes_next, slots, table)
    nrows = notes.shape[1]
    full, single = jnp.int32(0), jnp.int32(0)
    for r in range(nrows):
        more, rest = beyond(notes[slots, r])
        full, single = full + more, single + rest
    most = jnp.maximum(full + (single + 1) // PAIR, table[0, nrows])
    most_ref[...] = jnp.full(most_ref.shape, most, jnp.int32)


def read_notes(notes, notes_next, slots):
    return pl.pallas_call(
        functools.partial(read_kernel, slots),
        in_specs=[SMEM, SMEM],
        out_specs=[SMEM, pl.BlockSpec(memory_space=pltpu.VMEM)],
        out_shape=[table_shape(notes.shape[1]), jax.ShapeDtypeStruct((8, 128), jnp.int32)],
        cost_estimate=cost(20 << 30, 4096),
        compiler_params=params(2),
        name="read_notes",
    )(notes, notes_next)


def pick_kernel(ends, one_ref, other_ref, size):
    most = jnp.max(jnp.maximum(one_ref[...], other_ref[...]))
    index = jnp.int32(0)
    for end in ends[:-1]:
        index = index + (most > end).astype(jnp.int32)
    size[0] = index


def pick_size(ends, one, other):
    vector = pl.BlockSpec(memory_space=pltpu.VMEM)
    return pl.pallas_call(
        functools.partial(pick_kernel, ends),
        in_specs=[vector, vector],
        out_specs=SMEM,
        out_shape=jax.ShapeDtypeStruct((1,), jnp.int32),
        cost_estimate=cost(0, 4096),
        compiler_params=params(2),
        name="pick_size",
    )(one, other)


def leading_kernel(f_ref, cols_ref, counts_ref, out_ref):
    slots, nrows = cols_ref.shape
    tall = f_ref.shape[0]
    out_ref[pl.ds(0, tall), :] = f_ref[...]
    notes = jnp.concatenate([cols_ref[...], jnp.broadcast_to(counts_ref[...], (slots, nrows))], axis=0)
    out_ref[pl.ds(tall, 2 * slots), pl.ds(0, nrows)] = notes.astype(jnp.float32).astype(out_ref.dtype)


def leading_pieces(rows, f_blocks, cols, counts):
    slots, nrows = cols.shape
    edge = f_blocks.shape[0] // nrows
    shape = (rows * edge + 2 * slots, PAIR * edge)
    f_blocks, cols, counts = (in_hbm(x) for x in (f_blocks, cols, counts))
    return pl.pallas_call(
        leading_kernel,
        grid=(1,),
        in_specs=[
            pl.BlockSpec((rows * edge, PAIR * edge), lambda g: (0, 0)),
            pl.BlockSpec(cols.shape, lambda g: (0, 0)),
            pl.BlockSpec(counts.shape, lambda g: (0, 0)),
        ],
        out_specs=pl.BlockSpec(shape, lambda g: (0, 0)),
        out_shape=jax.ShapeDtypeStruct(shape, f_blocks.dtype),
        cost_estimate=cost(0, 4 * rows * edge * PAIR * edge),
        compiler_params=params(8),
        name="leading_pieces",
    )(f_blocks, cols, counts)


def pack_kernel(edge, slots, notes, f_ref, out_ref, extra_ref, table, f_here, packed, sems):
    nrows = notes.shape[1]
    parts = slots // PAIR
    fetched = []
    for g in range(nrows // GROUP):
        here = piece(edge, g * GROUP, GROUP)
        fetched.append(pltpu.make_async_copy(f_ref.at[here], f_here.at[here], sems.at[g]))
        fetched[-1].start()
    wide = PAIR * edge

    def strip(r, p):
        return f_here[pl.ds(r * edge, edge), pl.ds(pl.multiple_of(p * wide, wide), wide)]

    def full_at(r, at):
        if r % GROUP == 0:
            fetched[r // GROUP].wait()
        packed[pl.ds(r * edge, edge), :] = strip(r, 0)
        for p in range(1, parts):
            packed[piece(edge, nrows + at + (p - 1)), :] = strip(r, p)

    def single_at(r, at, shares):
        @pl.when(shares)
        def _():
            value = strip(r, 1 + beyond(notes[slots, r])[0])
            here = piece(edge, nrows + at)
            moved = jnp.concatenate([value[:, edge:], value[:, :edge]], axis=1)
            low = lax.broadcasted_iota(jnp.int32, value.shape, 1) < edge
            packed[here, :] = jnp.where(low, packed[here, :], moved)

    walk([notes[slots, r] for r in range(nrows)], full_at, single_at, lambda *_: None)
    copies = [
        pltpu.make_async_copy(packed.at[pl.ds(nrows * edge, extra_ref.shape[0])], extra_ref, sems.at[0]),
        pltpu.make_async_copy(packed, out_ref, sems.at[1]),
    ]
    for copy in copies:
        copy.start()
    write_table(notes, slots, table)
    for copy in copies:
        copy.wait()


def packed_pieces(notes, slots, always, f_blocks):
    nrows = notes.shape[1]
    edge = f_blocks.shape[0] // nrows
    shape = (nrows * slots // PAIR * edge, PAIR * edge)
    return pl.pallas_call(
        functools.partial(pack_kernel, edge, slots),
        in_specs=[SMEM, ANY],
        out_specs=[ANY, ANY, SMEM],
        scratch_shapes=[
            pltpu.VMEM(f_blocks.shape, f_blocks.dtype),
            pltpu.VMEM(shape, f_blocks.dtype),
            pltpu.SemaphoreType.DMA((nrows // GROUP,)),
        ],
        out_shape=[
            jax.ShapeDtypeStruct(shape, f_blocks.dtype),
            jax.ShapeDtypeStruct((always * edge, PAIR * edge), f_blocks.dtype),
            table_shape(nrows),
        ],
        cost_estimate=cost(0, 4 * f_blocks.size),
        compiler_params=params(16),
        name="pack_live_pieces",
    )(notes, f_blocks)


def cut_kernel(ranges, packed_ref, *refs):
    out_refs, sems = refs[: len(ranges)], refs[-1]
    copies = [
        pltpu.make_async_copy(packed_ref.at[pl.ds(low, high - low)], out_ref, sems.at[k])
        for k, ((low, high), out_ref) in enumerate(zip(ranges, out_refs))
    ]
    for copy in copies:
        copy.start()
    for copy in copies:
        copy.wait()


def cut_pieces(ranges, packed):
    edge = packed.shape[1] // PAIR
    rows = [(low * edge, high * edge) for low, high in ranges]
    return pl.pallas_call(
        functools.partial(cut_kernel, rows),
        in_specs=[ANY],
        out_specs=[ANY] * (2 * len(rows)),
        scratch_shapes=[pltpu.SemaphoreType.DMA((len(rows),))],
        out_shape=[jax.ShapeDtypeStruct((high - low, packed.shape[1]), packed.dtype) for low, high in rows] * 2,
        cost_estimate=cost(0, 4 * sum(high - low for low, high in rows) * packed.shape[1]),
        compiler_params=params(2),
        name="cut_pieces",
    )(packed)


def row_product(notes, table, slots, edge, row, held, p_ref):
    nrows = notes.shape[1]
    zero = p_ref.shape[0] // edge - 1
    count = notes[slots, row]
    full, single = beyond(count)
    code = table[1, row]
    second = code % 2
    left = [held[piece(edge, row), :]]
    picks = [notes[0, row], jnp.where(count > 1, notes[1, row], zero)]
    for p in range(slots // PAIR - 1):
        alone = jnp.logical_and(p == full, single == 1)
        at = jnp.where(p < full, nrows + table[0, row] + p, jnp.where(alone, nrows + code // 2, row))
        left.append(held[piece(edge, at), :])
        even, odd = notes[PAIR * (p + 1), row], notes[PAIR * (p + 1) + 1, row]
        picks.append(jnp.where(jnp.logical_or(p < full, jnp.logical_and(alone, second == 0)), even, zero))
        picks.append(jnp.where(p < full, odd, jnp.where(jnp.logical_and(alone, second == 1), even, zero)))
    picked = [p_ref[piece(edge, pick), :] for pick in picks]
    return jnp.dot(
        jnp.concatenate(left, axis=1), jnp.concatenate(picked, axis=0), preferred_element_type=jnp.float32
    )


def step_kernel(edge, slots, name, leading, places, notes, table, *refs):
    size = None
    if name == "late":
        size, *refs = refs
    part_refs, refs = refs[: len(places)], refs[len(places) :]
    p_ref, *refs = refs
    total_ref = None
    if name != "first":
        total_ref, *refs = refs
    if name == "late":
        _, *refs = refs
    out_ref, held, p_here, stage, sems, out_sems, *refs = refs
    nrows = notes.shape[1]
    groups = nrows // GROUP

    depth = p_ref.shape[0]
    p_copy = pltpu.make_async_copy(p_ref, p_here.at[pl.ds(0, depth)], sems.at[0])
    p_copy.start()
    p_here[pl.ds(depth, edge), :] = jnp.zeros((edge, p_here.shape[1]), p_here.dtype)

    low, high = 0, groups
    if name != "first":
        room = [count for kind, _, count in places if kind == "second"][0]
        done = jnp.int32(0)
        for g in range(leading // GROUP):
            done = done + (table[0, (g + 1) * GROUP] <= room).astype(jnp.int32)
        low, high = (0, done) if name == "early" else (done, groups)

    copies = []
    for (kind, at, count), part in zip(places, part_refs):
        step = count
        if name == "late" and kind == "second":
            step = -(-count // 4)
        for first in range(0, count, step):
            needed = None
            if name == "late" and kind == "first":
                needed = low < leading // GROUP
            elif name == "late" and kind == "second":
                needed = table[2, low * GROUP] < first + step
            elif not isinstance(kind, str):
                needed = size[0] == kind
            tall = min(step, count - first) * edge
            source = part.at[pl.ds(first * edge, tall)]
            target = held.at[pl.ds((at + first) * edge, tall)]
            copies.append((needed, pltpu.make_async_copy(source, target, sems.at[1 + len(copies)])))

    def each(act):
        for needed, copy in copies:
            if needed is None:
                act(copy)
            else:
                pl.when(needed)(functools.partial(act, copy))

    each(lambda copy: copy.start())

    def total_copy(g):
        here = piece(edge, g * GROUP, GROUP)
        return pltpu.make_async_copy(total_ref.at[here], refs[0].at[here], refs[1].at[g])

    def out_copy(g):
        here = piece(edge, g * GROUP, GROUP)
        return pltpu.make_async_copy(stage.at[here], out_ref.at[here], out_sems.at[g])

    def over(act):
        def step(g, carry):
            act(g)
            return carry

        lax.fori_loop(low, high, step, 0)

    each(lambda copy: copy.wait())
    p_copy.wait()
    if name != "first":
        over(lambda g: total_copy(g).start())

    def group(g):
        for r in range(GROUP):
            row = g * GROUP + r
            here = piece(edge, row)
            value = row_product(notes, table, slots, edge, row, held, p_here)
            if name != "first":
                if r == 0:
                    total_copy(g).wait()
                value = refs[0][here, :] + value
            stage[here, :] = value.astype(stage.dtype)
        out_copy(g).start()

    over(group)
    over(lambda g: out_copy(g).wait())


def step_product(name, notes, table, slots, leading, places, parts, p_tile, total=None, size=None, out=None):
    nrows = notes.shape[1]
    depth, width = p_tile.shape
    edge = parts[0].shape[1] // PAIR
    groups = nrows // GROUP
    room = max(at + rows for _, at, rows in places)
    dtype = jnp.float32 if name == "first" else jnp.bfloat16
    tall = nrows * edge
    later = name != "first"
    late = name == "late"
    return pl.pallas_call(
        functools.partial(step_kernel, edge, slots, name, leading, places),
        in_specs=[SMEM] * (2 + late) + [ANY] * len(parts) + [HBM] * (1 + later + late),
        out_specs=HBM,
        scratch_shapes=[
            pltpu.VMEM((room * edge, PAIR * edge), p_tile.dtype),
            pltpu.VMEM((depth + edge, width), p_tile.dtype),
            pltpu.VMEM((tall, width), dtype),
            pltpu.SemaphoreType.DMA((len(parts) + 8,)),
            pltpu.SemaphoreType.DMA((groups,)),
        ]
        + [pltpu.VMEM((tall, width), jnp.float32), pltpu.SemaphoreType.DMA((groups,))] * later,
        out_shape=pltpu.HBM((tall, width), dtype),
        input_output_aliases={5 + len(parts): 0} if late else {},
        cost_estimate=cost(tall * width * slots * edge, 4 * tall * width),
        compiler_params=params(16),
        name="step_" + name,
    )(
        notes,
        table,
        *([size] if late else []),
        *parts,
        in_hbm(p_tile),
        *([in_hbm(total)] if later else []),
        *([in_hbm(out)] if late else []),
    )


def remainder(k, slots, leading, places, rests, unused, notes, table, lead, extra, p_second, total):
    rest = [shifted(part, "col", -1) if k == n else other for n, (part, other) in enumerate(zip(rests, unused))]
    return step_product("early", notes, table, slots, leading, places, (lead, extra), p_second, total), rest


def body(f_blocks, block_cols, block_counts, p_matrix):
    nrows, slots = block_cols.shape
    edge = f_blocks.shape[0] // nrows
    cols, counts = block_cols.T, block_counts.T
    groups = nrows // GROUP
    leading = (groups - groups // 4) * GROUP
    others = nrows * (slots // PAIR - 1)
    unit = others // 24
    always = 10 * unit
    ends = [always + k * unit for k in (1, 2, 3, 4, 5, 6, 8)] + [others]

    lead = shifted(leading_pieces(leading, f_blocks, cols, counts), "col", -1)
    notes = jnp.concatenate([cols, jnp.broadcast_to(counts, (slots, nrows))], axis=0)
    packed, extra, table = packed_pieces(notes, slots, always, f_blocks)
    extra = shifted(extra, "col", -1)
    p_second, packed = lax.optimization_barrier((p_matrix, packed))
    p_second = shifted(p_second, "row", -1)
    rests = cut_pieces([(nrows + always, nrows + end) for end in ends] + [(leading, nrows)], packed)
    rests, later, unused = rests[: len(ends)], rests[len(ends)], rests[len(ends) + 1 : -1]
    every = packed.shape[0] // edge
    total = step_product("first", notes, table, slots, leading, [("all", 0, every)], (packed,), p_matrix)
    later, total, lead = lax.optimization_barrier((later, total, lead))
    later = shifted(later, "col", -1)

    notes_next = lead[leading * edge :, :nrows].astype(jnp.float32).astype(jnp.int32)
    table_next, most = read_notes(notes, notes_next, slots)
    other = most
    distance = 2
    while distance < lax.axis_size("col"):
        most = jnp.maximum(most, other)
        other = shifted(most, "col", -distance)
        distance *= 2
    size = pick_size(ends, most, other)
    early = [("first", 0, leading), ("second", nrows, always)]
    late = [early[0], ("later", leading, nrows - leading), early[1]]
    late += [(k, nrows + always, end - always) for k, end in enumerate(ends)]
    branches = [functools.partial(remainder, k, slots, leading, early) for k in range(len(ends))]
    out, rest = lax.switch(size[0], branches, rests, unused, notes_next, table_next, lead, extra, p_second, total)
    parts = (lead, later, extra, *rest)
    return step_product("late", notes_next, table_next, slots, leading, late, parts, p_second, total, size, out)


def solution(mesh):
    return jax.shard_map(
        body,
        mesh=mesh,
        in_specs=(P("row", "col"), P("row", "col"), P("row", "col"), P("row", "col")),
        out_specs=P("row", "col"),
        check_vma=False,
    )
```

```python
import functools

import jax
import jax.numpy as jnp
from jax import lax
from jax.experimental import pallas as pl
from jax.experimental.pallas import tpu as pltpu
from jax.sharding import PartitionSpec as P

GROUP = 4
PAIR = 2

SMEM = pl.BlockSpec(memory_space=pltpu.SMEM)
ANY = pl.BlockSpec(memory_space=pl.ANY)
HBM = pl.BlockSpec(memory_space=pltpu.HBM)


def shifted(block, axis, distance):
    devices = range(lax.axis_size(axis))
    route = [((i - distance) % len(devices), i) for i in devices]
    return lax.ppermute(block, axis, route)


def in_hbm(x):
    return pltpu.with_memory_space_constraint(x, pltpu.HBM)


def params(mib):
    return pltpu.CompilerParams(vmem_limit_bytes=mib << 20)


def cost(flops, moved):
    return pl.CostEstimate(flops=flops, bytes_accessed=moved, transcendentals=0)


def piece(edge, index, count=1):
    return pl.ds(pl.multiple_of(index * edge, edge), count * edge)


def beyond(count):
    more = jnp.maximum(count - PAIR, 0)
    return more // PAIR, more % PAIR


def walk(counts, full_at, single_at, row_done):
    at, opened = jnp.int32(0), jnp.int32(-1)
    for r in range(len(counts)):
        full, single = beyond(counts[r])
        full_at(r, at)
        shares = jnp.logical_and(single == 1, opened >= 0)
        opens = jnp.logical_and(single == 1, opened < 0)
        single_at(r, jnp.where(shares, opened, at + full), shares)
        opened = jnp.where(opens, at + full, jnp.where(shares, -1, opened))
        at = at + full + opens.astype(jnp.int32)
        row_done(r, at, opened)


def write_table(notes, slots, table):
    nrows = notes.shape[1]

    def full_at(r, at):
        table[0, r] = at

    def single_at(r, at, shares):
        table[1, r] = at * 2 + shares.astype(jnp.int32)

    def row_done(r, at, opened):
        table[0, r + 1] = at
        table[2, r + 1] = jnp.where(opened < 0, at, opened)

    table[2, 0] = jnp.int32(0)
    walk([notes[slots, r] for r in range(nrows)], full_at, single_at, row_done)


def table_shape(nrows):
    return jax.ShapeDtypeStruct((3, nrows + 1), jnp.int32)


def read_kernel(slots, notes, notes_next, table, most_ref):
    write_table(notes_next, slots, table)
    nrows = notes.shape[1]
    full, single = jnp.int32(0), jnp.int32(0)
    for r in range(nrows):
        more, rest = beyond(notes[slots, r])
        full, single = full + more, single + rest
    most = jnp.maximum(full + (single + 1) // PAIR, table[0, nrows])
    most_ref[...] = jnp.full(most_ref.shape, most, jnp.int32)


def read_notes(notes, notes_next, slots):
    return pl.pallas_call(
        functools.partial(read_kernel, slots),
        in_specs=[SMEM, SMEM],
        out_specs=[SMEM, pl.BlockSpec(memory_space=pltpu.VMEM)],
        out_shape=[table_shape(notes.shape[1]), jax.ShapeDtypeStruct((8, 128), jnp.int32)],
        cost_estimate=cost(20 << 30, 4096),
        compiler_params=params(2),
        name="read_notes",
    )(notes, notes_next)


def pick_kernel(ends, one_ref, other_ref, size):
    most = jnp.max(jnp.maximum(one_ref[...], other_ref[...]))
    index = jnp.int32(0)
    for end in ends[:-1]:
        index = index + (most > end).astype(jnp.int32)
    size[0] = index


def pick_size(ends, one, other):
    vector = pl.BlockSpec(memory_space=pltpu.VMEM)
    return pl.pallas_call(
        functools.partial(pick_kernel, ends),
        in_specs=[vector, vector],
        out_specs=SMEM,
        out_shape=jax.ShapeDtypeStruct((1,), jnp.int32),
        cost_estimate=cost(0, 4096),
        compiler_params=params(2),
        name="pick_size",
    )(one, other)


def leading_kernel(f_ref, cols_ref, counts_ref, out_ref):
    slots, nrows = cols_ref.shape
    tall = f_ref.shape[0]
    out_ref[pl.ds(0, tall), :] = f_ref[...]
    notes = jnp.concatenate([cols_ref[...], jnp.broadcast_to(counts_ref[...], (slots, nrows))], axis=0)
    out_ref[pl.ds(tall, 2 * slots), pl.ds(0, nrows)] = notes.astype(jnp.float32).astype(out_ref.dtype)


def leading_pieces(rows, f_blocks, cols, counts):
    slots, nrows = cols.shape
    edge = f_blocks.shape[0] // nrows
    shape = (rows * edge + 2 * slots, PAIR * edge)
    f_blocks, cols, counts = (in_hbm(x) for x in (f_blocks, cols, counts))
    return pl.pallas_call(
        leading_kernel,
        grid=(1,),
        in_specs=[
            pl.BlockSpec((rows * edge, PAIR * edge), lambda g: (0, 0)),
            pl.BlockSpec(cols.shape, lambda g: (0, 0)),
            pl.BlockSpec(counts.shape, lambda g: (0, 0)),
        ],
        out_specs=pl.BlockSpec(shape, lambda g: (0, 0)),
        out_shape=jax.ShapeDtypeStruct(shape, f_blocks.dtype),
        cost_estimate=cost(0, 4 * rows * edge * PAIR * edge),
        compiler_params=params(8),
        name="leading_pieces",
    )(f_blocks, cols, counts)


def pack_kernel(edge, slots, notes, f_ref, out_ref, extra_ref, table, f_here, packed, sems):
    nrows = notes.shape[1]
    parts = slots // PAIR
    fetched = []
    for g in range(nrows // GROUP):
        here = piece(edge, g * GROUP, GROUP)
        fetched.append(pltpu.make_async_copy(f_ref.at[here], f_here.at[here], sems.at[g]))
        fetched[-1].start()
    wide = PAIR * edge

    def strip(r, p):
        return f_here[pl.ds(r * edge, edge), pl.ds(pl.multiple_of(p * wide, wide), wide)]

    def full_at(r, at):
        if r % GROUP == 0:
            fetched[r // GROUP].wait()
        packed[pl.ds(r * edge, edge), :] = strip(r, 0)
        for p in range(1, parts):
            packed[piece(edge, nrows + at + (p - 1)), :] = strip(r, p)

    def single_at(r, at, shares):
        @pl.when(shares)
        def _():
            value = strip(r, 1 + beyond(notes[slots, r])[0])
            here = piece(edge, nrows + at)
            moved = jnp.concatenate([value[:, edge:], value[:, :edge]], axis=1)
            low = lax.broadcasted_iota(jnp.int32, value.shape, 1) < edge
            packed[here, :] = jnp.where(low, packed[here, :], moved)

    walk([notes[slots, r] for r in range(nrows)], full_at, single_at, lambda *_: None)
    copies = [
        pltpu.make_async_copy(packed.at[pl.ds(nrows * edge, extra_ref.shape[0])], extra_ref, sems.at[0]),
        pltpu.make_async_copy(packed, out_ref, sems.at[1]),
    ]
    for copy in copies:
        copy.start()
    write_table(notes, slots, table)
    for copy in copies:
        copy.wait()


def packed_pieces(notes, slots, always, f_blocks):
    nrows = notes.shape[1]
    edge = f_blocks.shape[0] // nrows
    shape = (nrows * slots // PAIR * edge, PAIR * edge)
    return pl.pallas_call(
        functools.partial(pack_kernel, edge, slots),
        in_specs=[SMEM, ANY],
        out_specs=[ANY, ANY, SMEM],
        scratch_shapes=[
            pltpu.VMEM(f_blocks.shape, f_blocks.dtype),
            pltpu.VMEM(shape, f_blocks.dtype),
            pltpu.SemaphoreType.DMA((nrows // GROUP,)),
        ],
        out_shape=[
            jax.ShapeDtypeStruct(shape, f_blocks.dtype),
            jax.ShapeDtypeStruct((always * edge, PAIR * edge), f_blocks.dtype),
            table_shape(nrows),
        ],
        cost_estimate=cost(0, 4 * f_blocks.size),
        compiler_params=params(16),
        name="pack_live_pieces",
    )(notes, f_blocks)


def cut_kernel(ranges, packed_ref, *refs):
    out_refs, sems = refs[: len(ranges)], refs[-1]
    copies = [
        pltpu.make_async_copy(packed_ref.at[pl.ds(low, high - low)], out_ref, sems.at[k])
        for k, ((low, high), out_ref) in enumerate(zip(ranges, out_refs))
    ]
    for copy in copies:
        copy.start()
    for copy in copies:
        copy.wait()


def cut_pieces(ranges, packed):
    edge = packed.shape[1] // PAIR
    rows = [(low * edge, high * edge) for low, high in ranges]
    return pl.pallas_call(
        functools.partial(cut_kernel, rows),
        in_specs=[ANY],
        out_specs=[ANY] * (2 * len(rows)),
        scratch_shapes=[pltpu.SemaphoreType.DMA((len(rows),))],
        out_shape=[jax.ShapeDtypeStruct((high - low, packed.shape[1]), packed.dtype) for low, high in rows] * 2,
        cost_estimate=cost(0, 4 * sum(high - low for low, high in rows) * packed.shape[1]),
        compiler_params=params(2),
        name="cut_pieces",
    )(packed)


def row_product(notes, table, slots, edge, row, held, p_ref):
    nrows = notes.shape[1]
    zero = p_ref.shape[0] // edge - 1
    count = notes[slots, row]
    full, single = beyond(count)
    code = table[1, row]
    second = code % 2
    left = [held[piece(edge, row), :]]
    picks = [notes[0, row], jnp.where(count > 1, notes[1, row], zero)]
    for p in range(slots // PAIR - 1):
        alone = jnp.logical_and(p == full, single == 1)
        at = jnp.where(p < full, nrows + table[0, row] + p, jnp.where(alone, nrows + code // 2, row))
        left.append(held[piece(edge, at), :])
        even, odd = notes[PAIR * (p + 1), row], notes[PAIR * (p + 1) + 1, row]
        picks.append(jnp.where(jnp.logical_or(p < full, jnp.logical_and(alone, second == 0)), even, zero))
        picks.append(jnp.where(p < full, odd, jnp.where(jnp.logical_and(alone, second == 1), even, zero)))
    picked = [p_ref[piece(edge, pick), :] for pick in picks]
    return jnp.dot(
        jnp.concatenate(left, axis=1), jnp.concatenate(picked, axis=0), preferred_element_type=jnp.float32
    )


def step_kernel(edge, slots, name, leading, places, notes, table, *refs):
    size = None
    if name == "late":
        size, *refs = refs
    part_refs, refs = refs[: len(places)], refs[len(places) :]
    p_ref, *refs = refs
    total_ref = None
    if name != "first":
        total_ref, *refs = refs
    if name == "late":
        _, *refs = refs
    out_ref, held, p_here, stage, sems, out_sems, *refs = refs
    nrows = notes.shape[1]
    groups = nrows // GROUP

    depth = p_ref.shape[0]
    p_copy = pltpu.make_async_copy(p_ref, p_here.at[pl.ds(0, depth)], sems.at[0])
    p_copy.start()
    p_here[pl.ds(depth, edge), :] = jnp.zeros((edge, p_here.shape[1]), p_here.dtype)

    low, high = 0, groups
    if name != "first":
        room = [count for kind, _, count in places if kind == "second"][0]
        done = jnp.int32(0)
        for g in range(leading // GROUP):
            done = done + (table[0, (g + 1) * GROUP] <= room).astype(jnp.int32)
        low, high = (0, done) if name == "early" else (done, groups)

    copies = []
    for (kind, at, count), part in zip(places, part_refs):
        step = count
        if name == "late" and kind == "second":
            step = -(-count // 4)
        for first in range(0, count, step):
            needed = None
            if name == "late" and kind == "first":
                needed = low < leading // GROUP
            elif name == "late" and kind == "second":
                needed = table[2, low * GROUP] < first + step
            elif not isinstance(kind, str):
                needed = size[0] == kind
            tall = min(step, count - first) * edge
            source = part.at[pl.ds(first * edge, tall)]
            target = held.at[pl.ds((at + first) * edge, tall)]
            copies.append((needed, pltpu.make_async_copy(source, target, sems.at[1 + len(copies)])))

    def each(act):
        for needed, copy in copies:
            if needed is None:
                act(copy)
            else:
                pl.when(needed)(functools.partial(act, copy))

    each(lambda copy: copy.start())

    def total_copy(g):
        here = piece(edge, g * GROUP, GROUP)
        return pltpu.make_async_copy(total_ref.at[here], refs[0].at[here], refs[1].at[g])

    def out_copy(g):
        here = piece(edge, g * GROUP, GROUP)
        return pltpu.make_async_copy(stage.at[here], out_ref.at[here], out_sems.at[g])

    def over(act):
        def step(g, carry):
            act(g)
            return carry

        lax.fori_loop(low, high, step, 0)

    if name != "first":
        over(lambda g: total_copy(g).start())
    each(lambda copy: copy.wait())
    p_copy.wait()

    def group(g):
        if name != "first":
            total_copy(g).wait()
        for r in range(GROUP):
            row = g * GROUP + r
            here = piece(edge, row)
            value = row_product(notes, table, slots, edge, row, held, p_here)
            if name != "first":
                value = refs[0][here, :] + value
            stage[here, :] = value.astype(stage.dtype)
        out_copy(g).start()

    over(group)
    over(lambda g: out_copy(g).wait())


def step_product(name, notes, table, slots, leading, places, parts, p_tile, total=None, size=None, out=None):
    nrows = notes.shape[1]
    depth, width = p_tile.shape
    edge = parts[0].shape[1] // PAIR
    groups = nrows // GROUP
    room = max(at + rows for _, at, rows in places)
    dtype = jnp.float32 if name == "first" else jnp.bfloat16
    tall = nrows * edge
    later = name != "first"
    late = name == "late"
    return pl.pallas_call(
        functools.partial(step_kernel, edge, slots, name, leading, places),
        in_specs=[SMEM] * (2 + late) + [ANY] * (len(parts) + 1 + later) + [HBM] * late,
        out_specs=HBM if later else ANY,
        scratch_shapes=[
            pltpu.VMEM((room * edge, PAIR * edge), p_tile.dtype),
            pltpu.VMEM((depth + edge, width), p_tile.dtype),
            pltpu.VMEM((tall, width), dtype),
            pltpu.SemaphoreType.DMA((len(parts) + 8,)),
            pltpu.SemaphoreType.DMA((groups,)),
        ]
        + [pltpu.VMEM((tall, width), jnp.float32), pltpu.SemaphoreType.DMA((groups,))] * later,
        out_shape=(pltpu.HBM if later else jax.ShapeDtypeStruct)((tall, width), dtype),
        input_output_aliases={5 + len(parts): 0} if late else {},
        cost_estimate=cost(tall * width * slots * edge, 4 * tall * width),
        compiler_params=params(16),
        name="step_" + name,
    )(
        notes,
        table,
        *([size] if late else []),
        *parts,
        p_tile,
        *([total] if later else []),
        *([in_hbm(out)] if late else []),
    )


def remainder(k, slots, leading, places, rests, unused, notes, table, lead, extra, p_second, total):
    rest = [shifted(part, "col", -1) if k == n else other for n, (part, other) in enumerate(zip(rests, unused))]
    return step_product("early", notes, table, slots, leading, places, (lead, extra), p_second, total), rest


def body(f_blocks, block_cols, block_counts, p_matrix):
    nrows, slots = block_cols.shape
    edge = f_blocks.shape[0] // nrows
    cols, counts = block_cols.T, block_counts.T
    groups = nrows // GROUP
    leading = (groups - groups // 4) * GROUP
    others = nrows * (slots // PAIR - 1)
    unit = others // 24
    always = 9 * unit
    ends = [always + k * unit for k in (1, 2, 3, 4, 5, 6, 8)] + [others]

    lead = shifted(leading_pieces(leading, f_blocks, cols, counts), "col", -1)
    notes = jnp.concatenate([cols, jnp.broadcast_to(counts, (slots, nrows))], axis=0)
    packed, extra, table = packed_pieces(notes, slots, always, f_blocks)
    p_second, packed = lax.optimization_barrier((p_matrix, packed))
    p_second = shifted(p_second, "row", -1)
    rests = cut_pieces([(nrows + always, nrows + end) for end in ends] + [(leading, nrows)], packed)
    rests, later, unused = rests[: len(ends)], rests[len(ends)], rests[len(ends) + 1 : -1]
    extra, *rests = lax.optimization_barrier((extra, *rests))
    extra = shifted(extra, "col", -1)
    every = packed.shape[0] // edge
    total = step_product("first", notes, table, slots, leading, [("all", 0, every)], (packed,), p_matrix)
    later, total, lead = lax.optimization_barrier((later, total, lead))
    later = shifted(later, "col", -1)

    notes_next = lead[leading * edge :, :nrows].astype(jnp.float32).astype(jnp.int32)
    table_next, most = read_notes(notes, notes_next, slots)
    other = most
    distance = 2
    while distance < lax.axis_size("col"):
        most = jnp.maximum(most, other)
        other = shifted(most, "col", -distance)
        distance *= 2
    size = pick_size(ends, most, other)
    early = [("first", 0, leading), ("second", nrows, always)]
    late = [early[0], ("later", leading, nrows - leading), early[1]]
    late += [(k, nrows + always, end - always) for k, end in enumerate(ends)]
    branches = [functools.partial(remainder, k, slots, leading, early) for k in range(len(ends))]
    out, rest = lax.switch(size[0], branches, rests, unused, notes_next, table_next, lead, extra, p_second, total)
    parts = (lead, later, extra, *rest)
    return step_product("late", notes_next, table_next, slots, leading, late, parts, p_second, total, size, out)


def solution(mesh):
    return jax.shard_map(
        body,
        mesh=mesh,
        in_specs=(P("row", "col"), P("row", "col"), P("row", "col"), P("row", "col")),
        out_specs=P("row", "col"),
        check_vma=False,
    )
```

```python
import functools

import jax
import jax.numpy as jnp
from jax import lax
from jax.experimental import pallas as pl
from jax.experimental.pallas import tpu as pltpu
from jax.sharding import PartitionSpec as P

GROUP = 4
PAIR = 2

SMEM = pl.BlockSpec(memory_space=pltpu.SMEM)
ANY = pl.BlockSpec(memory_space=pl.ANY)
HBM = pl.BlockSpec(memory_space=pltpu.HBM)


def shifted(block, axis, distance):
    devices = range(lax.axis_size(axis))
    route = [((i - distance) % len(devices), i) for i in devices]
    return lax.ppermute(block, axis, route)


def in_hbm(x):
    return pltpu.with_memory_space_constraint(x, pltpu.HBM)


def params(mib):
    return pltpu.CompilerParams(vmem_limit_bytes=mib << 20)


def cost(flops, moved):
    return pl.CostEstimate(flops=flops, bytes_accessed=moved, transcendentals=0)


def piece(edge, index, count=1):
    return pl.ds(pl.multiple_of(index * edge, edge), count * edge)


def beyond(count):
    more = jnp.maximum(count - PAIR, 0)
    return more // PAIR, more % PAIR


def walk(counts, full_at, single_at, row_done):
    at, opened = jnp.int32(0), jnp.int32(-1)
    for r in range(len(counts)):
        full, single = beyond(counts[r])
        full_at(r, at)
        shares = jnp.logical_and(single == 1, opened >= 0)
        opens = jnp.logical_and(single == 1, opened < 0)
        single_at(r, jnp.where(shares, opened, at + full), shares)
        opened = jnp.where(opens, at + full, jnp.where(shares, -1, opened))
        at = at + full + opens.astype(jnp.int32)
        row_done(r, at, opened)


def write_table(notes, slots, table):
    nrows = notes.shape[1]

    def full_at(r, at):
        table[0, r] = at

    def single_at(r, at, shares):
        table[1, r] = at * 2 + shares.astype(jnp.int32)

    def row_done(r, at, opened):
        table[0, r + 1] = at
        table[2, r + 1] = jnp.where(opened < 0, at, opened)

    table[2, 0] = jnp.int32(0)
    walk([notes[slots, r] for r in range(nrows)], full_at, single_at, row_done)


def table_shape(nrows):
    return jax.ShapeDtypeStruct((3, nrows + 1), jnp.int32)


def read_kernel(slots, notes, notes_next, table, most_ref):
    write_table(notes_next, slots, table)
    nrows = notes.shape[1]
    full, single = jnp.int32(0), jnp.int32(0)
    for r in range(nrows):
        more, rest = beyond(notes[slots, r])
        full, single = full + more, single + rest
    most = jnp.maximum(full + (single + 1) // PAIR, table[0, nrows])
    most_ref[...] = jnp.full(most_ref.shape, most, jnp.int32)


def read_notes(notes, notes_next, slots):
    return pl.pallas_call(
        functools.partial(read_kernel, slots),
        in_specs=[SMEM, SMEM],
        out_specs=[SMEM, pl.BlockSpec(memory_space=pltpu.VMEM)],
        out_shape=[table_shape(notes.shape[1]), jax.ShapeDtypeStruct((8, 128), jnp.int32)],
        cost_estimate=cost(20 << 30, 4096),
        compiler_params=params(2),
        name="read_notes",
    )(notes, notes_next)


def pick_kernel(ends, one_ref, other_ref, size):
    most = jnp.max(jnp.maximum(one_ref[...], other_ref[...]))
    index = jnp.int32(0)
    for end in ends[:-1]:
        index = index + (most > end).astype(jnp.int32)
    size[0] = index


def pick_size(ends, one, other):
    vector = pl.BlockSpec(memory_space=pltpu.VMEM)
    return pl.pallas_call(
        functools.partial(pick_kernel, ends),
        in_specs=[vector, vector],
        out_specs=SMEM,
        out_shape=jax.ShapeDtypeStruct((1,), jnp.int32),
        cost_estimate=cost(0, 4096),
        compiler_params=params(2),
        name="pick_size",
    )(one, other)


def leading_kernel(f_ref, cols_ref, counts_ref, out_ref):
    slots, nrows = cols_ref.shape
    tall = f_ref.shape[0]
    out_ref[pl.ds(0, tall), :] = f_ref[...]
    notes = jnp.concatenate([cols_ref[...], jnp.broadcast_to(counts_ref[...], (slots, nrows))], axis=0)
    out_ref[pl.ds(tall, 2 * slots), pl.ds(0, nrows)] = notes.astype(jnp.float32).astype(out_ref.dtype)


def leading_pieces(rows, f_blocks, cols, counts):
    slots, nrows = cols.shape
    edge = f_blocks.shape[0] // nrows
    shape = (rows * edge + 2 * slots, PAIR * edge)
    f_blocks, cols, counts = (in_hbm(x) for x in (f_blocks, cols, counts))
    return pl.pallas_call(
        leading_kernel,
        grid=(1,),
        in_specs=[
            pl.BlockSpec((rows * edge, PAIR * edge), lambda g: (0, 0)),
            pl.BlockSpec(cols.shape, lambda g: (0, 0)),
            pl.BlockSpec(counts.shape, lambda g: (0, 0)),
        ],
        out_specs=pl.BlockSpec(shape, lambda g: (0, 0)),
        out_shape=jax.ShapeDtypeStruct(shape, f_blocks.dtype),
        cost_estimate=cost(0, 4 * rows * edge * PAIR * edge),
        compiler_params=params(8),
        name="leading_pieces",
    )(f_blocks, cols, counts)


def pack_kernel(edge, slots, notes, f_ref, out_ref, extra_ref, table, f_here, packed, sems):
    nrows = notes.shape[1]
    parts = slots // PAIR
    fetched = []
    for g in range(nrows // GROUP):
        here = piece(edge, g * GROUP, GROUP)
        fetched.append(pltpu.make_async_copy(f_ref.at[here], f_here.at[here], sems.at[g]))
        fetched[-1].start()
    wide = PAIR * edge

    def strip(r, p):
        return f_here[pl.ds(r * edge, edge), pl.ds(pl.multiple_of(p * wide, wide), wide)]

    def full_at(r, at):
        if r % GROUP == 0:
            fetched[r // GROUP].wait()
        packed[pl.ds(r * edge, edge), :] = strip(r, 0)
        for p in range(1, parts):
            packed[piece(edge, nrows + at + (p - 1)), :] = strip(r, p)

    def single_at(r, at, shares):
        @pl.when(shares)
        def _():
            value = strip(r, 1 + beyond(notes[slots, r])[0])
            here = piece(edge, nrows + at)
            moved = jnp.concatenate([value[:, edge:], value[:, :edge]], axis=1)
            low = lax.broadcasted_iota(jnp.int32, value.shape, 1) < edge
            packed[here, :] = jnp.where(low, packed[here, :], moved)

    walk([notes[slots, r] for r in range(nrows)], full_at, single_at, lambda *_: None)
    copies = [
        pltpu.make_async_copy(packed.at[pl.ds(nrows * edge, extra_ref.shape[0])], extra_ref, sems.at[0]),
        pltpu.make_async_copy(packed, out_ref, sems.at[1]),
    ]
    for copy in copies:
        copy.start()
    write_table(notes, slots, table)
    for copy in copies:
        copy.wait()


def packed_pieces(notes, slots, always, f_blocks):
    nrows = notes.shape[1]
    edge = f_blocks.shape[0] // nrows
    shape = (nrows * slots // PAIR * edge, PAIR * edge)
    return pl.pallas_call(
        functools.partial(pack_kernel, edge, slots),
        in_specs=[SMEM, ANY],
        out_specs=[ANY, ANY, SMEM],
        scratch_shapes=[
            pltpu.VMEM(f_blocks.shape, f_blocks.dtype),
            pltpu.VMEM(shape, f_blocks.dtype),
            pltpu.SemaphoreType.DMA((nrows // GROUP,)),
        ],
        out_shape=[
            jax.ShapeDtypeStruct(shape, f_blocks.dtype),
            jax.ShapeDtypeStruct((always * edge, PAIR * edge), f_blocks.dtype),
            table_shape(nrows),
        ],
        cost_estimate=cost(0, 4 * f_blocks.size),
        compiler_params=params(16),
        name="pack_live_pieces",
    )(notes, f_blocks)


def cut_kernel(ranges, packed_ref, *refs):
    out_refs, sems = refs[: len(ranges)], refs[-1]
    copies = [
        pltpu.make_async_copy(packed_ref.at[pl.ds(low, high - low)], out_ref, sems.at[k])
        for k, ((low, high), out_ref) in enumerate(zip(ranges, out_refs))
    ]
    for copy in copies:
        copy.start()
    for copy in copies:
        copy.wait()


def cut_pieces(ranges, packed):
    edge = packed.shape[1] // PAIR
    rows = [(low * edge, high * edge) for low, high in ranges]
    return pl.pallas_call(
        functools.partial(cut_kernel, rows),
        in_specs=[ANY],
        out_specs=[ANY] * (2 * len(rows)),
        scratch_shapes=[pltpu.SemaphoreType.DMA((len(rows),))],
        out_shape=[jax.ShapeDtypeStruct((high - low, packed.shape[1]), packed.dtype) for low, high in rows] * 2,
        cost_estimate=cost(0, 4 * sum(high - low for low, high in rows) * packed.shape[1]),
        compiler_params=params(2),
        name="cut_pieces",
    )(packed)


def row_product(notes, table, slots, edge, row, held, p_ref):
    nrows = notes.shape[1]
    zero = p_ref.shape[0] // edge - 1
    count = notes[slots, row]
    full, single = beyond(count)
    code = table[1, row]
    second = code % 2
    left = [held[piece(edge, row), :]]
    picks = [notes[0, row], jnp.where(count > 1, notes[1, row], zero)]
    for p in range(slots // PAIR - 1):
        alone = jnp.logical_and(p == full, single == 1)
        at = jnp.where(p < full, nrows + table[0, row] + p, jnp.where(alone, nrows + code // 2, row))
        left.append(held[piece(edge, at), :])
        even, odd = notes[PAIR * (p + 1), row], notes[PAIR * (p + 1) + 1, row]
        picks.append(jnp.where(jnp.logical_or(p < full, jnp.logical_and(alone, second == 0)), even, zero))
        picks.append(jnp.where(p < full, odd, jnp.where(jnp.logical_and(alone, second == 1), even, zero)))
    picked = [p_ref[piece(edge, pick), :] for pick in picks]
    return jnp.dot(
        jnp.concatenate(left, axis=1), jnp.concatenate(picked, axis=0), preferred_element_type=jnp.float32
    )


def step_kernel(edge, slots, name, leading, places, notes, table, *refs):
    size = None
    if name == "late":
        size, *refs = refs
    part_refs, refs = refs[: len(places)], refs[len(places) :]
    p_ref, *refs = refs
    total_ref = None
    if name != "first":
        total_ref, *refs = refs
    if name == "late":
        _, *refs = refs
    out_ref, held, p_here, stage, sems, out_sems, *refs = refs
    nrows = notes.shape[1]
    groups = nrows // GROUP

    depth = p_ref.shape[0]
    p_copy = pltpu.make_async_copy(p_ref, p_here.at[pl.ds(0, depth)], sems.at[0])
    p_copy.start()
    p_here[pl.ds(depth, edge), :] = jnp.zeros((edge, p_here.shape[1]), p_here.dtype)

    low, high = 0, groups
    if name != "first":
        room = [count for kind, _, count in places if kind == "second"][0]
        done = jnp.int32(0)
        for g in range(leading // GROUP):
            done = done + (table[0, (g + 1) * GROUP] <= room).astype(jnp.int32)
        low, high = (0, done) if name == "early" else (done, groups)

    copies = []
    for (kind, at, count), part in zip(places, part_refs):
        step = count
        if name == "late" and kind == "second":
            step = -(-count // 4)
        for first in range(0, count, step):
            needed = None
            if name == "late" and kind == "first":
                needed = low < leading // GROUP
            elif name == "late" and kind == "second":
                needed = table[2, low * GROUP] < first + step
            elif not isinstance(kind, str):
                needed = size[0] == kind
            tall = min(step, count - first) * edge
            source = part.at[pl.ds(first * edge, tall)]
            target = held.at[pl.ds((at + first) * edge, tall)]
            copies.append((needed, pltpu.make_async_copy(source, target, sems.at[1 + len(copies)])))

    def each(act):
        for needed, copy in copies:
            if needed is None:
                act(copy)
            else:
                pl.when(needed)(functools.partial(act, copy))

    each(lambda copy: copy.start())

    def total_copy(g):
        here = piece(edge, g * GROUP, GROUP)
        return pltpu.make_async_copy(total_ref.at[here], refs[0].at[here], refs[1].at[g])

    def out_copy(g):
        here = piece(edge, g * GROUP, GROUP)
        return pltpu.make_async_copy(stage.at[here], out_ref.at[here], out_sems.at[g])

    def over(act):
        def step(g, carry):
            act(g)
            return carry

        lax.fori_loop(low, high, step, 0)

    if name != "first":
        over(lambda g: total_copy(g).start())
    each(lambda copy: copy.wait())
    p_copy.wait()

    def group(g):
        if name != "first":
            total_copy(g).wait()
        for r in range(GROUP):
            row = g * GROUP + r
            here = piece(edge, row)
            value = row_product(notes, table, slots, edge, row, held, p_here)
            if name != "first":
                value = refs[0][here, :] + value
            stage[here, :] = value.astype(stage.dtype)
        out_copy(g).start()

    over(group)
    over(lambda g: out_copy(g).wait())


def step_product(name, notes, table, slots, leading, places, parts, p_tile, total=None, size=None, out=None):
    nrows = notes.shape[1]
    depth, width = p_tile.shape
    edge = parts[0].shape[1] // PAIR
    groups = nrows // GROUP
    room = max(at + rows for _, at, rows in places)
    dtype = jnp.float32 if name == "first" else jnp.bfloat16
    tall = nrows * edge
    later = name != "first"
    late = name == "late"
    return pl.pallas_call(
        functools.partial(step_kernel, edge, slots, name, leading, places),
        in_specs=[SMEM] * (2 + late) + [ANY] * (len(parts) + 1 + later) + [HBM] * late,
        out_specs=HBM if later else ANY,
        scratch_shapes=[
            pltpu.VMEM((room * edge, PAIR * edge), p_tile.dtype),
            pltpu.VMEM((depth + edge, width), p_tile.dtype),
            pltpu.VMEM((tall, width), dtype),
            pltpu.SemaphoreType.DMA((len(parts) + 8,)),
            pltpu.SemaphoreType.DMA((groups,)),
        ]
        + [pltpu.VMEM((tall, width), jnp.float32), pltpu.SemaphoreType.DMA((groups,))] * later,
        out_shape=(pltpu.HBM if later else jax.ShapeDtypeStruct)((tall, width), dtype),
        input_output_aliases={5 + len(parts): 0} if late else {},
        cost_estimate=cost(tall * width * slots * edge, 4 * tall * width),
        compiler_params=params(16),
        name="step_" + name,
    )(
        notes,
        table,
        *([size] if late else []),
        *parts,
        p_tile,
        *([total] if later else []),
        *([in_hbm(out)] if late else []),
    )


def remainder(k, slots, leading, places, rests, unused, notes, table, lead, extra, p_second, total):
    rest = [shifted(part, "col", -1) if k == n else other for n, (part, other) in enumerate(zip(rests, unused))]
    return step_product("early", notes, table, slots, leading, places, (lead, extra), p_second, total), rest


def body(f_blocks, block_cols, block_counts, p_matrix):
    nrows, slots = block_cols.shape
    edge = f_blocks.shape[0] // nrows
    cols, counts = block_cols.T, block_counts.T
    groups = nrows // GROUP
    leading = (groups - groups // 4) * GROUP
    others = nrows * (slots // PAIR - 1)
    unit = others // 24
    always = 10 * unit
    ends = [always + k * unit for k in (1, 2, 3, 4, 5, 6, 8)] + [others]

    lead = shifted(leading_pieces(leading, f_blocks, cols, counts), "col", -1)
    notes = jnp.concatenate([cols, jnp.broadcast_to(counts, (slots, nrows))], axis=0)
    packed, extra, table = packed_pieces(notes, slots, always, f_blocks)
    p_second, packed = lax.optimization_barrier((p_matrix, packed))
    p_second = shifted(p_second, "row", -1)
    rests = cut_pieces([(nrows + always, nrows + end) for end in ends] + [(leading, nrows)], packed)
    rests, later, unused = rests[: len(ends)], rests[len(ends)], rests[len(ends) + 1 : -1]
    extra, *rests = lax.optimization_barrier((extra, *rests))
    extra = shifted(extra, "col", -1)
    every = packed.shape[0] // edge
    total = step_product("first", notes, table, slots, leading, [("all", 0, every)], (packed,), p_matrix)
    later, total, lead = lax.optimization_barrier((later, total, lead))
    later = shifted(later, "col", -1)

    notes_next = lead[leading * edge :, :nrows].astype(jnp.float32).astype(jnp.int32)
    table_next, most = read_notes(notes, notes_next, slots)
    other = most
    distance = 2
    while distance < lax.axis_size("col"):
        most = jnp.maximum(most, other)
        other = shifted(most, "col", -distance)
        distance *= 2
    size = pick_size(ends, most, other)
    early = [("first", 0, leading), ("second", nrows, always)]
    late = [early[0], ("later", leading, nrows - leading), early[1]]
    late += [(k, nrows + always, end - always) for k, end in enumerate(ends)]
    branches = [functools.partial(remainder, k, slots, leading, early) for k in range(len(ends))]
    out, rest = lax.switch(size[0], branches, rests, unused, notes_next, table_next, lead, extra, p_second, total)
    parts = (lead, later, extra, *rest)
    return step_product("late", notes_next, table_next, slots, leading, late, parts, p_second, total, size, out)


def solution(mesh):
    return jax.shard_map(
        body,
        mesh=mesh,
        in_specs=(P("row", "col"), P("row", "col"), P("row", "col"), P("row", "col")),
        out_specs=P("row", "col"),
        check_vma=False,
    )
```

```python
import functools

import jax
import jax.numpy as jnp
from jax import lax
from jax.experimental import pallas as pl
from jax.experimental.pallas import tpu as pltpu
from jax.sharding import PartitionSpec as P

GROUP = 4
PAIR = 2

SMEM = pl.BlockSpec(memory_space=pltpu.SMEM)
ANY = pl.BlockSpec(memory_space=pl.ANY)
HBM = pl.BlockSpec(memory_space=pltpu.HBM)


def shifted(block, axis, distance):
    devices = range(lax.axis_size(axis))
    route = [((i - distance) % len(devices), i) for i in devices]
    return lax.ppermute(block, axis, route)


def in_hbm(x):
    return pltpu.with_memory_space_constraint(x, pltpu.HBM)


def params(mib):
    return pltpu.CompilerParams(vmem_limit_bytes=mib << 20)


def cost(flops, moved):
    return pl.CostEstimate(flops=flops, bytes_accessed=moved, transcendentals=0)


def piece(edge, index, count=1):
    return pl.ds(pl.multiple_of(index * edge, edge), count * edge)


def beyond(count):
    more = jnp.maximum(count - PAIR, 0)
    return more // PAIR, more % PAIR


def walk(counts, full_at, single_at, row_done):
    at, opened = jnp.int32(0), jnp.int32(-1)
    for r in range(len(counts)):
        full, single = beyond(counts[r])
        full_at(r, at)
        shares = jnp.logical_and(single == 1, opened >= 0)
        opens = jnp.logical_and(single == 1, opened < 0)
        single_at(r, jnp.where(shares, opened, at + full), shares)
        opened = jnp.where(opens, at + full, jnp.where(shares, -1, opened))
        at = at + full + opens.astype(jnp.int32)
        row_done(r, at, opened)


def write_table(notes, slots, table):
    nrows = notes.shape[1]

    def full_at(r, at):
        table[0, r] = at

    def single_at(r, at, shares):
        table[1, r] = at * 2 + shares.astype(jnp.int32)

    def row_done(r, at, opened):
        table[0, r + 1] = at
        table[2, r + 1] = jnp.where(opened < 0, at, opened)

    table[2, 0] = jnp.int32(0)
    walk([notes[slots, r] for r in range(nrows)], full_at, single_at, row_done)


def table_shape(nrows):
    return jax.ShapeDtypeStruct((3, nrows + 1), jnp.int32)


def read_kernel(slots, notes, notes_next, table, most_ref):
    write_table(notes_next, slots, table)
    nrows = notes.shape[1]
    full, single = jnp.int32(0), jnp.int32(0)
    for r in range(nrows):
        more, rest = beyond(notes[slots, r])
        full, single = full + more, single + rest
    most = jnp.maximum(full + (single + 1) // PAIR, table[0, nrows])
    most_ref[...] = jnp.full(most_ref.shape, most, jnp.int32)


def read_notes(notes, notes_next, slots):
    return pl.pallas_call(
        functools.partial(read_kernel, slots),
        in_specs=[SMEM, SMEM],
        out_specs=[SMEM, pl.BlockSpec(memory_space=pltpu.VMEM)],
        out_shape=[table_shape(notes.shape[1]), jax.ShapeDtypeStruct((8, 128), jnp.int32)],
        cost_estimate=cost(20 << 30, 4096),
        compiler_params=params(2),
        name="read_notes",
    )(notes, notes_next)


def pick_kernel(ends, one_ref, other_ref, size):
    most = jnp.max(jnp.maximum(one_ref[...], other_ref[...]))
    index = jnp.int32(0)
    for end in ends[:-1]:
        index = index + (most > end).astype(jnp.int32)
    size[0] = index


def pick_size(ends, one, other):
    vector = pl.BlockSpec(memory_space=pltpu.VMEM)
    return pl.pallas_call(
        functools.partial(pick_kernel, ends),
        in_specs=[vector, vector],
        out_specs=SMEM,
        out_shape=jax.ShapeDtypeStruct((1,), jnp.int32),
        cost_estimate=cost(0, 4096),
        compiler_params=params(2),
        name="pick_size",
    )(one, other)


def leading_kernel(f_ref, cols_ref, counts_ref, out_ref):
    slots, nrows = cols_ref.shape
    tall = f_ref.shape[0]
    out_ref[pl.ds(0, tall), :] = f_ref[...]
    notes = jnp.concatenate([cols_ref[...], jnp.broadcast_to(counts_ref[...], (slots, nrows))], axis=0)
    out_ref[pl.ds(tall, 2 * slots), pl.ds(0, nrows)] = notes.astype(jnp.float32).astype(out_ref.dtype)


def leading_pieces(rows, f_blocks, cols, counts):
    slots, nrows = cols.shape
    edge = f_blocks.shape[0] // nrows
    shape = (rows * edge + 2 * slots, PAIR * edge)
    f_blocks, cols, counts = (in_hbm(x) for x in (f_blocks, cols, counts))
    return pl.pallas_call(
        leading_kernel,
        grid=(1,),
        in_specs=[
            pl.BlockSpec((rows * edge, PAIR * edge), lambda g: (0, 0)),
            pl.BlockSpec(cols.shape, lambda g: (0, 0)),
            pl.BlockSpec(counts.shape, lambda g: (0, 0)),
        ],
        out_specs=pl.BlockSpec(shape, lambda g: (0, 0)),
        out_shape=jax.ShapeDtypeStruct(shape, f_blocks.dtype),
        cost_estimate=cost(0, 4 * rows * edge * PAIR * edge),
        compiler_params=params(8),
        name="leading_pieces",
    )(f_blocks, cols, counts)


def pack_kernel(edge, slots, notes, f_ref, out_ref, extra_ref, f_here, packed, sems):
    nrows = notes.shape[1]
    parts = slots // PAIR
    fetched = []
    for g in range(nrows // GROUP):
        here = piece(edge, g * GROUP, GROUP)
        fetched.append(pltpu.make_async_copy(f_ref.at[here], f_here.at[here], sems.at[g]))
        fetched[-1].start()
    wide = PAIR * edge

    def strip(r, p):
        return f_here[pl.ds(r * edge, edge), pl.ds(pl.multiple_of(p * wide, wide), wide)]

    def full_at(r, at):
        if r % GROUP == 0:
            fetched[r // GROUP].wait()
        packed[pl.ds(r * edge, edge), :] = strip(r, 0)
        for p in range(1, parts):
            packed[piece(edge, nrows + at + (p - 1)), :] = strip(r, p)

    def single_at(r, at, shares):
        @pl.when(shares)
        def _():
            value = strip(r, 1 + beyond(notes[slots, r])[0])
            here = piece(edge, nrows + at)
            moved = jnp.concatenate([value[:, edge:], value[:, :edge]], axis=1)
            low = lax.broadcasted_iota(jnp.int32, value.shape, 1) < edge
            packed[here, :] = jnp.where(low, packed[here, :], moved)

    walk([notes[slots, r] for r in range(nrows)], full_at, single_at, lambda *_: None)
    copies = [
        pltpu.make_async_copy(packed.at[pl.ds(nrows * edge, extra_ref.shape[0])], extra_ref, sems.at[0]),
        pltpu.make_async_copy(packed, out_ref, sems.at[1]),
    ]
    for copy in copies:
        copy.start()
    for copy in copies:
        copy.wait()


def packed_pieces(notes, slots, always, f_blocks):
    nrows = notes.shape[1]
    edge = f_blocks.shape[0] // nrows
    shape = (nrows * slots // PAIR * edge, PAIR * edge)
    return pl.pallas_call(
        functools.partial(pack_kernel, edge, slots),
        in_specs=[SMEM, ANY],
        out_specs=[ANY, ANY],
        scratch_shapes=[
            pltpu.VMEM(f_blocks.shape, f_blocks.dtype),
            pltpu.VMEM(shape, f_blocks.dtype),
            pltpu.SemaphoreType.DMA((nrows // GROUP,)),
        ],
        out_shape=[
            jax.ShapeDtypeStruct(shape, f_blocks.dtype),
            jax.ShapeDtypeStruct((always * edge, PAIR * edge), f_blocks.dtype),
        ],
        cost_estimate=cost(0, 4 * f_blocks.size),
        compiler_params=params(16),
        name="pack_live_pieces",
    )(notes, f_blocks)


def cut_kernel(ranges, slots, notes, packed_ref, table, *refs):
    out_refs, sems = refs[: len(ranges)], refs[-1]
    copies = [
        pltpu.make_async_copy(packed_ref.at[pl.ds(low, high - low)], out_ref, sems.at[k])
        for k, ((low, high), out_ref) in enumerate(zip(ranges, out_refs))
    ]
    for copy in copies:
        copy.start()
    write_table(notes, slots, table)
    for copy in copies:
        copy.wait()


def cut_pieces(ranges, notes, slots, packed):
    edge = packed.shape[1] // PAIR
    rows = [(low * edge, high * edge) for low, high in ranges]
    return pl.pallas_call(
        functools.partial(cut_kernel, rows, slots),
        in_specs=[SMEM, ANY],
        out_specs=[SMEM] + [ANY] * (2 * len(rows)),
        scratch_shapes=[pltpu.SemaphoreType.DMA((len(rows),))],
        out_shape=[table_shape(notes.shape[1])]
        + [jax.ShapeDtypeStruct((high - low, packed.shape[1]), packed.dtype) for low, high in rows] * 2,
        cost_estimate=cost(0, 4 * sum(high - low for low, high in rows) * packed.shape[1]),
        compiler_params=params(2),
        name="cut_pieces",
    )(notes, packed)


def row_product(notes, table, slots, edge, row, held, p_ref):
    nrows = notes.shape[1]
    zero = p_ref.shape[0] // edge - 1
    count = notes[slots, row]
    full, single = beyond(count)
    code = table[1, row]
    second = code % 2
    left = [held[piece(edge, row), :]]
    picks = [notes[0, row], jnp.where(count > 1, notes[1, row], zero)]
    for p in range(slots // PAIR - 1):
        alone = jnp.logical_and(p == full, single == 1)
        at = jnp.where(p < full, nrows + table[0, row] + p, jnp.where(alone, nrows + code // 2, row))
        left.append(held[piece(edge, at), :])
        even, odd = notes[PAIR * (p + 1), row], notes[PAIR * (p + 1) + 1, row]
        picks.append(jnp.where(jnp.logical_or(p < full, jnp.logical_and(alone, second == 0)), even, zero))
        picks.append(jnp.where(p < full, odd, jnp.where(jnp.logical_and(alone, second == 1), even, zero)))
    picked = [p_ref[piece(edge, pick), :] for pick in picks]
    return jnp.dot(
        jnp.concatenate(left, axis=1), jnp.concatenate(picked, axis=0), preferred_element_type=jnp.float32
    )


def step_kernel(edge, slots, name, leading, places, notes, table, *refs):
    size = None
    if name == "late":
        size, *refs = refs
    part_refs, refs = refs[: len(places)], refs[len(places) :]
    p_ref, *refs = refs
    total_ref = None
    if name != "first":
        total_ref, *refs = refs
    if name == "late":
        _, *refs = refs
    out_ref, held, p_here, stage, sems, out_sems, *refs = refs
    nrows = notes.shape[1]
    groups = nrows // GROUP

    depth = p_ref.shape[0]
    p_copy = pltpu.make_async_copy(p_ref, p_here.at[pl.ds(0, depth)], sems.at[0])
    p_copy.start()
    p_here[pl.ds(depth, edge), :] = jnp.zeros((edge, p_here.shape[1]), p_here.dtype)

    low, high = 0, groups
    if name != "first":
        room = [count for kind, _, count in places if kind == "second"][0]
        done = jnp.int32(0)
        for g in range(leading // GROUP):
            done = done + (table[0, (g + 1) * GROUP] <= room).astype(jnp.int32)
        low, high = (0, done) if name == "early" else (done, groups)

    copies = []
    for (kind, at, count), part in zip(places, part_refs):
        step = count
        if name == "late" and kind == "second":
            step = -(-count // 4)
        for first in range(0, count, step):
            needed = None
            if name == "late" and kind == "first":
                needed = low < leading // GROUP
            elif name == "late" and kind == "second":
                needed = table[2, low * GROUP] < first + step
            elif not isinstance(kind, str):
                needed = size[0] == kind
            tall = min(step, count - first) * edge
            source = part.at[pl.ds(first * edge, tall)]
            target = held.at[pl.ds((at + first) * edge, tall)]
            copies.append((needed, pltpu.make_async_copy(source, target, sems.at[1 + len(copies)])))

    def each(act):
        for needed, copy in copies:
            if needed is None:
                act(copy)
            else:
                pl.when(needed)(functools.partial(act, copy))

    each(lambda copy: copy.start())

    def total_copy(g):
        here = piece(edge, g * GROUP, GROUP)
        return pltpu.make_async_copy(total_ref.at[here], refs[0].at[here], refs[1].at[g])

    def out_copy(g):
        here = piece(edge, g * GROUP, GROUP)
        return pltpu.make_async_copy(stage.at[here], out_ref.at[here], out_sems.at[g])

    def over(act):
        def step(g, carry):
            act(g)
            return carry

        lax.fori_loop(low, high, step, 0)

    if name != "first":
        over(lambda g: total_copy(g).start())
    each(lambda copy: copy.wait())
    p_copy.wait()

    def group(g):
        if name != "first":
            total_copy(g).wait()
        for r in range(GROUP):
            row = g * GROUP + r
            here = piece(edge, row)
            value = row_product(notes, table, slots, edge, row, held, p_here)
            if name != "first":
                value = refs[0][here, :] + value
            stage[here, :] = value.astype(stage.dtype)
        out_copy(g).start()

    over(group)
    over(lambda g: out_copy(g).wait())


def step_product(name, notes, table, slots, leading, places, parts, p_tile, total=None, size=None, out=None):
    nrows = notes.shape[1]
    depth, width = p_tile.shape
    edge = parts[0].shape[1] // PAIR
    groups = nrows // GROUP
    room = max(at + rows for _, at, rows in places)
    dtype = jnp.float32 if name == "first" else jnp.bfloat16
    tall = nrows * edge
    later = name != "first"
    late = name == "late"
    return pl.pallas_call(
        functools.partial(step_kernel, edge, slots, name, leading, places),
        in_specs=[SMEM] * (2 + late) + [ANY] * (len(parts) + 1 + later) + [HBM] * late,
        out_specs=HBM if later else ANY,
        scratch_shapes=[
            pltpu.VMEM((room * edge, PAIR * edge), p_tile.dtype),
            pltpu.VMEM((depth + edge, width), p_tile.dtype),
            pltpu.VMEM((tall, width), dtype),
            pltpu.SemaphoreType.DMA((len(parts) + 8,)),
            pltpu.SemaphoreType.DMA((groups,)),
        ]
        + [pltpu.VMEM((tall, width), jnp.float32), pltpu.SemaphoreType.DMA((groups,))] * later,
        out_shape=(pltpu.HBM if later else jax.ShapeDtypeStruct)((tall, width), dtype),
        input_output_aliases={5 + len(parts): 0} if late else {},
        cost_estimate=cost(tall * width * slots * edge, 4 * tall * width),
        compiler_params=params(16),
        name="step_" + name,
    )(
        notes,
        table,
        *([size] if late else []),
        *parts,
        p_tile,
        *([total] if later else []),
        *([in_hbm(out)] if late else []),
    )


def remainder(k, slots, leading, places, rests, unused, notes, table, lead, extra, p_second, total):
    rest = [shifted(part, "col", -1) if k == n else other for n, (part, other) in enumerate(zip(rests, unused))]
    return step_product("early", notes, table, slots, leading, places, (lead, extra), p_second, total), rest


def body(f_blocks, block_cols, block_counts, p_matrix):
    nrows, slots = block_cols.shape
    edge = f_blocks.shape[0] // nrows
    cols, counts = block_cols.T, block_counts.T
    groups = nrows // GROUP
    leading = (groups - groups // 4) * GROUP
    others = nrows * (slots // PAIR - 1)
    unit = others // 24
    always = 19 * unit // 2
    ends = [always + k * unit for k in (1, 2, 3, 4, 5, 6, 8)] + [others]

    lead = shifted(leading_pieces(leading, f_blocks, cols, counts), "col", -1)
    notes = jnp.concatenate([cols, jnp.broadcast_to(counts, (slots, nrows))], axis=0)
    packed, extra = packed_pieces(notes, slots, always, f_blocks)
    p_second, packed = lax.optimization_barrier((p_matrix, packed))
    p_second = shifted(p_second, "row", -1)
    ranges = [(nrows + always, nrows + end) for end in ends] + [(leading, nrows)]
    table, *rests = cut_pieces(ranges, notes, slots, packed)
    rests, later, unused = rests[: len(ends)], rests[len(ends)], rests[len(ends) + 1 : -1]
    extra, *rests = lax.optimization_barrier((extra, *rests))
    extra = shifted(extra, "col", -1)
    every = packed.shape[0] // edge
    total = step_product("first", notes, table, slots, leading, [("all", 0, every)], (packed,), p_matrix)
    later, total, lead = lax.optimization_barrier((later, total, lead))
    later = shifted(later, "col", -1)

    notes_next = lead[leading * edge :, :nrows].astype(jnp.float32).astype(jnp.int32)
    table_next, most = read_notes(notes, notes_next, slots)
    other = most
    distance = 2
    while distance < lax.axis_size("col"):
        most = jnp.maximum(most, other)
        other = shifted(most, "col", -distance)
        distance *= 2
    size = pick_size(ends, most, other)
    early = [("first", 0, leading), ("second", nrows, always)]
    late = [early[0], ("later", leading, nrows - leading), early[1]]
    late += [(k, nrows + always, end - always) for k, end in enumerate(ends)]
    branches = [functools.partial(remainder, k, slots, leading, early) for k in range(len(ends))]
    out, rest = lax.switch(size[0], branches, rests, unused, notes_next, table_next, lead, extra, p_second, total)
    parts = (lead, later, extra, *rest)
    return step_product("late", notes_next, table_next, slots, leading, late, parts, p_second, total, size, out)


def solution(mesh):
    return jax.shard_map(
        body,
        mesh=mesh,
        in_specs=(P("row", "col"), P("row", "col"), P("row", "col"), P("row", "col")),
        out_specs=P("row", "col"),
        check_vma=False,
    )
```
